256 devices in a mesh: gx: 16 (over z, y_hi), gy: 8 (over x, core), gz: 2 (over y_lo).
Axes of the slice: x: 4, y: 4 (y_hi: 2, y_lo: 2; y = y_hi * 2 + y_lo), z: 8, core: 2. Of those that a mesh axis runs over, the one named last changes fastest.
Arguments:
- features: bfloat16 [128, 256, 32, 128], P('gx', 'gy', 'gz'), may hold values from 0 to 15
- active: int32 [128, 256, 64], P('gx', 'gy', 'gz'), may hold values from 0 to 1
- weight: bfloat16 [3, 3, 3, 64, 128], replicated, may hold values from -0.15625 to 0.15625
- gain: float32 [128], replicated, may hold values from 0.1 to 1.9
- bias: float32 [128], replicated, may hold values from -1 to 1
- cotangent: bfloat16 [64, 128, 32, 128], P('gx', 'gy', 'gz'), may hold values from -5 to 5
Outputs:
- section_out: bfloat16 [64, 128, 32, 128], P('gx', 'gy', 'gz')
- grad_features: bfloat16 [128, 256, 32, 128], P('gx', 'gy', 'gz')
- grad_weight: float32 [3, 3, 3, 64, 128], replicated
- gain_gradient: float32 [128], replicated
- shift_gradient: float32 [128], replicated
The draws below stay inside these ranges and needn't reach their ends.
All inputs are finite; a program needn't handle non-finite values.
Results may differ from the reference program's by a relative error of at most 0.0049.
Values may be sent and summed in bfloat16 or wider, within the bound.
No kernel may reach another device: no remote copies, remote signals or barrier semaphores. Data moves between devices by JAX's collectives and lax.ppermute only.
A program may use at most 64 MiB of HBM per device.

```python
import jax
import jax.numpy as jnp
from jax import lax

CIN = 64
COUT = 128
NX = 128
NY = 256
NZ = 64
N_GX = 16


def draw_features(key, part):
    key = jax.random.fold_in(key, 11)
    shape = (NX, NY, NZ // 2, 2 * CIN)
    place = lax.broadcasted_iota(jnp.float32, shape, 0) / NX
    base = jnp.minimum(jnp.abs(jax.random.normal(key, shape, jnp.float32)), 5.0) * (1.0 + 2.0 * place)
    return base.astype(jnp.bfloat16)


def draw_active(key, part):
    key = jax.random.fold_in(key, 12)
    first, second = jax.random.split(key)
    leaves = jax.random.randint(first, (NX // 8, NY // 8, NZ // 8), 0, 4) > 0
    leaves = jnp.repeat(jnp.repeat(jnp.repeat(leaves, 8, axis=0), 8, axis=1), 8, axis=2)
    place = lax.broadcasted_iota(jnp.int32, (NX, NY, NZ), 0)
    level = 250 + 500 * place // NX
    voxels = jax.random.randint(second, (NX, NY, NZ), 0, 1000) < level
    return (leaves & voxels).astype(jnp.int32)


def draw_cotangent(key, part):
    key = jax.random.fold_in(key, 13)
    first, second = jax.random.split(key)
    shape = (NX // 2, NY // 2, NZ // 2, COUT)
    offset = jax.random.uniform(second, (COUT,), jnp.float32, -1.0, 1.0)
    base = jnp.clip(jax.random.normal(first, shape, jnp.float32), -4.0, 4.0) + offset
    return base.astype(jnp.bfloat16)


def normal_values(rng, shape, scale, limit, kind=jnp.bfloat16):
    result = scale * jax.random.normal(rng, shape, jnp.float32)
    return jnp.clip(result, min=-limit, max=limit).astype(kind)


def setup_inputs(seed: int = 0) -> dict:
    keys = jax.random.split(jax.random.key(seed), 7)
    return {
        "features": draw_features(jax.random.fold_in(keys[6], 71), 0),
        "active": draw_active(jax.random.fold_in(keys[6], 71), 0),
        "weight": normal_values(keys[2], (3, 3, 3, CIN, COUT), (27 * CIN) ** -0.5, 0.15625),
        "gain": jnp.clip(1.0 + 0.18 * jax.random.normal(keys[3], (COUT,), jnp.float32), 0.1, 1.9),
        "bias": jnp.clip(jax.random.uniform(keys[4], (COUT,), jnp.float32, -1.0, 1.0), -1.0, 1.0),
        "cotangent": draw_cotangent(jax.random.fold_in(keys[6], 71), 0),
    }


HIGH = lax.Precision.HIGHEST

def taps_forward(xe, w, mx, my, mz):
    acc = jnp.zeros((mx, my, mz, w.shape[4]), jnp.float32)
    for a in range(3):
        for b in range(3):
            for t in range(3):
                piece = xe[a:a + 2 * mx:2, b:b + 2 * my:2, t:t + 2 * mz:2]
                acc = acc + jnp.einsum('xyzc,co->xyzo', piece, w[a, b, t], precision=HIGH)
    return acc

def taps_weight(xe, grad, mx, my, mz):
    rows = []
    for a in range(3):
        for b in range(3):
            for t in range(3):
                piece = xe[a:a + 2 * mx:2, b:b + 2 * my:2, t:t + 2 * mz:2]
                rows.append(jnp.einsum('xyzc,xyzo->co', piece, grad, precision=HIGH))
    return jnp.stack(rows).reshape(3, 3, 3, xe.shape[3], grad.shape[3])

def taps_transpose(de, w, mx, my, mz):
    cin = w.shape[3]
    total = jnp.zeros((2 * mx + 3, 2 * my + 3, 2 * mz + 3, cin), jnp.float32)
    for a in range(3):
        for b in range(3):
            for t in range(3):
                term = jnp.einsum('xyzo,co->xyzc', de, w[a, b, t], precision=HIGH)
                total = total.at[a:a + 2 * (mx + 1):2, b:b + 2 * (my + 1):2, t:t + 2 * (mz + 1):2].add(term)
    return total[1:2 * mx + 1, 1:2 * my + 1, 1:2 * mz + 1]

def reference(features, active, weight, gain, bias, cotangent):
    nx, ny, nz2, width = features.shape
    nz = 2 * nz2
    cin = width // 2
    cx, cy, cz = (nx // 2, ny // 2, nz // 2)
    w = weight.astype(jnp.float32)
    slab = cx // N_GX
    count_slabs = N_GX
    xin = features.reshape(nx, ny, nz, cin) * active[..., None].astype(jnp.bfloat16)
    padded = jnp.pad(xin, ((1, 0), (1, 0), (1, 0), (0, 0)))

    def forward_slab(index):
        xe = lax.dynamic_slice_in_dim(padded, (index * 2 * slab).astype(jnp.int32), 2 * slab + 1, 0).astype(jnp.float32)
        return taps_forward(xe, w, slab, cy, cz)
    preactivation = lax.map(forward_slab, jnp.arange(count_slabs, dtype=jnp.int32)).reshape(cx, cy, cz, w.shape[4])
    silu_activation = active.reshape(cx, 2, cy, 2, cz, 2).max(axis=(1, 3, 5)).astype(jnp.float32)[..., None]
    active_count = jnp.sum(silu_activation)
    batch_mean = lax.optimization_barrier(jnp.sum(silu_activation * preactivation, axis=(0, 1, 2))) / active_count
    var = lax.optimization_barrier(jnp.sum(silu_activation * (preactivation - batch_mean) ** 2, axis=(0, 1, 2))) / active_count
    inverse_deviation = lax.rsqrt(var + 1e-05)
    standardized_input = (preactivation - batch_mean) * inverse_deviation
    normalized_output = standardized_input * gain + bias
    sig = jax.nn.sigmoid(normalized_output)
    section_out = (silu_activation * normalized_output * sig).astype(jnp.bfloat16)
    silu_slope = silu_activation * cotangent.astype(jnp.float32) * sig * (1.0 + normalized_output * (1.0 - sig))
    shift_gradient = lax.optimization_barrier(jnp.sum(silu_slope, axis=(0, 1, 2))) / active_count
    gain_gradient = lax.optimization_barrier(jnp.sum(silu_slope * standardized_input, axis=(0, 1, 2))) / active_count
    preactivation_gradient = (silu_activation * inverse_deviation * gain * (silu_slope - shift_gradient - standardized_input * gain_gradient)).astype(jnp.bfloat16)
    dpad = jnp.pad(preactivation_gradient, ((0, 1), (0, 1), (0, 1), (0, 0)))

    def backward_slab(index):
        start = (index * slab).astype(jnp.int32)
        xe = lax.dynamic_slice_in_dim(padded, (index * 2 * slab).astype(jnp.int32), 2 * slab + 1, 0).astype(jnp.float32)
        de = lax.dynamic_slice_in_dim(dpad, start, slab + 1, 0).astype(jnp.float32)
        part_w = taps_weight(xe, de[:slab, :cy, :cz], slab, cy, cz)
        gin = taps_transpose(de, w, slab, cy, cz)
        mask = lax.dynamic_slice_in_dim(active, (index * 2 * slab).astype(jnp.int32), 2 * slab, 0)
        gin = (gin * mask[..., None].astype(jnp.float32)).astype(jnp.bfloat16)
        return (gin, part_w)
    gins, parts = lax.map(backward_slab, jnp.arange(count_slabs, dtype=jnp.int32))
    grad_features = gins.reshape(nx, ny, nz2, width)
    grad_weight = lax.optimization_barrier(jnp.sum(parts, axis=0)) / active_count
    return (section_out, grad_features, grad_weight, gain_gradient, shift_gradient)
```

```python
import jax
import jax.numpy as jnp
from jax import lax
from jax.sharding import PartitionSpec as P


def from_behind(value, axis, steps):
    count = lax.axis_size(axis)
    first, last = (max(0, -steps), min(count, count - steps))
    return lax.ppermute(value, axis, [(source, source + steps) for source in range(first, last)])


def extend(block, by, lower):
    rows = block.shape[0]
    face = block[rows - 1 : rows] if by == 1 else block[0:1]
    got = from_behind(face, "gx", by)
    block = (
        jnp.concatenate([got, block], axis=0) if by == 1 else jnp.concatenate([block, got], axis=0)
    )
    cols = block.shape[1]
    face = block[:, cols - 1 : cols] if by == 1 else block[:, 0:1]
    got = from_behind(face, "gy", by)
    block = (
        jnp.concatenate([got, block], axis=1) if by == 1 else jnp.concatenate([block, got], axis=1)
    )
    depth = block.shape[2]
    face = block[:, :, depth - 1 : depth, lower:] if by == 1 else block[:, :, 0:1, lower:]
    got = from_behind(face, "gz", by)
    return (block, got)


ALL = ("gx", "gy", "gz")


def gathered(value, axes):
    count = lax.axis_size(axes)
    return lax.all_to_all(jnp.broadcast_to(value, (count,) + value.shape), axes, 0, 0)


def merged(parts):
    counts, sums, squares = (parts[:, 0], parts[:, 1], parts[:, 2])
    count = jnp.sum(counts, axis=0)
    total = jnp.sum(sums, axis=0)
    mean = total / jnp.maximum(count, 1.0)
    apart = sums / jnp.maximum(counts, 1.0) - mean
    return jnp.stack([count, total, jnp.sum(squares + counts * apart * apart, axis=0)])


def weight_totals(partial_value, count):
    devices = lax.axis_size(ALL)
    rows = -(-partial_value.shape[0] // (8 * devices)) * 8
    padded = jnp.pad(partial_value, ((0, rows * devices - partial_value.shape[0]), (0, 0)))
    chunks = padded.astype(jnp.bfloat16).reshape(devices, rows, -1)
    mine = jnp.sum(lax.all_to_all(chunks, ALL, 0, 0).astype(jnp.float32), axis=0) / count
    whole = gathered(mine.astype(jnp.bfloat16), ALL)
    return whole.reshape(devices * rows, -1)[: partial_value.shape[0]].astype(jnp.float32)


def local(features, active, weight, gain, bias, cotangent):
    vx, vy, vzp, width = features.shape
    cin = width // 2
    cout = weight.shape[4]
    mx, my, mz = (vx // 2, vy // 2, vzp)
    pairmask = active.reshape(vx, vy, vzp, 2, 1).astype(jnp.bfloat16)
    xin = (features.reshape(vx, vy, vzp, 2, cin) * pairmask).reshape(vx, vy, vzp, width)
    extended, zplane = extend(xin, 1, cin)
    odd_prev = jnp.concatenate([zplane, extended[:, :, : vzp - 1, cin:]], axis=2)
    pair_w = jnp.concatenate([weight[:, :, 1], weight[:, :, 2]], axis=2)
    preactivation = jnp.zeros((mx, my, mz, cout), jnp.float32)
    for a in range(3):
        for b in range(3):
            pair_in = extended[a : a + 2 * mx : 2, b : b + 2 * my : 2]
            odd_in = odd_prev[a : a + 2 * mx : 2, b : b + 2 * my : 2]
            preactivation = preactivation + jnp.einsum(
                "xyzk,ko->xyzo", pair_in, pair_w[a, b], preferred_element_type=jnp.float32
            )
            preactivation = preactivation + jnp.einsum(
                "xyzk,ko->xyzo", odd_in, weight[a, b, 0], preferred_element_type=jnp.float32
            )
    voxel_mask4 = (
        active.reshape(mx, 2, my, 2, mz, 2).max(axis=(1, 3, 5)).astype(jnp.float32)[..., None]
    )
    mask3 = voxel_mask4[..., 0]
    own_count = jnp.sum(mask3)
    own_total = jnp.sum(voxel_mask4 * preactivation, axis=(0, 1, 2))
    own_mean = own_total / jnp.maximum(own_count, 1.0)
    own_squares = jnp.sum(voxel_mask4 * (preactivation - own_mean) ** 2, axis=(0, 1, 2))
    stats = jnp.stack([jnp.full((cout,), own_count), own_total, own_squares])
    stats = merged(gathered(merged(gathered(stats, ("gy", "gz"))), "gx"))
    count = stats[0, 0]
    batch_mean = stats[1] / count
    var = stats[2] / count
    inverse_deviation = lax.rsqrt(var + 1e-05)
    standardized_input = (preactivation - batch_mean) * inverse_deviation
    normalized_output = standardized_input * gain + bias
    sig = jax.nn.sigmoid(normalized_output)
    section_out = (voxel_mask4 * normalized_output * sig).astype(jnp.bfloat16)
    silu_slope = (
        voxel_mask4 * cotangent.astype(jnp.float32) * sig * (1.0 + normalized_output * (1.0 - sig))
    )
    sums = jnp.stack(
        [
            jnp.sum(silu_slope, axis=(0, 1, 2)),
            jnp.sum(silu_slope * standardized_input, axis=(0, 1, 2)),
        ]
    )
    sums = jnp.sum(gathered(jnp.sum(gathered(sums, ("gy", "gz")), axis=0), "gx"), axis=0)
    sum_slope, sum_prod = (sums[0], sums[1])
    shift_gradient = sum_slope / count
    gain_gradient = sum_prod / count
    preactivation_gradient = (
        voxel_mask4
        * inverse_deviation
        * gain
        * (silu_slope - shift_gradient - standardized_input * gain_gradient)
    ).astype(jnp.bfloat16)
    dext, zrim = extend(preactivation_gradient, -1, 0)
    padded = jnp.concatenate([dext, zrim], axis=2)
    taps = (((1, 0),), ((2, 0), (0, 1)))
    rows = []
    for px in range(2):
        cols = []
        for py in range(2):
            accum = jnp.zeros((mx, my, mz, width), jnp.float32)
            odd = jnp.zeros((mx, my, mz, cin), jnp.float32)
            for input_a, sx in taps[px]:
                for input_b, sy in taps[py]:
                    here = padded[sx : sx + mx, sy : sy + my, :mz]
                    after = padded[sx : sx + mx, sy : sy + my, 1 : mz + 1]
                    accum = accum + jnp.einsum(
                        "xyzo,ko->xyzk",
                        here,
                        pair_w[input_a, input_b],
                        preferred_element_type=jnp.float32,
                    )
                    odd = odd + jnp.einsum(
                        "xyzo,ko->xyzk",
                        after,
                        weight[input_a, input_b, 0],
                        preferred_element_type=jnp.float32,
                    )
            accum = accum + jnp.concatenate([jnp.zeros_like(odd), odd], axis=3)
            cols.append(accum)
        rows.append(jnp.stack(cols, axis=2))
    whole = jnp.stack(rows, axis=1).reshape(vx, vy, vzp, 2, cin)
    grad_features = (whole * pairmask).reshape(vx, vy, vzp, width).astype(jnp.bfloat16)
    blocks = []
    for a in range(3):
        for b in range(3):
            pair_in = extended[a : a + 2 * mx : 2, b : b + 2 * my : 2]
            odd_in = odd_prev[a : a + 2 * mx : 2, b : b + 2 * my : 2]
            pair_grad = jnp.einsum(
                "xyzk,xyzo->ko", pair_in, preactivation_gradient, preferred_element_type=jnp.float32
            )
            odd_grad = jnp.einsum(
                "xyzk,xyzo->ko", odd_in, preactivation_gradient, preferred_element_type=jnp.float32
            )
            blocks.append(jnp.stack([odd_grad, pair_grad[:cin], pair_grad[cin:]]))
    flat = jnp.stack(blocks).reshape(27 * cin, cout)
    grad_weight = weight_totals(flat, count).reshape(3, 3, 3, cin, cout)
    return (section_out, grad_features, grad_weight, gain_gradient, shift_gradient)


def solution(mesh):
    in_specs = (
        P("gx", "gy", "gz", None),
        P("gx", "gy", "gz"),
        P(),
        P(),
        P(),
        P("gx", "gy", "gz", None),
    )
    out_specs = (P("gx", "gy", "gz", None), P("gx", "gy", "gz", None), P(), P(), P())
    return jax.shard_map(local, mesh=mesh, in_specs=in_specs, out_specs=out_specs, check_vma=False)
```

```python
import jax
import jax.numpy as jnp
from jax import lax
from jax.experimental import pallas as pl
from jax.experimental.pallas import tpu as pltpu
from jax.sharding import Mesh, PartitionSpec as P

BF = jnp.bfloat16
F32 = jnp.float32
ALL = ("z", "yh", "x", "c", "yl")
NEAR = ("yh", "x", "c", "yl")
FAR = ("z",)
PARAMS = pltpu.CompilerParams(vmem_limit_bytes=48 * 1024 * 1024)


def call(kernel, outs, args, scratch=(), flops=100_000_000):
    size = sum(a.size * a.dtype.itemsize for a in args) + sum(o.size * o.dtype.itemsize for o in outs)
    return pl.pallas_call(
        kernel,
        out_shape=outs,
        in_specs=[pl.BlockSpec(memory_space=pltpu.VMEM) for _ in args],
        out_specs=[pl.BlockSpec(memory_space=pltpu.VMEM) for _ in outs],
        scratch_shapes=list(scratch),
        compiler_params=PARAMS,
        cost_estimate=pl.CostEstimate(flops=flops, bytes_accessed=size, transcendentals=0),
    )(*args)


def shape(dims, dtype):
    return jax.ShapeDtypeStruct(dims, dtype)


def dot(left, right, dims=((1,), (0,))):
    return lax.dot_general(left, right, (dims, ((), ())), preferred_element_type=F32)


def row_picker(rows, step, offset):
    r = lax.broadcasted_iota(jnp.int32, (rows, rows * step), 0)
    k = lax.broadcasted_iota(jnp.int32, (rows, rows * step), 1)
    return (k == r * step + offset).astype(BF)


def with_edge(value, edge, at, shift):
    groups, depth, lanes = value.shape
    moved = pltpu.roll(value.reshape(groups * depth, lanes), shift % (groups * depth), 0)
    moved = moved.reshape(groups, depth, lanes)
    q = lax.broadcasted_iota(jnp.int32, value.shape, 1)
    return jnp.where(q == at, jnp.broadcast_to(edge[:, None, :], value.shape), moved)


def mask_kernel(feat, active, xin, mask, act, zface):
    nx, _, my, mz, width = xin.shape
    z = active.shape[2]
    sel = (
        lax.broadcasted_iota(jnp.int32, (mz, z), 1) // 2 == lax.broadcasted_iota(jnp.int32, (mz, z), 0)
    ).astype(F32)
    lane = lax.broadcasted_iota(jnp.int32, (z, width), 1) // (width // 2)
    spread = (lax.broadcasted_iota(jnp.int32, (z, width), 0) % 2 == lane).astype(BF)
    pick = row_picker(my, mz, mz - 1)
    count = None
    for x in range(nx):
        a = active[x].astype(F32)
        rep = jnp.broadcast_to(a[:, None, :], (2 * my, mz, z)) * sel[None]
        m = dot(rep.astype(BF).reshape(2 * my * mz, z), spread).astype(BF)
        m = m.reshape(my, 2, mz, width)
        value = feat[x].reshape(my, 2, mz, width) * m
        for py in range(2):
            part = m[:, py]
            mask[x, py] = part
            held = value[:, py]
            xin[x, py] = held
            zface[x, py] = dot(pick, held.reshape(my * mz, width)).astype(BF)
            term = part.astype(F32).reshape(my * mz, width)
            count = term if count is None else count + term
        if x % 2 == 1:
            both = count + pltpu.roll(count, width // 2, 1)
            act[x // 2] = (both > 0.0).astype(F32).astype(BF).reshape(my, mz, width)
            count = None


def tile_of(xin, xh, yh, row, b):
    py = 0 if b == 1 else 1
    my = xin.shape[2]
    base = xh[py, :my] if row == 0 else xin[row - 1, py]
    if b == 0:
        base = jnp.concatenate([yh[row][None], base[: my - 1]], axis=0)
    return base


def edge_of(zh, ch, row, b):
    base = zh[row, 0 if b == 1 else 1]
    if b == 0:
        wide = base.astype(F32)
        wide = jnp.concatenate([ch[row : row + 1].astype(F32), wide[: wide.shape[0] - 1]], axis=0)
        base = wide.astype(BF)
    return base


TAPS = [(a, b) for a in range(3) for b in range(3)]


def forward_kernel(xin, act, xh, yh, zh, ch, weight, pre, stats, wmat):
    mx, my, mz, cout = pre.shape
    width = xin.shape[4]
    half = width // 2
    zero = jnp.zeros((half, cout), BF)
    for i, (a, b) in enumerate(TAPS):
        lo = i * width
        wmat[lo : lo + half, :cout] = weight[a, b, 1]
        wmat[lo + half : lo + width, :cout] = weight[a, b, 2]
        wmat[lo : lo + half, cout:] = zero
        wmat[lo + half : lo + width, cout:] = weight[a, b, 0]
    rows = my * mz
    total = jnp.zeros((1, cout), F32)
    count = jnp.zeros((1, cout), F32)
    w = wmat[...]
    for m in range(mx):
        left = jnp.concatenate(
            [tile_of(xin, xh, yh, 2 * m + a, b).reshape(rows, width) for a, b in TAPS], axis=1
        )
        edge = jnp.concatenate([edge_of(zh, ch, 2 * m + a, b) for a, b in TAPS], axis=1)
        out = dot(left, w)
        rim = dot(edge, w[:, cout:])
        prev = with_edge(out[:, cout:].reshape(my, mz, cout), rim, 0, 1)
        value = out[:, :cout].reshape(my, mz, cout) + prev
        pre[m] = value
        on = act[m].astype(F32)
        total = total + jnp.sum((on * value).reshape(rows, cout), axis=0, keepdims=True)
        count = count + jnp.sum(on.reshape(rows, cout), axis=0, keepdims=True)
    mean = total / jnp.maximum(count, 1.0)
    squares = jnp.zeros((1, cout), F32)
    for m in range(mx):
        apart = pre[m].reshape(rows, cout) - mean
        on = act[m].astype(F32).reshape(rows, cout)
        squares = squares + jnp.sum(on * apart * apart, axis=0, keepdims=True)
    for i in range(stats.shape[0]):
        stats[i, 0:1] = count
        stats[i, 1:2] = total
        stats[i, 2:3] = squares


def slope_kernel(pre, act, cot, par, out, slope, sums):
    mx, my, mz, cout = pre.shape
    rows = my * mz
    mean, rstd, gain, bias = (par[i : i + 1] for i in range(4))
    first = jnp.zeros((1, cout), F32)
    second = jnp.zeros((1, cout), F32)
    for m in range(mx):
        on = act[m].astype(F32).reshape(rows, cout)
        hat = (pre[m].reshape(rows, cout) - mean) * rstd
        normed = hat * gain + bias
        sig = jax.nn.sigmoid(normed)
        out[m] = (on * normed * sig).astype(BF).reshape(my, mz, cout)
        tilt = on * cot[m].astype(F32).reshape(rows, cout) * sig * (1.0 + normed * (1.0 - sig))
        slope[m] = tilt.reshape(my, mz, cout)
        first = first + jnp.sum(tilt, axis=0, keepdims=True)
        second = second + jnp.sum(tilt * hat, axis=0, keepdims=True)
    for i in range(sums.shape[0]):
        sums[i, 0:1] = first
        sums[i, 1:2] = second


def weight_kernel(slope, pre, act, par, xin, xh, yh, zh, ch, dpre, pack, zface, dw):
    mx, my, mz, cout = pre.shape
    width = xin.shape[4]
    half = width // 2
    rows = my * mz
    mean, rstd, gain, shift, tilt = (par[i : i + 1] for i in range(5))
    pick = row_picker(my, mz, 0)
    last = lax.broadcasted_iota(jnp.int32, (my, mz, cout), 1) == mz - 1
    total = None
    rims = []
    for m in range(mx):
        on = act[m].astype(F32).reshape(rows, cout)
        hat = (pre[m].reshape(rows, cout) - mean) * rstd
        grad = on * rstd * gain * (slope[m].reshape(rows, cout) - shift - hat * tilt)
        held = grad.astype(BF)
        dpre[m] = held.reshape(my, mz, cout)
        first = dot(pick, held)
        zface[m] = first.astype(BF)
        if m == 0:
            pack[:my] = held.reshape(my, mz, cout)
            pack[my] = first.astype(BF)
        rims.append(first)
        wide = held.astype(F32)
        after = pltpu.roll(wide, rows - 1, 0).reshape(my, mz, cout)
        after = jnp.where(last, 0.0, after).reshape(rows, cout)
        right = jnp.concatenate([wide.T, after.T], axis=0).astype(BF)
        left = jnp.concatenate(
            [tile_of(xin, xh, yh, 2 * m + a, b).reshape(rows, width) for a, b in TAPS], axis=1
        )
        term = dot(right, left)
        total = term if total is None else total + term
    rim = jnp.concatenate(rims, axis=0).T.astype(BF)
    edge = jnp.concatenate(
        [
            jnp.concatenate([edge_of(zh, ch, 2 * m + a, b) for a, b in TAPS], axis=1)
            for m in range(mx)
        ],
        axis=0,
    )
    low = total[cout:] + dot(rim, edge)
    for i in range(len(TAPS)):
        at = i * width
        own = total[:cout, at : at + width].T
        prev = low[:, at : at + width].T
        dw[3 * half * i : 3 * half * i + half] = prev[half:].astype(BF)
        dw[3 * half * i + half : 3 * half * (i + 1)] = own.astype(BF)
    used = 3 * half * len(TAPS)
    if dw.shape[0] > used:
        dw[used:] = jnp.zeros((dw.shape[0] - used, cout), BF)


def input_kernel(dpre, xh, yh, zh, ch, wmat, mask, out, ext, nxt):
    mx, my, mz, cout = dpre.shape
    width = mask.shape[4]
    rows = my * mz
    for r in range(mx + 1):
        base = dpre[r] if r < mx else xh[:my]
        ext[r, :my] = base
        ext[r, my] = yh[r]
        whole = jnp.concatenate([base, yh[r][None]], axis=0).astype(F32)
        rim = jnp.concatenate([zh[r].astype(F32), ch[r : r + 1].astype(F32)], axis=0)
        nxt[r] = with_edge(whole, rim, mz - 1, -1).astype(BF)
    taps = (((1, 0),), ((2, 0), (0, 1)))
    for m in range(mx):
        for px in range(2):
            for py in range(2):
                left, right = ([], [])
                for a, sx in taps[px]:
                    for b, sy in taps[py]:
                        left.append(ext[m + sx, sy : sy + my].reshape(rows, cout))
                        left.append(nxt[m + sx, sy : sy + my].reshape(rows, cout))
                        at = (a * 3 + b) * width
                        right.append(wmat[at : at + width])
                left = jnp.concatenate(left, axis=1)
                right = jnp.concatenate(right, axis=1)
                value = dot(left, right, ((1,), (1,)))
                x = 2 * m + px
                value = value * mask[x, py].astype(F32).reshape(rows, width)
                out[x, :, py] = value.astype(BF).reshape(my, mz, width)


def moved(value, sizes, by):
    nx, ny, nz = sizes
    pairs = []
    for i in range(nx):
        for j in range(ny):
            for k in range(nz):
                i2, j2, k2 = (i + by[0], j + by[1], k + by[2])
                if 0 <= i2 < nx and 0 <= j2 < ny and 0 <= k2 < nz:
                    pairs.append(((i * ny + j) * nz + k, (i2 * ny + j2) * nz + k2))
    return lax.ppermute(value, ALL, pairs)


def exchanged(value, axes):
    return lax.all_to_all(value, axes, 0, 0)


def spread(value, axes):
    return exchanged(jnp.broadcast_to(value, (lax.axis_size(axes),) + value.shape), axes)


def merged(parts):
    counts, sums, squares = (parts[:, 0], parts[:, 1], parts[:, 2])
    count = jnp.sum(counts, axis=0)
    total = jnp.sum(sums, axis=0)
    mean = total / jnp.maximum(count, 1.0)
    apart = sums / jnp.maximum(counts, 1.0) - mean
    return jnp.stack([count, total, jnp.sum(squares + counts * apart * apart, axis=0)])


def local(sizes, features, active, weight, gain, bias, cotangent):
    vx, vy, mz, width = features.shape
    cin = width // 2
    cout = weight.shape[4]
    mx, my = (vx // 2, vy // 2)
    near = lax.axis_size(NEAR)
    xin, mask, act, zface = call(
        mask_kernel,
        [
            shape((vx, 2, my, mz, width), BF),
            shape((vx, 2, my, mz, width), BF),
            shape((mx, my, mz, width), BF),
            shape((vx, 2, my, width), BF),
        ],
        [features, active],
    )
    pack = jnp.concatenate([xin[vx - 1], zface[vx - 1][:, None]], axis=1)
    xh = moved(pack, sizes, (1, 0, 0))
    yface = jnp.concatenate([xh[1:2, my - 1], xin[:, 1, my - 1]], axis=0)
    zfaces = jnp.concatenate([xh[None, :, my], zface], axis=0)
    corner = zfaces[:, 1, my - 1]
    yh = moved(yface, sizes, (0, 1, 0))
    zh = moved(zfaces, sizes, (0, 0, 1))
    ch = moved(corner, sizes, (0, 1, 1))
    pre, stats, wmat = call(
        forward_kernel,
        [
            shape((mx, my, mz, cout), F32),
            shape((near, 3, cout), F32),
            shape((9 * width, 2 * cout), BF),
        ],
        [xin, act, xh, yh, zh, ch, weight],
        flops=1_200_000_000,
    )
    stats = merged(spread(merged(exchanged(stats, NEAR)), FAR))
    count = stats[0]
    mean = stats[1] / count
    rstd = lax.rsqrt(stats[2] / count + 1e-05)
    par = jnp.stack([mean, rstd, gain, bias])
    section_out, slope, sums = call(
        slope_kernel,
        [
            shape((mx, my, mz, cout), BF),
            shape((mx, my, mz, cout), F32),
            shape((near, 2, cout), F32),
        ],
        [pre, act, cotangent, par],
    )
    sums = jnp.sum(spread(jnp.sum(exchanged(sums, NEAR), axis=0), FAR), axis=0)
    shift_gradient = sums[0] / count
    gain_gradient = sums[1] / count
    par = jnp.stack([mean, rstd, gain, shift_gradient, gain_gradient])
    taps = 27 * cin
    rows = -(-taps // (16 * near)) * 16
    if near * (rows - 8) >= taps and near * (rows - 8) % 16 == 0:
        rows = rows - 8
    dpre, pack, zface, dw = call(
        weight_kernel,
        [
            shape((mx, my, mz, cout), BF),
            shape((my + 1, mz, cout), BF),
            shape((mx, my, cout), BF),
            shape((near * rows, cout), BF),
        ],
        [slope, pre, act, par, xin, xh, yh, zh, ch],
        flops=1_200_000_000,
    )
    xd = moved(pack, sizes, (-1, 0, 0))
    mine = jnp.sum(exchanged(dw.reshape(near, rows, cout), NEAR).astype(F32), axis=0)
    zfaces = jnp.concatenate([zface, xd[my:]], axis=0)
    yd = moved(jnp.concatenate([dpre[:, 0], xd[:1]], axis=0), sizes, (0, -1, 0))
    zd = moved(zfaces, sizes, (0, 0, -1))
    cd = moved(zfaces[:, 0], sizes, (0, -1, -1))
    mine = jnp.sum(spread(mine, FAR), axis=0) / count[0]
    grad_weight = spread(mine.astype(BF), NEAR).reshape(near * rows, cout)[:taps]
    grad_weight = grad_weight.astype(F32).reshape(weight.shape)
    (grad_features,) = call(
        input_kernel,
        [shape((vx, my, 2, mz, width), BF)],
        [dpre, xd, yd, zd, cd, wmat, mask],
        scratch=[pltpu.VMEM((mx + 1, my + 1, mz, cout), BF)] * 2,
        flops=1_200_000_000,
    )
    grad_features = grad_features.reshape(features.shape)
    return (section_out, grad_features, grad_weight, gain_gradient, shift_gradient)


def solution(mesh):
    gx, gy, gz = (mesh.shape[name] for name in ("gx", "gy", "gz"))
    fine = Mesh(mesh.devices.reshape(gx // 2, 2, gy // 2, 2, gz), ALL)
    block = (("z", "yh"), ("x", "c"), "yl")
    in_specs = (P(*block, None), P(*block), P(), P(), P(), P(*block, None))
    out_specs = (P(*block, None), P(*block, None), P(), P(), P())

    def body(*args):
        return local((gx, gy, gz), *args)

    return jax.shard_map(body, mesh=fine, in_specs=in_specs, out_specs=out_specs, check_vma=False)
```

```python
import jax
import jax.numpy as jnp
from jax import lax
from jax.experimental import pallas as pl
from jax.experimental.pallas import tpu as pltpu
from jax.sharding import Mesh, PartitionSpec as P

BF = jnp.bfloat16
F32 = jnp.float32
ALL = ("z", "yh", "x", "c", "yl")
NEAR = ("yh", "x", "c", "yl")
FAR = ("z",)
PARAMS = pltpu.CompilerParams(vmem_limit_bytes=48 * 1024 * 1024)


def call(kernel, outs, args, scratch=(), flops=100_000_000):
    size = sum(a.size * a.dtype.itemsize for a in args) + sum(o.size * o.dtype.itemsize for o in outs)
    return pl.pallas_call(
        kernel,
        out_shape=outs,
        in_specs=[pl.BlockSpec(memory_space=pltpu.VMEM) for _ in args],
        out_specs=[pl.BlockSpec(memory_space=pltpu.VMEM) for _ in outs],
        scratch_shapes=list(scratch),
        compiler_params=PARAMS,
        cost_estimate=pl.CostEstimate(flops=flops, bytes_accessed=size, transcendentals=0),
    )(*args)


def shape(dims, dtype):
    return jax.ShapeDtypeStruct(dims, dtype)


def dot(left, right, dims=((1,), (0,))):
    return lax.dot_general(left, right, (dims, ((), ())), preferred_element_type=F32)


def row_picker(rows, step, offset):
    r = lax.broadcasted_iota(jnp.int32, (rows, rows * step), 0)
    k = lax.broadcasted_iota(jnp.int32, (rows, rows * step), 1)
    return (k == r * step + offset).astype(BF)


def with_edge(value, edge, at, shift):
    groups, depth, lanes = value.shape
    moved = pltpu.roll(value.reshape(groups * depth, lanes), shift % (groups * depth), 0)
    moved = moved.reshape(groups, depth, lanes)
    q = lax.broadcasted_iota(jnp.int32, value.shape, 1)
    return jnp.where(q == at, jnp.broadcast_to(edge[:, None, :], value.shape), moved)


def masked_row(feat, active):
    ny, mz, width = feat.shape
    z = active.shape[1]
    pair = lax.broadcasted_iota(jnp.int32, (mz, z), 1) // 2
    sel = (pair == lax.broadcasted_iota(jnp.int32, (mz, z), 0)).astype(F32)
    lane = lax.broadcasted_iota(jnp.int32, (z, width), 1) // (width // 2)
    widen = (lax.broadcasted_iota(jnp.int32, (z, width), 0) % 2 == lane).astype(BF)
    rep = jnp.broadcast_to(active.astype(F32)[:, None, :], (ny, mz, z)) * sel[None]
    m = dot(rep.astype(BF).reshape(ny * mz, z), widen).astype(BF)
    m = m.reshape(ny // 2, 2, mz, width)
    return m, feat.reshape(ny // 2, 2, mz, width) * m


def face_kernel(feat, active, pack):
    _, slabs, mz, width = pack.shape
    my = slabs - 1
    last = lax.axis_size("z") * lax.axis_size("yh") - 1
    here = lax.axis_index("z") * lax.axis_size("yh") + lax.axis_index("yh")
    keep = jnp.where(here == last, 0.0, 1.0)
    _, value = masked_row(feat[0], active[0])
    pick = row_picker(my, mz, mz - 1)
    for py in range(2):
        held = (value[:, py].astype(F32) * keep).astype(BF)
        pack[py, :my] = held
        pack[py, my] = dot(pick, held.reshape(my * mz, width)).astype(BF)


def mask_kernel(feat, active, xin, mask, act, zface):
    nx, _, my, mz, width = xin.shape
    pick = row_picker(my, mz, mz - 1)
    count = None
    for x in range(nx):
        m, value = masked_row(feat[x], active[x])
        for py in range(2):
            part = m[:, py]
            mask[x, py] = part
            held = value[:, py]
            xin[x, py] = held
            zface[x, py] = dot(pick, held.reshape(my * mz, width)).astype(BF)
            term = part.astype(F32).reshape(my * mz, width)
            count = term if count is None else count + term
        if x % 2 == 1:
            both = count + pltpu.roll(count, width // 2, 1)
            act[x // 2] = (both > 0.0).astype(F32).astype(BF).reshape(my, mz, width)
            count = None


def tile_of(xin, xh, yh, row, b):
    py = 0 if b == 1 else 1
    my = xin.shape[2]
    base = xh[py, :my] if row == 0 else xin[row - 1, py]
    if b == 0:
        base = jnp.concatenate([yh[row][None], base[: my - 1]], axis=0)
    return base


def edge_of(zh, row, b):
    base = zh[2 * row + (0 if b == 1 else 1)]
    if b == 0:
        wide = base.astype(F32)
        first = zh[zh.shape[0] - 1].astype(F32)[row : row + 1]
        wide = jnp.concatenate([first, wide[: wide.shape[0] - 1]], axis=0)
        base = wide.astype(BF)
    return base


TAPS = [(a, b) for a in range(3) for b in range(3)]


def forward_kernel(xin, act, xh, yh, zh, weight, pre, stats, wmat):
    mx, my, mz, cout = pre.shape
    width = xin.shape[4]
    half = width // 2
    zero = jnp.zeros((half, cout), BF)
    for i, (a, b) in enumerate(TAPS):
        lo = i * width
        wmat[lo : lo + half, :cout] = weight[a, b, 1]
        wmat[lo + half : lo + width, :cout] = weight[a, b, 2]
        wmat[lo : lo + half, cout:] = zero
        wmat[lo + half : lo + width, cout:] = weight[a, b, 0]
    rows = my * mz
    total = jnp.zeros((1, cout), F32)
    count = jnp.zeros((1, cout), F32)
    w = wmat[...]
    for m in range(mx):
        left = jnp.concatenate(
            [tile_of(xin, xh, yh, 2 * m + a, b).reshape(rows, width) for a, b in TAPS], axis=1
        )
        edge = jnp.concatenate([edge_of(zh, 2 * m + a, b) for a, b in TAPS], axis=1)
        out = dot(left, w)
        rim = dot(edge, w[:, cout:])
        prev = with_edge(out[:, cout:].reshape(my, mz, cout), rim, 0, 1)
        value = out[:, :cout].reshape(my, mz, cout) + prev
        pre[m] = value
        on = act[m].astype(F32)
        total = total + jnp.sum((on * value).reshape(rows, cout), axis=0, keepdims=True)
        count = count + jnp.sum(on.reshape(rows, cout), axis=0, keepdims=True)
    mean = total / jnp.maximum(count, 1.0)
    squares = jnp.zeros((1, cout), F32)
    for m in range(mx):
        apart = pre[m].reshape(rows, cout) - mean
        on = act[m].astype(F32).reshape(rows, cout)
        squares = squares + jnp.sum(on * apart * apart, axis=0, keepdims=True)
    for i in range(stats.shape[0]):
        stats[i, 0:1] = count
        stats[i, 1:2] = total
        stats[i, 2:3] = squares


def slope_kernel(pre, act, cot, par, out, slope, sums):
    mx, my, mz, cout = pre.shape
    rows = my * mz
    mean, rstd, gain, bias = (par[i : i + 1] for i in range(4))
    first = jnp.zeros((1, cout), F32)
    second = jnp.zeros((1, cout), F32)
    for m in range(mx):
        on = act[m].astype(F32).reshape(rows, cout)
        hat = (pre[m].reshape(rows, cout) - mean) * rstd
        normed = hat * gain + bias
        sig = jax.nn.sigmoid(normed)
        out[m] = (on * normed * sig).astype(BF).reshape(my, mz, cout)
        tilt = on * cot[m].astype(F32).reshape(rows, cout) * sig * (1.0 + normed * (1.0 - sig))
        slope[m] = tilt.reshape(my, mz, cout)
        first = first + jnp.sum(tilt, axis=0, keepdims=True)
        second = second + jnp.sum(tilt * hat, axis=0, keepdims=True)
    for i in range(sums.shape[0]):
        sums[i, 0:1] = first
        sums[i, 1:2] = second


def weight_kernel(slope, pre, act, par, xin, xh, yh, zh, dpre, pack, zface, dw):
    mx, my, mz, cout = pre.shape
    width = xin.shape[4]
    half = width // 2
    rows = my * mz
    mean, rstd, gain, shift, tilt = (par[i : i + 1] for i in range(5))
    pick = row_picker(my, mz, 0)
    last = lax.broadcasted_iota(jnp.int32, (my, mz, cout), 1) == mz - 1
    total = None
    rims = []
    for m in range(mx):
        on = act[m].astype(F32).reshape(rows, cout)
        hat = (pre[m].reshape(rows, cout) - mean) * rstd
        grad = on * rstd * gain * (slope[m].reshape(rows, cout) - shift - hat * tilt)
        held = grad.astype(BF)
        dpre[m] = held.reshape(my, mz, cout)
        first = dot(pick, held)
        zface[m] = first.astype(BF)
        if m == 0:
            here = lax.axis_index("z") * lax.axis_size("yh") + lax.axis_index("yh")
            keep = jnp.where(here == 0, 0.0, 1.0)
            pack[:my] = (held.astype(F32) * keep).astype(BF).reshape(my, mz, cout)
            pack[my] = (first * keep).astype(BF)
        rims.append(first)
        wide = held.astype(F32)
        after = pltpu.roll(wide, rows - 1, 0).reshape(my, mz, cout)
        after = jnp.where(last, 0.0, after).reshape(rows, cout)
        right = jnp.concatenate([wide.T, after.T], axis=0).astype(BF)
        left = jnp.concatenate(
            [tile_of(xin, xh, yh, 2 * m + a, b).reshape(rows, width) for a, b in TAPS], axis=1
        )
        term = dot(right, left)
        total = term if total is None else total + term
    rim = jnp.concatenate(rims, axis=0).T.astype(BF)
    edge = jnp.concatenate(
        [
            jnp.concatenate([edge_of(zh, 2 * m + a, b) for a, b in TAPS], axis=1)
            for m in range(mx)
        ],
        axis=0,
    )
    low = total[cout:] + dot(rim, edge)
    for i in range(len(TAPS)):
        at = i * width
        own = total[:cout, at : at + width].T
        prev = low[:, at : at + width].T
        dw[3 * half * i : 3 * half * i + half] = prev[half:].astype(BF)
        dw[3 * half * i + half : 3 * half * (i + 1)] = own.astype(BF)
    used = 3 * half * len(TAPS)
    if dw.shape[0] > used:
        dw[used:] = jnp.zeros((dw.shape[0] - used, cout), BF)


def input_kernel(dpre, xh, yh, zh, wmat, mask, out, ext, nxt):
    mx, my, mz, cout = dpre.shape
    width = mask.shape[4]
    rows = my * mz
    for r in range(mx + 1):
        base = dpre[r] if r < mx else xh[:my]
        ext[r, :my] = base
        ext[r, my] = yh[r]
        whole = jnp.concatenate([base, yh[r][None]], axis=0).astype(F32)
        rim = jnp.concatenate([zh[r].astype(F32), zh[mx + 1].astype(F32)[r : r + 1]], axis=0)
        nxt[r] = with_edge(whole, rim, mz - 1, -1).astype(BF)
    taps = (((1, 0),), ((2, 0), (0, 1)))
    for m in range(mx):
        for px in range(2):
            for py in range(2):
                left, right = ([], [])
                for a, sx in taps[px]:
                    for b, sy in taps[py]:
                        left.append(ext[m + sx, sy : sy + my].reshape(rows, cout))
                        left.append(nxt[m + sx, sy : sy + my].reshape(rows, cout))
                        at = (a * 3 + b) * width
                        right.append(wmat[at : at + width])
                left = jnp.concatenate(left, axis=1)
                right = jnp.concatenate(right, axis=1)
                value = dot(left, right, ((1,), (1,)))
                x = 2 * m + px
                value = value * mask[x, py].astype(F32).reshape(rows, width)
                out[x, :, py] = value.astype(BF).reshape(my, mz, width)


def moved(value, axes, by):
    count = lax.axis_size(axes)
    return lax.ppermute(value, axes, [(i, (i + by) % count) for i in range(count)])


GX, GY, GZ = (("z", "yh"), ("x", "c"), ("yl",))


def beyond(value, axes, by):
    end = lax.axis_size(axes) - 1 if by > 0 else 0
    keep = (lax.axis_index(axes) != end).astype(value.dtype)
    return moved(value * keep, axes, by)


def slab(rows, like):
    return jnp.pad(rows, ((0, like - rows.shape[0]), (0, 0)))[None]


def exchanged(value, axes):
    return lax.all_to_all(value, axes, 0, 0)


def spread(value, axes):
    return exchanged(jnp.broadcast_to(value, (lax.axis_size(axes),) + value.shape), axes)


def merged(parts):
    counts, sums, squares = (parts[:, 0], parts[:, 1], parts[:, 2])
    count = jnp.sum(counts, axis=0)
    total = jnp.sum(sums, axis=0)
    mean = total / jnp.maximum(count, 1.0)
    apart = sums / jnp.maximum(counts, 1.0) - mean
    return jnp.stack([count, total, jnp.sum(squares + counts * apart * apart, axis=0)])


def local(features, active, weight, gain, bias, cotangent):
    vx, vy, mz, width = features.shape
    cin = width // 2
    cout = weight.shape[4]
    mx, my = (vx // 2, vy // 2)
    near = lax.axis_size(NEAR)
    pack = pl.pallas_call(
        face_kernel,
        out_shape=shape((2, my + 1, mz, width), BF),
        grid=(1,),
        in_specs=[
            pl.BlockSpec((1, vy, mz, width), lambda i: (0, 0, 0, 0)),
            pl.BlockSpec((1, vy, 2 * mz), lambda i: (0, 0, 0)),
        ],
        out_specs=pl.BlockSpec((2, my + 1, mz, width), lambda i: (0, 0, 0, 0)),
        compiler_params=PARAMS,
        cost_estimate=pl.CostEstimate(flops=10_000_000, bytes_accessed=400_000, transcendentals=0),
    )(features[vx - 1 :], active[vx - 1 :])
    xh = moved(pack, GX, 1)
    xin, mask, act, zface = call(
        mask_kernel,
        [
            shape((vx, 2, my, mz, width), BF),
            shape((vx, 2, my, mz, width), BF),
            shape((mx, my, mz, width), BF),
            shape((vx, 2, my, width), BF),
        ],
        [features, active],
    )
    yface = jnp.concatenate([xh[1:2, my - 1], xin[:, 1, my - 1]], axis=0)
    zfaces = jnp.concatenate([xh[None, :, my], zface], axis=0)
    rows = vx + 1
    yh = beyond(jnp.concatenate([yface, slab(zfaces[:, 1, my - 1], mz)], axis=0), GY, 1)
    zfaces = jnp.concatenate([zfaces.reshape(2 * rows, my, width), yh[rows:]], axis=0)
    zh = beyond(zfaces, GZ, 1)
    pre, stats, wmat = call(
        forward_kernel,
        [
            shape((mx, my, mz, cout), F32),
            shape((near, 3, cout), F32),
            shape((9 * width, 2 * cout), BF),
        ],
        [xin, act, xh, yh, zh, weight],
        flops=1_200_000_000,
    )
    stats = merged(spread(merged(exchanged(stats, NEAR)), FAR))
    count = stats[0]
    mean = stats[1] / count
    rstd = lax.rsqrt(stats[2] / count + 1e-05)
    par = jnp.stack([mean, rstd, gain, bias])
    section_out, slope, sums = call(
        slope_kernel,
        [
            shape((mx, my, mz, cout), BF),
            shape((mx, my, mz, cout), F32),
            shape((near, 2, cout), F32),
        ],
        [pre, act, cotangent, par],
    )
    sums = jnp.sum(spread(jnp.sum(exchanged(sums, NEAR), axis=0), FAR), axis=0)
    shift_gradient = sums[0] / count
    gain_gradient = sums[1] / count
    par = jnp.stack([mean, rstd, gain, shift_gradient, gain_gradient])
    taps = 27 * cin
    rows = -(-taps // (16 * near)) * 16
    if near * (rows - 8) >= taps and near * (rows - 8) % 16 == 0:
        rows = rows - 8
    dpre, pack, zface, dw = call(
        weight_kernel,
        [
            shape((mx, my, mz, cout), BF),
            shape((my + 1, mz, cout), BF),
            shape((mx, my, cout), BF),
            shape((near * rows, cout), BF),
        ],
        [slope, pre, act, par, xin, xh, yh, zh],
        flops=1_200_000_000,
    )
    xd = moved(pack, GX, -1)
    mine = jnp.sum(exchanged(dw.reshape(near, rows, cout), NEAR).astype(F32), axis=0)
    zfaces = jnp.concatenate([zface, xd[my:]], axis=0)
    yd = jnp.concatenate([dpre[:, 0], xd[:1], slab(zfaces[:, 0], mz)], axis=0)
    yd = beyond(yd, GY, -1)
    zd = beyond(jnp.concatenate([zfaces, yd[mx + 1 :]], axis=0), GZ, -1)
    mine = jnp.sum(spread(mine, FAR), axis=0) / count[0]
    grad_weight = spread(mine.astype(BF), NEAR).reshape(near * rows, cout)[:taps]
    grad_weight = grad_weight.astype(F32).reshape(weight.shape)
    (grad_features,) = call(
        input_kernel,
        [shape((vx, my, 2, mz, width), BF)],
        [dpre, xd, yd, zd, wmat, mask],
        scratch=[pltpu.VMEM((mx + 1, my + 1, mz, cout), BF)] * 2,
        flops=1_200_000_000,
    )
    grad_features = grad_features.reshape(features.shape)
    return (section_out, grad_features, grad_weight, gain_gradient, shift_gradient)


def solution(mesh):
    gx, gy, gz = (mesh.shape[name] for name in ("gx", "gy", "gz"))
    fine = Mesh(mesh.devices.reshape(gx // 2, 2, gy // 2, 2, gz), ALL)
    block = (("z", "yh"), ("x", "c"), "yl")
    in_specs = (P(*block, None), P(*block), P(), P(), P(), P(*block, None))
    out_specs = (P(*block, None), P(*block, None), P(), P(), P())
    return jax.shard_map(local, mesh=fine, in_specs=in_specs, out_specs=out_specs, check_vma=False)
```

```python
import jax
import jax.numpy as jnp
from jax import lax
from jax.experimental import pallas as pl
from jax.experimental.pallas import tpu as pltpu
from jax.sharding import Mesh, PartitionSpec as P

BF = jnp.bfloat16
F32 = jnp.float32
ALL = ("z", "yh", "x", "c", "yl")
NEAR = ("yh", "x", "c", "yl")
FAR = ("z",)
PARAMS = pltpu.CompilerParams(vmem_limit_bytes=48 * 1024 * 1024)


def call(kernel, outs, args, scratch=(), flops=100_000_000):
    size = sum(a.size * a.dtype.itemsize for a in args) + sum(o.size * o.dtype.itemsize for o in outs)
    return pl.pallas_call(
        kernel,
        out_shape=outs,
        in_specs=[pl.BlockSpec(memory_space=pltpu.VMEM) for _ in args],
        out_specs=[pl.BlockSpec(memory_space=pltpu.VMEM) for _ in outs],
        scratch_shapes=list(scratch),
        compiler_params=PARAMS,
        cost_estimate=pl.CostEstimate(flops=flops, bytes_accessed=size, transcendentals=0),
    )(*args)


def shape(dims, dtype):
    return jax.ShapeDtypeStruct(dims, dtype)


def dot(left, right, dims=((1,), (0,))):
    return lax.dot_general(left, right, (dims, ((), ())), preferred_element_type=F32)


def row_picker(rows, step, offset):
    r = lax.broadcasted_iota(jnp.int32, (rows, rows * step), 0)
    k = lax.broadcasted_iota(jnp.int32, (rows, rows * step), 1)
    return (k == r * step + offset).astype(BF)


def with_edge(value, edge, at, shift):
    groups, depth, lanes = value.shape
    moved = pltpu.roll(value.reshape(groups * depth, lanes), shift % (groups * depth), 0)
    moved = moved.reshape(groups, depth, lanes)
    q = lax.broadcasted_iota(jnp.int32, value.shape, 1)
    return jnp.where(q == at, jnp.broadcast_to(edge[:, None, :], value.shape), moved)


def masked_row(feat, active):
    ny, mz, width = feat.shape
    z = active.shape[1]
    pair = lax.broadcasted_iota(jnp.int32, (mz, z), 1) // 2
    sel = (pair == lax.broadcasted_iota(jnp.int32, (mz, z), 0)).astype(F32)
    lane = lax.broadcasted_iota(jnp.int32, (z, width), 1) // (width // 2)
    widen = (lax.broadcasted_iota(jnp.int32, (z, width), 0) % 2 == lane).astype(BF)
    rep = jnp.broadcast_to(active.astype(F32)[:, None, :], (ny, mz, z)) * sel[None]
    m = dot(rep.astype(BF).reshape(ny * mz, z), widen).astype(BF)
    m = m.reshape(ny // 2, 2, mz, width)
    return m, feat.reshape(ny // 2, 2, mz, width) * m


def face_kernel(feat, active, pack):
    _, slabs, mz, width = pack.shape
    my = slabs - 1
    last = lax.axis_size("z") * lax.axis_size("yh") - 1
    here = lax.axis_index("z") * lax.axis_size("yh") + lax.axis_index("yh")
    keep = jnp.where(here == last, 0.0, 1.0)
    _, value = masked_row(feat[0], active[0])
    pick = row_picker(my, mz, mz - 1)
    for py in range(2):
        held = (value[:, py].astype(F32) * keep).astype(BF)
        pack[py, :my] = held
        pack[py, my] = dot(pick, held.reshape(my * mz, width)).astype(BF)


def mask_kernel(feat, active, xin, mask, act, zface):
    nx, _, my, mz, width = xin.shape
    pick = row_picker(my, mz, mz - 1)
    count = None
    for x in range(nx):
        m, value = masked_row(feat[x], active[x])
        for py in range(2):
            part = m[:, py]
            mask[x, py] = part
            held = value[:, py]
            xin[x, py] = held
            zface[x, py] = dot(pick, held.reshape(my * mz, width)).astype(BF)
            term = part.astype(F32).reshape(my * mz, width)
            count = term if count is None else count + term
        if x % 2 == 1:
            both = count + pltpu.roll(count, width // 2, 1)
            act[x // 2] = (both > 0.0).astype(F32).astype(BF).reshape(my, mz, width)
            count = None


def tile_of(xin, xh, yh, row, b):
    py = 0 if b == 1 else 1
    my = xin.shape[2]
    base = xh[py, :my] if row == 0 else xin[row - 1, py]
    if b == 0:
        base = jnp.concatenate([yh[row][None], base[: my - 1]], axis=0)
    return base


def edge_of(zh, row, b):
    base = zh[2 * row + (0 if b == 1 else 1)]
    if b == 0:
        wide = base.astype(F32)
        first = zh[zh.shape[0] - 1].astype(F32)[row : row + 1]
        wide = jnp.concatenate([first, wide[: wide.shape[0] - 1]], axis=0)
        base = wide.astype(BF)
    return base


TAPS = [(a, b) for a in range(3) for b in range(3)]


def forward_kernel(xin, act, xh, yh, zh, weight, pre, stats, wmat):
    mx, my, mz, cout = pre.shape
    width = xin.shape[4]
    half = width // 2
    zero = jnp.zeros((half, cout), BF)
    for i, (a, b) in enumerate(TAPS):
        lo = i * width
        wmat[lo : lo + half, :cout] = weight[a, b, 1]
        wmat[lo + half : lo + width, :cout] = weight[a, b, 2]
        wmat[lo : lo + half, cout:] = zero
        wmat[lo + half : lo + width, cout:] = weight[a, b, 0]
    rows = my * mz
    total = jnp.zeros((1, cout), F32)
    count = jnp.zeros((1, cout), F32)
    w = wmat[...]
    for m in range(mx):
        left = jnp.concatenate(
            [tile_of(xin, xh, yh, 2 * m + a, b).reshape(rows, width) for a, b in TAPS], axis=1
        )
        edge = jnp.concatenate([edge_of(zh, 2 * m + a, b) for a, b in TAPS], axis=1)
        out = dot(left, w)
        rim = dot(edge, w[:, cout:])
        prev = with_edge(out[:, cout:].reshape(my, mz, cout), rim, 0, 1)
        value = out[:, :cout].reshape(my, mz, cout) + prev
        pre[m] = value
        on = act[m].astype(F32)
        total = total + jnp.sum((on * value).reshape(rows, cout), axis=0, keepdims=True)
        count = count + jnp.sum(on.reshape(rows, cout), axis=0, keepdims=True)
    mean = total / jnp.maximum(count, 1.0)
    squares = jnp.zeros((1, cout), F32)
    for m in range(mx):
        apart = pre[m].reshape(rows, cout) - mean
        on = act[m].astype(F32).reshape(rows, cout)
        squares = squares + jnp.sum(on * apart * apart, axis=0, keepdims=True)
    for i in range(stats.shape[0]):
        stats[i, 0:1] = count
        stats[i, 1:2] = total
        stats[i, 2:3] = squares


def split(value, parts):
    out = []
    for _ in range(parts):
        out.append(value.astype(BF).astype(F32))
        value = value - out[-1]
    return out


def rounded(value):
    high, low = split(value, 2)
    return high + low


def outer(column, rows):
    return lax.dot_general(
        column, rows, (((0,), (0,)), ((), ())), precision=lax.Precision.HIGHEST, preferred_element_type=F32
    )


def write_chunk(ref, i, body, column, common):
    left, right = common
    line = lax.broadcasted_iota(jnp.int32, left.shape, 0)
    for at, part in enumerate(split(column, 3)):
        left = jnp.where(line == at, part, left)
    ref[i] = jnp.concatenate([body, jnp.concatenate([left, right], axis=1)], axis=0).astype(BF)


def common_rows(first, second, alpha, beta, high):
    zero = jnp.zeros_like(first)
    rows = split(first, 3) + split(second, 3) + split(alpha, 3) + split(beta, 2) + split(high, 2)
    return (
        jnp.concatenate([zero] * 3 + rows[:5], axis=0),
        jnp.concatenate(rows[5:], axis=0),
    )


def read_chunks(ref):
    devices, depth, _ = ref.shape
    rows = depth - 8
    cout = ref.shape[2] // 2
    slopes = hats = None
    firsts = seconds = None
    columns, vectors, betas = ([], [], None)
    for j in range(devices):
        value = ref[j].astype(F32)
        left, right = (value[rows:, :cout], value[rows:, cout:])
        part = value[:rows, cout:]
        beta = right[4:5] + right[5:6]
        term = value[:rows, :cout] + part * beta
        first = left[3:4] + left[4:5] + left[5:6]
        second = left[6:7] + left[7:8] + right[0:1]
        alpha = right[1:2] + right[2:3] + right[3:4]
        columns.append(left[0:1] + left[1:2] + left[2:3])
        vectors.append(jnp.concatenate([alpha, right[6:7] + right[7:8]], axis=1))
        if j == 0:
            slopes, hats, firsts, seconds, betas = (term, part, first, second, beta)
        else:
            slopes, hats = (slopes + term, hats + part)
            firsts, seconds, betas = (firsts + first, seconds + second, betas + beta)
    columns = jnp.concatenate(columns, axis=0)
    vectors = jnp.concatenate(vectors, axis=0)
    both = outer(columns, vectors)[:rows]
    slopes = slopes + both[:, :cout]
    hats = hats + both[:, cout:]
    column = jnp.sum(columns, axis=0, keepdims=True)
    middle = jnp.sum(vectors, axis=0, keepdims=True) / devices
    return slopes, hats, column, firsts, seconds, middle[:, :cout], betas / devices, middle[:, cout:]


def eight(row):
    return jnp.broadcast_to(row, (8, row.shape[1]))


def lone(row):
    return jnp.where(lax.broadcasted_iota(jnp.int32, (8, row.shape[1]), 0) == 0, eight(row), 0.0)


def slope_kernel(pre, act, cot, par, xin, xh, yh, zh, out, slope, big, acc):
    mx, my, mz, cout = pre.shape
    width = xin.shape[4]
    half = width // 2
    rows = my * mz
    mean, rstd, gain, bias = (par[i : i + 1] for i in range(4))
    first, second, count, high, square = (jnp.zeros((1, cout), F32) for _ in range(5))
    for m in range(mx):
        on = act[m].astype(F32).reshape(rows, cout)
        hat = (pre[m].reshape(rows, cout) - mean) * rstd
        normed = hat * gain + bias
        sig = jax.nn.sigmoid(normed)
        out[m] = (on * normed * sig).astype(BF).reshape(my, mz, cout)
        tilt = on * cot[m].astype(F32).reshape(rows, cout) * sig * (1.0 + normed * (1.0 - sig))
        slope[m] = tilt.reshape(my, mz, cout)
        first = first + jnp.sum(tilt, axis=0, keepdims=True)
        second = second + jnp.sum(tilt * hat, axis=0, keepdims=True)
        count = count + jnp.sum(on, axis=0, keepdims=True)
        high = high + jnp.sum(on * hat, axis=0, keepdims=True)
        square = square + jnp.sum(on * hat * hat, axis=0, keepdims=True)
    some = jnp.maximum(count, 1.0)
    alpha = first / some
    high = rounded(high / some)
    beta = (second - high * first) / jnp.maximum(square - count * high * high, 0.01 * some)
    beta = rounded(beta)
    pick = row_picker(my, mz, 0)
    last = lax.broadcasted_iota(jnp.int32, (my, mz, cout), 1) == mz - 1
    total = None
    rims = [[], [], []]
    for m in range(mx):
        on = act[m].astype(F32).reshape(rows, cout)
        hat = on * ((pre[m].reshape(rows, cout) - mean) * rstd - high)
        rest = slope[m].reshape(rows, cout) - on * alpha - hat * beta
        here, after = ([], [])
        for i, part in enumerate((rest, hat, on)):
            held = part.astype(BF)
            keep = 8 if i == 2 else cout
            rims[i].append(dot(pick, held))
            wide = held.astype(F32)
            nxt = pltpu.roll(wide, rows - 1, 0).reshape(my, mz, cout)
            nxt = jnp.where(last, 0.0, nxt).reshape(rows, cout)
            here.append(wide.T[:keep])
            after.append(nxt.T[:keep])
        right = jnp.concatenate(here + after, axis=0).astype(BF)
        left = jnp.concatenate(
            [tile_of(xin, xh, yh, 2 * m + a, b).reshape(rows, width) for a, b in TAPS], axis=1
        )
        term = dot(right, left)
        total = term if total is None else total + term
    rim = [jnp.concatenate(parts, axis=0).T for parts in rims]
    rim = jnp.concatenate([rim[0], rim[1], rim[2][:8]], axis=0).astype(BF)
    edge = jnp.concatenate(
        [
            jnp.concatenate([edge_of(zh, 2 * m + a, b) for a, b in TAPS], axis=1)
            for m in range(mx)
        ],
        axis=0,
    )
    size = 2 * cout + 8
    own = total[:size]
    low = total[size:] + dot(rim, edge)
    taps = 3 * len(TAPS)
    for i in range(len(TAPS)):
        at = i * width
        to = 3 * half * i
        acc[to : to + half] = low[: 2 * cout, at : at + width].T[half:]
        acc[to + half : to + 3 * half] = own[: 2 * cout, at : at + width].T
    if acc.shape[0] > half * taps:
        acc[half * taps :] = jnp.zeros((acc.shape[0] - half * taps, 2 * cout), F32)
    common = common_rows(first, second, alpha, beta, high)
    lane = lax.broadcasted_iota(jnp.int32, (8, width), 1)
    near, depth, _ = big.shape
    depth = depth - 8
    for n in range(near):
        column = jnp.zeros((8, width), F32)
        for tap in range(taps):
            start = half * tap - depth * n
            lo, hi = (max(start, 0), min(start + half, depth))
            if lo < hi:
                at = tap // 3 * width
                row = (low if tap % 3 == 0 else own)[2 * cout :, at : at + width]
                shift = (start - (0 if tap % 3 == 1 else half)) % width
                if shift:
                    row = pltpu.roll(row, shift, 1)
                column = jnp.where((lane >= lo) & (lane < hi), row, column)
        write_chunk(big, n, acc[depth * n : depth * (n + 1)], column, common)


def near_kernel(parts, out):
    slopes, hats, column, first, second, alpha, beta, high = read_chunks(parts)
    rows = slopes.shape[0]
    cout = slopes.shape[1]
    beta, high = (rounded(beta), rounded(high))
    both = outer(lone(column), lone(jnp.concatenate([alpha, high], axis=1)))[:rows]
    hats = hats - both[:, cout:]
    slopes = slopes - both[:, :cout] - hats * beta
    common = common_rows(first, second, alpha, beta, high)
    body = jnp.concatenate([slopes, hats], axis=1)
    for i in range(out.shape[0]):
        write_chunk(out, i, body, eight(column), common)


def far_kernel(parts, par, slope, pre, act, dw, grads, dpre, pack, zface):
    mx, my, mz, cout = pre.shape
    rows = my * mz
    mean, rstd, gain, _, count = (par[i : i + 1] for i in range(5))
    slopes, hats, column, first, second, _, _, _ = read_chunks(parts)
    shift, tilt = (first / count, second / count)
    grads[0:1] = shift
    grads[1:2] = tilt
    pick = row_picker(my, mz, 0)
    for m in range(mx):
        on = act[m].astype(F32).reshape(rows, cout)
        hat = (pre[m].reshape(rows, cout) - mean) * rstd
        grad = on * rstd * gain * (slope[m].reshape(rows, cout) - shift - hat * tilt)
        held = grad.astype(BF)
        dpre[m] = held.reshape(my, mz, cout)
        edge = dot(pick, held)
        zface[m] = edge.astype(BF)
        if m == 0:
            here = lax.axis_index("z") * lax.axis_size("yh") + lax.axis_index("yh")
            keep = jnp.where(here == 0, 0.0, 1.0)
            pack[:my] = (held.astype(F32) * keep).astype(BF).reshape(my, mz, cout)
            pack[my] = (edge * keep).astype(BF)
    value = slopes - outer(lone(column), lone(shift))[: slopes.shape[0]] - hats * tilt
    value = (value * (rstd * gain / count)).astype(BF)
    for i in range(dw.shape[0]):
        dw[i] = value


def input_kernel(dpre, xh, yh, zh, wmat, mask, out, ext, nxt):
    mx, my, mz, cout = dpre.shape
    width = mask.shape[4]
    rows = my * mz
    for r in range(mx + 1):
        base = dpre[r] if r < mx else xh[:my]
        ext[r, :my] = base
        ext[r, my] = yh[r]
        whole = jnp.concatenate([base, yh[r][None]], axis=0).astype(F32)
        rim = jnp.concatenate([zh[r].astype(F32), zh[mx + 1].astype(F32)[r : r + 1]], axis=0)
        nxt[r] = with_edge(whole, rim, mz - 1, -1).astype(BF)
    taps = (((1, 0),), ((2, 0), (0, 1)))
    for m in range(mx):
        for px in range(2):
            for py in range(2):
                left, right = ([], [])
                for a, sx in taps[px]:
                    for b, sy in taps[py]:
                        left.append(ext[m + sx, sy : sy + my].reshape(rows, cout))
                        left.append(nxt[m + sx, sy : sy + my].reshape(rows, cout))
                        at = (a * 3 + b) * width
                        right.append(wmat[at : at + width])
                left = jnp.concatenate(left, axis=1)
                right = jnp.concatenate(right, axis=1)
                value = dot(left, right, ((1,), (1,)))
                x = 2 * m + px
                value = value * mask[x, py].astype(F32).reshape(rows, width)
                out[x, :, py] = value.astype(BF).reshape(my, mz, width)


def moved(value, axes, by):
    count = lax.axis_size(axes)
    return lax.ppermute(value, axes, [(i, (i + by) % count) for i in range(count)])


GX, GY, GZ = (("z", "yh"), ("x", "c"), ("yl",))


def beyond(value, axes, by):
    end = lax.axis_size(axes) - 1 if by > 0 else 0
    keep = (lax.axis_index(axes) != end).astype(value.dtype)
    return moved(value * keep, axes, by)


def slab(rows, like):
    return jnp.pad(rows, ((0, like - rows.shape[0]), (0, 0)))[None]


def exchanged(value, axes):
    return lax.all_to_all(value, axes, 0, 0)


def spread(value, axes):
    return exchanged(jnp.broadcast_to(value, (lax.axis_size(axes),) + value.shape), axes)


def merged(parts):
    counts, sums, squares = (parts[:, 0], parts[:, 1], parts[:, 2])
    count = jnp.sum(counts, axis=0)
    total = jnp.sum(sums, axis=0)
    mean = total / jnp.maximum(count, 1.0)
    apart = sums / jnp.maximum(counts, 1.0) - mean
    return jnp.stack([count, total, jnp.sum(squares + counts * apart * apart, axis=0)])


def local(features, active, weight, gain, bias, cotangent):
    vx, vy, mz, width = features.shape
    cin = width // 2
    cout = weight.shape[4]
    mx, my = (vx // 2, vy // 2)
    near = lax.axis_size(NEAR)
    pack = pl.pallas_call(
        face_kernel,
        out_shape=shape((2, my + 1, mz, width), BF),
        grid=(1,),
        in_specs=[
            pl.BlockSpec((1, vy, mz, width), lambda i: (0, 0, 0, 0)),
            pl.BlockSpec((1, vy, 2 * mz), lambda i: (0, 0, 0)),
        ],
        out_specs=pl.BlockSpec((2, my + 1, mz, width), lambda i: (0, 0, 0, 0)),
        compiler_params=PARAMS,
        cost_estimate=pl.CostEstimate(flops=10_000_000, bytes_accessed=400_000, transcendentals=0),
    )(features[vx - 1 :], active[vx - 1 :])
    xh = moved(pack, GX, 1)
    xin, mask, act, zface = call(
        mask_kernel,
        [
            shape((vx, 2, my, mz, width), BF),
            shape((vx, 2, my, mz, width), BF),
            shape((mx, my, mz, width), BF),
            shape((vx, 2, my, width), BF),
        ],
        [features, active],
    )
    yface = jnp.concatenate([xh[1:2, my - 1], xin[:, 1, my - 1]], axis=0)
    zfaces = jnp.concatenate([xh[None, :, my], zface], axis=0)
    rows = vx + 1
    yh = beyond(jnp.concatenate([yface, slab(zfaces[:, 1, my - 1], mz)], axis=0), GY, 1)
    zfaces = jnp.concatenate([zfaces.reshape(2 * rows, my, width), yh[rows:]], axis=0)
    zh = beyond(zfaces, GZ, 1)
    pre, stats, wmat = call(
        forward_kernel,
        [
            shape((mx, my, mz, cout), F32),
            shape((near, 3, cout), F32),
            shape((9 * width, 2 * cout), BF),
        ],
        [xin, act, xh, yh, zh, weight],
        flops=1_200_000_000,
    )
    stats = merged(spread(merged(exchanged(stats, NEAR)), FAR))
    count = stats[0]
    mean = stats[1] / count
    rstd = lax.rsqrt(stats[2] / count + 1e-05)
    par = jnp.stack([mean, rstd, gain, bias, count])
    taps = 27 * cin
    rows = -(-taps // (8 * near)) * 8
    section_out, slope, big = call(
        slope_kernel,
        [
            shape((mx, my, mz, cout), BF),
            shape((mx, my, mz, cout), F32),
            shape((near, rows + 8, 2 * cout), BF),
        ],
        [pre, act, cotangent, par, xin, xh, yh, zh],
        scratch=[pltpu.VMEM((near * rows, 2 * cout), F32)],
        flops=2_400_000_000,
    )
    far = lax.axis_size(FAR)
    (big,) = call(near_kernel, [shape((far, rows + 8, 2 * cout), BF)], [exchanged(big, NEAR)])
    dw, grads, dpre, pack, zface = call(
        far_kernel,
        [
            shape((near, rows, cout), BF),
            shape((2, cout), F32),
            shape((mx, my, mz, cout), BF),
            shape((my + 1, mz, cout), BF),
            shape((mx, my, cout), BF),
        ],
        [exchanged(big, FAR), par, slope, pre, act],
    )
    shift_gradient, gain_gradient = (grads[0], grads[1])
    xd = moved(pack, GX, -1)
    zfaces = jnp.concatenate([zface, xd[my:]], axis=0)
    yd = jnp.concatenate([dpre[:, 0], xd[:1], slab(zfaces[:, 0], mz)], axis=0)
    yd = beyond(yd, GY, -1)
    zd = beyond(jnp.concatenate([zfaces, yd[mx + 1 :]], axis=0), GZ, -1)
    grad_weight = exchanged(dw, NEAR).reshape(near * rows, cout)[:taps]
    grad_weight = grad_weight.astype(F32).reshape(weight.shape)
    (grad_features,) = call(
        input_kernel,
        [shape((vx, my, 2, mz, width), BF)],
        [dpre, xd, yd, zd, wmat, mask],
        scratch=[pltpu.VMEM((mx + 1, my + 1, mz, cout), BF)] * 2,
        flops=1_200_000_000,
    )
    grad_features = grad_features.reshape(features.shape)
    return (section_out, grad_features, grad_weight, gain_gradient, shift_gradient)


def solution(mesh):
    gx, gy, gz = (mesh.shape[name] for name in ("gx", "gy", "gz"))
    fine = Mesh(mesh.devices.reshape(gx // 2, 2, gy // 2, 2, gz), ALL)
    block = (("z", "yh"), ("x", "c"), "yl")
    in_specs = (P(*block, None), P(*block), P(), P(), P(), P(*block, None))
    out_specs = (P(*block, None), P(*block, None), P(), P(), P())
    return jax.shard_map(local, mesh=fine, in_specs=in_specs, out_specs=out_specs, check_vma=False)
```

```python
import jax
import jax.numpy as jnp
from jax import lax
from jax.experimental import pallas as pl
from jax.experimental.pallas import tpu as pltpu
from jax.sharding import Mesh, PartitionSpec as P

BF = jnp.bfloat16
F32 = jnp.float32
ALL = ("z", "yh", "x", "c", "yl")
NEAR = ("c", "yh", "x", "yl")
PLANE = ("yh", "x", "yl")
GX, GY, GZ = (("z", "yh"), ("x", "c"), ("yl",))
FAR = ("z",)
PARAMS = pltpu.CompilerParams(vmem_limit_bytes=24 * 1024 * 1024)
WIDE = pltpu.CompilerParams(vmem_limit_bytes=60 * 1024 * 1024)


def call(kernel, outs, args, scratch=(), flops=100_000_000):
    size = sum(a.size * a.dtype.itemsize for a in args) + sum(o.size * o.dtype.itemsize for o in outs)
    return pl.pallas_call(
        kernel,
        out_shape=outs,
        in_specs=[pl.BlockSpec(memory_space=pltpu.VMEM) for _ in args],
        out_specs=[pl.BlockSpec(memory_space=pltpu.VMEM) for _ in outs],
        scratch_shapes=list(scratch),
        compiler_params=PARAMS,
        cost_estimate=pl.CostEstimate(flops=flops, bytes_accessed=size, transcendentals=0),
    )(*args)


def shape(dims, dtype):
    return jax.ShapeDtypeStruct(dims, dtype)


def dot(left, right, dims=((1,), (0,))):
    return lax.dot_general(left, right, (dims, ((), ())), preferred_element_type=F32)


def row_picker(rows, step, offset):
    r = lax.broadcasted_iota(jnp.int32, (rows, rows * step), 0)
    k = lax.broadcasted_iota(jnp.int32, (rows, rows * step), 1)
    return (k == r * step + offset).astype(BF)


def rows_at(value, depth):
    return jnp.concatenate([value[i, depth : depth + 1] for i in range(value.shape[0])], axis=0)


def with_edge(value, edge, at, shift):
    groups, depth, lanes = value.shape
    moved = pltpu.roll(value.reshape(groups * depth, lanes), shift % (groups * depth), 0)
    moved = moved.reshape(groups, depth, lanes)
    q = lax.broadcasted_iota(jnp.int32, value.shape, 1)
    return jnp.where(q == at, jnp.broadcast_to(edge[:, None, :], value.shape), moved)


def mask_row(active, mz, width):
    ny, z = active.shape
    pair = lax.broadcasted_iota(jnp.int32, (mz, z), 1) // 2
    sel = (pair == lax.broadcasted_iota(jnp.int32, (mz, z), 0)).astype(F32)
    lane = lax.broadcasted_iota(jnp.int32, (z, width), 1) // (width // 2)
    widen = (lax.broadcasted_iota(jnp.int32, (z, width), 0) % 2 == lane).astype(BF)
    rep = jnp.broadcast_to(active.astype(F32)[:, None, :], (ny, mz, z)) * sel[None]
    m = dot(rep.astype(BF).reshape(ny * mz, z), widen).astype(BF)
    return m.reshape(ny // 2, 2, mz, width)


def ring_index(axes):
    index = 0
    for name in axes:
        index = index * lax.axis_size(name) + lax.axis_index(name)
    return index


def ring_size(axes):
    size = 1
    for name in axes:
        size = size * lax.axis_size(name)
    return size


def unless(condition):
    return jnp.where(condition, 0.0, 1.0)


def face_kernel(feat, active, pack, row, cells, sems):
    _, slabs, mz, width = pack.shape
    my = slabs - 1
    copies = [
        pltpu.make_async_copy(feat.at[feat.shape[0] - 1], row, sems.at[0]),
        pltpu.make_async_copy(active.at[active.shape[0] - 1], cells, sems.at[1]),
    ]
    for copy in copies:
        copy.start()
    keep = unless(ring_index(GX) == ring_size(GX) - 1)
    pick = row_picker(my, mz, mz - 1)
    for copy in copies:
        copy.wait()
    m = mask_row(cells[...], mz, width)
    value = row[...].reshape(m.shape) * m
    for py in range(2):
        held = (value[:, py].astype(F32) * keep).astype(BF)
        pack[py, :my] = held
        pack[py, my] = dot(pick, held.reshape(my * mz, width)).astype(BF)


def mask_kernel(feat, active, gain, bias, xin, act, zface, norm):
    nx, _, my, mz, width = xin.shape
    pick = row_picker(my, mz, mz - 1)
    norm[0:1] = gain[...]
    norm[1:2] = bias[...]
    count = None
    for x in range(nx):
        m = mask_row(active[x], mz, width)
        value = feat[x].reshape(m.shape) * m
        for py in range(2):
            part = m[:, py]
            held = value[:, py]
            xin[x, py] = held
            zface[x, py] = dot(pick, held.reshape(my * mz, width)).astype(BF)
            term = part.astype(F32).reshape(my * mz, width)
            count = term if count is None else count + term
        if x % 2 == 1:
            both = count + pltpu.roll(count, width // 2, 1)
            act[x // 2] = (both > 0.0).astype(F32).astype(BF).reshape(my, mz, width)
            count = None


def tile_of(xin, xh, yh, row, b):
    py = 0 if b == 1 else 1
    my = xin.shape[2]
    base = xh[py, :my] if row == 0 else xin[row - 1, py]
    if b == 0:
        base = jnp.concatenate([yh[row][None], base[: my - 1]], axis=0)
    return base


def edge_of(zh, row, b):
    base = zh[2 * row + (0 if b == 1 else 1)]
    if b == 0:
        wide = base.astype(F32)
        first = zh[zh.shape[0] - 1].astype(F32)[row : row + 1]
        wide = jnp.concatenate([first, wide[: wide.shape[0] - 1]], axis=0)
        base = wide.astype(BF)
    return base


TAPS = [(a, b) for a in range(3) for b in range(3)]


def build_matrix(weight, wmat):
    half, cout = weight.shape[3:]
    width = 2 * half
    zero = jnp.zeros((half, cout), BF)
    for i, (a, b) in enumerate(TAPS):
        lo = i * width
        wmat[lo : lo + half, :cout] = weight[a, b, 1]
        wmat[lo + half : lo + width, :cout] = weight[a, b, 2]
        wmat[lo : lo + half, cout:] = zero
        wmat[lo + half : lo + width, cout:] = weight[a, b, 0]


OFF = 1e30


def standardized(value, mean, rstd):
    active = value < 0.1 * OFF
    return jnp.where(active, 1.0, 0.0), jnp.where(active, value - mean, 0.0) * rstd


def slope_of(normed, sig, cot):
    return cot * sig * (1.0 + normed * (1.0 - sig))


def rim_parts(value, on, cot):
    high, low = split(value, 2)
    return [part.astype(BF) for part in (jnp.where(on > 0.0, high, OFF), low, cot)]


def merge_kernel(parts, xd, yface, zface, out, yplane):
    mx = yface.shape[1]
    my = zface.shape[2]
    counts, sums, squares = (
        jnp.concatenate([parts[j, i : i + 1] for j in range(parts.shape[0])], axis=0) for i in range(3)
    )
    count = jnp.sum(counts, axis=0, keepdims=True)
    total = jnp.sum(sums, axis=0, keepdims=True)
    mean = total / jnp.maximum(count, 1.0)
    apart = sums / jnp.maximum(counts, 1.0) - mean
    square = jnp.sum(squares + counts * apart * apart, axis=0, keepdims=True)
    for i in range(out.shape[0]):
        out[i, 0:1] = count
        out[i, 1:2] = total
        out[i, 2:3] = square
    depth = yplane.shape[2]
    yplane[:, :mx] = yface[...]
    yplane[:, mx] = xd[:, 0]
    for i in range(3):
        rows = [zface[i, m].astype(F32)[0:1] for m in range(mx)] + [xd[i, my].astype(F32)[0:1]]
        rows.append(jnp.zeros((depth - mx - 1, yplane.shape[3]), F32))
        yplane[i, mx + 1] = jnp.concatenate(rows, axis=0).astype(BF)


def forward_kernel(
    xin, act, xh, yh, zh, weight, cot, pre, stats, xface, yface, zface, wmat
):
    mx, my, mz, cout = pre.shape
    width = xin.shape[4]
    build_matrix(weight, wmat)
    rows = my * mz
    total = jnp.zeros((1, cout), F32)
    count = jnp.zeros((1, cout), F32)
    w = wmat[...]
    for m in range(mx):
        left = jnp.concatenate(
            [tile_of(xin, xh, yh, 2 * m + a, b).reshape(rows, width) for a, b in TAPS], axis=1
        )
        edge = jnp.concatenate([edge_of(zh, 2 * m + a, b) for a, b in TAPS], axis=1)
        out = dot(left, w)
        rim = dot(edge, w[:, cout:])
        prev = with_edge(out[:, cout:].reshape(my, mz, cout), rim, 0, 1)
        value = out[:, :cout].reshape(my, mz, cout) + prev
        on = act[m].astype(F32)
        pre[m] = jnp.where(on > 0.0, value, OFF)
        planes = (value, on, cot[m].astype(F32))
        side = rim_parts(*[rows_at(part, 0) for part in planes])
        line = rim_parts(*[part[0] for part in planes])
        whole = rim_parts(*planes) if m == 0 else None
        for i in range(3):
            yface[i, m] = line[i]
            zface[i, m] = side[i]
            if m == 0:
                xface[i, :my] = whole[i]
                xface[i, my] = side[i]
        total = total + jnp.sum((on * value).reshape(rows, cout), axis=0, keepdims=True)
        count = count + jnp.sum(on.reshape(rows, cout), axis=0, keepdims=True)
    mean = total / jnp.maximum(count, 1.0)
    squares = jnp.zeros((1, cout), F32)
    for m in range(mx):
        on = act[m].astype(F32).reshape(rows, cout)
        apart = jnp.where(on > 0.0, pre[m].reshape(rows, cout) - mean, 0.0)
        squares = squares + jnp.sum(apart * apart, axis=0, keepdims=True)
    for i in range(stats.shape[0]):
        stats[i, 0:1] = count
        stats[i, 1:2] = total
        stats[i, 2:3] = squares


def split(value, parts):
    out = []
    for _ in range(parts):
        out.append(value.astype(BF).astype(F32))
        value = value - out[-1]
    return out


def rounded(value):
    high, low = split(value, 2)
    return high + low


def outer(column, rows):
    return lax.dot_general(
        column, rows, (((0,), (0,)), ((), ())), precision=lax.Precision.HIGHEST, preferred_element_type=F32
    )


def write_chunk(ref, i, body, column, common):
    left, right = common
    line = lax.broadcasted_iota(jnp.int32, left.shape, 0)
    for at, part in enumerate(split(column, 3)):
        left = jnp.where(line == at, part, left)
    ref[i] = jnp.concatenate([body, jnp.concatenate([left, right], axis=1)], axis=0).astype(BF)


def common_rows(first, second, alpha, beta, high):
    zero = jnp.zeros_like(first)
    rows = split(first, 3) + split(second, 3) + split(alpha, 3) + split(beta, 2) + split(high, 2)
    return (
        jnp.concatenate([zero] * 3 + rows[:5], axis=0),
        jnp.concatenate(rows[5:], axis=0),
    )


def read_chunks(ref):
    devices, depth, _ = ref.shape
    rows = depth - 8
    cout = ref.shape[2] // 2
    slopes = hats = None
    firsts = seconds = None
    columns, vectors, betas = ([], [], None)
    for j in range(devices):
        value = ref[j].astype(F32)
        left, right = (value[rows:, :cout], value[rows:, cout:])
        part = value[:rows, cout:]
        beta = right[4:5] + right[5:6]
        term = value[:rows, :cout] + part * beta
        first = left[3:4] + left[4:5] + left[5:6]
        second = left[6:7] + left[7:8] + right[0:1]
        alpha = right[1:2] + right[2:3] + right[3:4]
        columns.append(left[0:1] + left[1:2] + left[2:3])
        vectors.append(jnp.concatenate([alpha, right[6:7] + right[7:8]], axis=1))
        if j == 0:
            slopes, hats, firsts, seconds, betas = (term, part, first, second, beta)
        else:
            slopes, hats = (slopes + term, hats + part)
            firsts, seconds, betas = (firsts + first, seconds + second, betas + beta)
    columns = jnp.concatenate(columns, axis=0)
    vectors = jnp.concatenate(vectors, axis=0)
    both = outer(columns, vectors)[:rows]
    slopes = slopes + both[:, :cout]
    hats = hats + both[:, cout:]
    column = jnp.sum(columns, axis=0, keepdims=True)
    middle = jnp.sum(vectors, axis=0, keepdims=True) / devices
    return slopes, hats, column, firsts, seconds, middle[:, :cout], betas / devices, middle[:, cout:]


def eight(row):
    return jnp.broadcast_to(row, (8, row.shape[1]))


def lone(row):
    return jnp.where(lax.broadcasted_iota(jnp.int32, (8, row.shape[1]), 0) == 0, eight(row), 0.0)


def slope_kernel(
    pre, cot, par, xin, xh, yh, zh, xd, yd, zface, out, big, zplane, slope, acc
):
    mx, my, mz, cout = pre.shape
    width = xin.shape[4]
    half = width // 2
    rows = my * mz
    mean, rstd, gain, bias = (par[i : i + 1] for i in range(4))
    first, second, count, high, square = (jnp.zeros((1, cout), F32) for _ in range(5))
    zplane[:, :mx] = zface[...]
    zplane[:, mx] = xd[:, my]
    zplane[:, mx + 1] = yd[:, mx + 1]
    for m in range(mx):
        on, hat = standardized(pre[m].reshape(rows, cout), mean, rstd)
        normed = hat * gain + bias
        sig = jax.nn.sigmoid(normed)
        out[m] = (on * normed * sig).astype(BF).reshape(my, mz, cout)
        tilt = slope_of(normed, sig, on * cot[m].astype(F32).reshape(rows, cout))
        slope[m] = tilt.reshape(my, mz, cout)
        first = first + jnp.sum(tilt, axis=0, keepdims=True)
        second = second + jnp.sum(tilt * hat, axis=0, keepdims=True)
        count = count + jnp.sum(on, axis=0, keepdims=True)
        high = high + jnp.sum(on * hat, axis=0, keepdims=True)
        square = square + jnp.sum(on * hat * hat, axis=0, keepdims=True)
    some = jnp.maximum(count, 1.0)
    alpha = first / some
    high = rounded(high / some)
    beta = (second - high * first) / jnp.maximum(square - count * high * high, 0.01 * some)
    beta = rounded(beta)
    last = lax.broadcasted_iota(jnp.int32, (my, mz, cout), 1) == mz - 1
    total = None
    rims = [[], [], []]
    for m in range(mx):
        on, hat = standardized(pre[m].reshape(rows, cout), mean, rstd)
        hat = on * (hat - high)
        rest = slope[m].reshape(rows, cout) - on * alpha - hat * beta
        here, after = ([], [])
        for i, part in enumerate((rest, hat, on)):
            held = part.astype(BF)
            keep = 8 if i == 2 else cout
            wide = held.astype(F32)
            rims[i].append(rows_at(wide.reshape(my, mz, cout), 0))
            nxt = pltpu.roll(wide, rows - 1, 0).reshape(my, mz, cout)
            nxt = jnp.where(last, 0.0, nxt).reshape(rows, cout)
            here.append(wide.T[:keep])
            after.append(nxt.T[:keep])
        right = jnp.concatenate(here + after, axis=0).astype(BF)
        left = jnp.concatenate(
            [tile_of(xin, xh, yh, 2 * m + a, b).reshape(rows, width) for a, b in TAPS], axis=1
        )
        term = dot(right, left)
        total = term if total is None else total + term
    rim = [jnp.concatenate(parts, axis=0).T for parts in rims]
    rim = jnp.concatenate([rim[0], rim[1], rim[2][:8]], axis=0).astype(BF)
    edge = jnp.concatenate(
        [
            jnp.concatenate([edge_of(zh, 2 * m + a, b) for a, b in TAPS], axis=1)
            for m in range(mx)
        ],
        axis=0,
    )
    size = 2 * cout + 8
    own = total[:size]
    low = total[size:] + dot(rim, edge)
    taps = 3 * len(TAPS)
    for i in range(len(TAPS)):
        at = i * width
        to = 3 * half * i
        acc[to : to + half] = low[: 2 * cout, at : at + width].T[half:]
        acc[to + half : to + 3 * half] = own[: 2 * cout, at : at + width].T
    if acc.shape[0] > half * taps:
        acc[half * taps :] = jnp.zeros((acc.shape[0] - half * taps, 2 * cout), F32)
    common = common_rows(first, second, alpha, beta, high)
    lane = lax.broadcasted_iota(jnp.int32, (8, width), 1)
    near, depth, _ = big.shape
    depth = depth - 8
    for n in range(near):
        column = jnp.zeros((8, width), F32)
        for tap in range(taps):
            start = half * tap - depth * n
            lo, hi = (max(start, 0), min(start + half, depth))
            if lo < hi:
                at = tap // 3 * width
                row = (low if tap % 3 == 0 else own)[2 * cout :, at : at + width]
                shift = (start - (0 if tap % 3 == 1 else half)) % width
                if shift:
                    row = pltpu.roll(row, shift, 1)
                column = jnp.where((lane >= lo) & (lane < hi), row, column)
        write_chunk(big, n, acc[depth * n : depth * (n + 1)], column, common)


def near_kernel(parts, out):
    slopes, hats, column, first, second, alpha, beta, high = read_chunks(parts)
    rows = slopes.shape[0]
    cout = slopes.shape[1]
    beta, high = (rounded(beta), rounded(high))
    both = outer(lone(column), lone(jnp.concatenate([alpha, high], axis=1)))[:rows]
    hats = hats - both[:, cout:]
    slopes = slopes - both[:, :cout] - hats * beta
    common = common_rows(first, second, alpha, beta, high)
    body = jnp.concatenate([slopes, hats], axis=1)
    for i in range(out.shape[0]):
        write_chunk(out, i, body, eight(column), common)


def far_kernel(parts, par, dw, shift_out, tilt_out, both):
    _, rstd, gain, _, count = (par[i : i + 1] for i in range(5))
    slopes, hats, column, first, second, _, _, _ = read_chunks(parts)
    shift, tilt = (first / count, second / count)
    shift_out[...] = shift
    tilt_out[...] = tilt
    both[0:1] = shift
    both[1:2] = tilt
    value = slopes - outer(lone(column), lone(shift))[: slopes.shape[0]] - hats * tilt
    value = (value * (rstd * gain / count)).astype(BF)
    for i in range(dw.shape[0]):
        dw[i] = value


def input_kernel(pre, cot, par, grads, xd, yd, zd, active, weight, out, ext, nxt, wmat):
    mx, my, mz, cout = pre.shape
    width = out.shape[4]
    rows = my * mz
    mean, rstd, gain, bias = (par[i : i + 1] for i in range(4))
    shift, tilt = (grads[i : i + 1] for i in range(2))
    scale = rstd * gain
    inside = [
        unless(ring_index(axes) == ring_size(axes) - 1) for axes in (GX, GY, GZ)
    ]

    def gradient(value, cot, keep):
        on, hat = standardized(value, mean, rstd)
        normed = hat * gain + bias
        slope = slope_of(normed, jax.nn.sigmoid(normed), cot)
        return (on * keep * scale * (slope - shift - hat * tilt)).astype(BF)

    def rim(parts, keep):
        high, low, cot = (part.astype(F32) for part in parts)
        return gradient(high + low, cot, keep)

    build_matrix(weight, wmat)
    for r in range(mx + 1):
        keep = 1.0 if r < mx else inside[0]
        if r < mx:
            own = cot[r].astype(F32).reshape(rows, cout)
            base = gradient(pre[r].reshape(rows, cout), own, keep).reshape(my, mz, cout)
        else:
            flat = [xd[i, :my].reshape(rows, cout) for i in range(3)]
            base = rim(flat, keep).reshape(my, mz, cout)
        row = rim([yd[i, r] for i in range(3)], keep * inside[1])
        ext[r, :my] = base
        ext[r, my] = row
        whole = jnp.concatenate([base, row[None]], axis=0).astype(F32)
        side = rim([zd[i, r] for i in range(3)], keep * inside[2]).astype(F32)
        last = [zd[i, mx + 1].astype(F32)[r : r + 1] for i in range(3)]
        last = rim(last, keep * inside[1] * inside[2]).astype(F32)
        nxt[r] = with_edge(whole, jnp.concatenate([side, last], axis=0), mz - 1, -1).astype(BF)
    taps = (((1, 0),), ((2, 0), (0, 1)))
    for m in range(mx):
        for px in range(2):
            x = 2 * m + px
            mask = mask_row(active[x], mz, width)
            for py in range(2):
                left, right = ([], [])
                for a, sx in taps[px]:
                    for b, sy in taps[py]:
                        left.append(ext[m + sx, sy : sy + my].reshape(rows, cout))
                        left.append(nxt[m + sx, sy : sy + my].reshape(rows, cout))
                        at = (a * 3 + b) * width
                        right.append(wmat[at : at + width])
                left = jnp.concatenate(left, axis=1)
                right = jnp.concatenate(right, axis=1)
                value = dot(left, right, ((1,), (1,)))
                value = value * mask[:, py].astype(F32).reshape(rows, width)
                out[x, :, py] = value.astype(BF).reshape(my, mz, width)


def moved(value, axes, by):
    count = lax.axis_size(axes)
    return lax.ppermute(value, axes, [(i, (i + by) % count) for i in range(count)])


def beyond(value, axes, by):
    end = lax.axis_size(axes) - 1 if by > 0 else 0
    keep = (lax.axis_index(axes) != end).astype(value.dtype)
    return moved(value * keep, axes, by)


def slab(rows, like):
    return jnp.pad(rows, ((0, like - rows.shape[0]), (0, 0)))[None]


def exchanged(value, axes):
    return lax.all_to_all(value, axes, 0, 0)


def merged(parts):
    counts, sums, squares = (parts[:, 0], parts[:, 1], parts[:, 2])
    count = jnp.sum(counts, axis=0)
    total = jnp.sum(sums, axis=0)
    mean = total / jnp.maximum(count, 1.0)
    apart = sums / jnp.maximum(counts, 1.0) - mean
    return jnp.stack([count, total, jnp.sum(squares + counts * apart * apart, axis=0)])


def local(features, active, weight, gain, bias, cotangent):
    vx, vy, mz, width = features.shape
    cin = width // 2
    cout = weight.shape[4]
    mx, my = (vx // 2, vy // 2)
    near = lax.axis_size(NEAR)
    pack = pl.pallas_call(
        face_kernel,
        out_shape=shape((2, my + 1, mz, width), BF),
        in_specs=[pl.BlockSpec(memory_space=pltpu.HBM)] * 2,
        out_specs=pl.BlockSpec(memory_space=pltpu.VMEM),
        scratch_shapes=[
            pltpu.VMEM((vy, mz, width), BF),
            pltpu.VMEM((vy, 2 * mz), jnp.int32),
            pltpu.SemaphoreType.DMA((2,)),
        ],
        compiler_params=WIDE,
        cost_estimate=pl.CostEstimate(flops=10_000_000, bytes_accessed=400_000, transcendentals=0),
    )(features, active)
    xh = moved(pack, GX, 1)
    xin, act, zface, norm = call(
        mask_kernel,
        [
            shape((vx, 2, my, mz, width), BF),
            shape((mx, my, mz, width), BF),
            shape((vx, 2, my, width), BF),
            shape((2, cout), F32),
        ],
        [features, active, gain[None], bias[None]],
    )
    yface = jnp.concatenate([xh[1:2, my - 1], xin[:, 1, my - 1]], axis=0)
    zfaces = jnp.concatenate([xh[None, :, my], zface], axis=0)
    rows = vx + 1
    yh = beyond(jnp.concatenate([yface, slab(zfaces[:, 1, my - 1], mz)], axis=0), GY, 1)
    zfaces = jnp.concatenate([zfaces.reshape(2 * rows, my, width), yh[rows:]], axis=0)
    zh = beyond(zfaces, GZ, 1)
    pre, stats, xface, yface, zface = call(
        forward_kernel,
        [
            shape((mx, my, mz, cout), F32),
            shape((near, 3, cout), F32),
            shape((3, my + 1, mz, cout), BF),
            shape((3, mx, mz, cout), BF),
            shape((3, mx, my, cout), BF),
        ],
        [xin, act, xh, yh, zh, weight, cotangent],
        scratch=[pltpu.VMEM((9 * width, 2 * cout), BF)],
        flops=1_200_000_000,
    )
    xd = moved(xface, GX, -1)
    stats, yplane = call(
        merge_kernel,
        [shape((lax.axis_size(FAR), 3, cout), F32), shape((3, mx + 2, mz, cout), BF)],
        [exchanged(stats, NEAR), xd, yface, zface],
    )
    yd = moved(yplane, GY, -1)
    stats = merged(exchanged(stats, FAR))
    count = stats[0]
    mean = stats[1] / count
    rstd = lax.rsqrt(stats[2] / count + 1e-05)
    par = jnp.stack([mean, rstd, norm[0], norm[1], count])
    taps = 27 * cin
    rows = -(-taps // (8 * near)) * 8
    section_out, big, zplane = call(
        slope_kernel,
        [
            shape((mx, my, mz, cout), BF),
            shape((near, rows + 8, 2 * cout), BF),
            shape((3, mx + 2, my, cout), BF),
        ],
        [pre, cotangent, par, xin, xh, yh, zh, xd, yd, zface],
        scratch=[pltpu.VMEM(pre.shape, F32), pltpu.VMEM((near * rows, 2 * cout), F32)],
        flops=2_400_000_000,
    )
    zd = moved(zplane, GZ, -1)
    far = lax.axis_size(FAR)
    (big,) = call(near_kernel, [shape((far, rows + 8, 2 * cout), BF)], [exchanged(big, NEAR)])
    plane = lax.axis_size(PLANE)
    dw, shift, tilt, grads = call(
        far_kernel,
        [
            shape((plane, rows, cout), BF),
            shape((1, cout), F32),
            shape((1, cout), F32),
            shape((2, cout), F32),
        ],
        [exchanged(big, FAR), par],
    )
    shift_gradient, gain_gradient = (shift.reshape(cout), tilt.reshape(cout))
    (grad_features,) = call(
        input_kernel,
        [shape((vx, my, 2, mz, width), BF)],
        [pre, cotangent, par, grads, xd, yd, zd, active, weight],
        scratch=[
            pltpu.VMEM((mx + 1, my + 1, mz, cout), BF),
            pltpu.VMEM((mx + 1, my + 1, mz, cout), BF),
            pltpu.VMEM((9 * width, 2 * cout), BF),
        ],
        flops=2_400_000_000,
    )
    mine, grad_features = lax.optimization_barrier((exchanged(dw, PLANE), grad_features))
    other = moved(mine, "c", 1)
    low = lax.axis_index("c") == 0
    grad_weight = jnp.stack([jnp.where(low, mine, other), jnp.where(low, other, mine)])
    grad_weight = grad_weight.reshape(near * rows, cout)[:taps]
    grad_weight = grad_weight.astype(F32).reshape(weight.shape)
    grad_features = grad_features.reshape(features.shape)
    return (section_out, grad_features, grad_weight, gain_gradient, shift_gradient)


def solution(mesh):
    gx, gy, gz = (mesh.shape[name] for name in ("gx", "gy", "gz"))
    fine = Mesh(mesh.devices.reshape(gx // 2, 2, gy // 2, 2, gz), ALL)
    block = (("z", "yh"), ("x", "c"), "yl")
    in_specs = (P(*block, None), P(*block), P(), P(), P(), P(*block, None))
    out_specs = (P(*block, None), P(*block, None), P(), P(), P())
    return jax.shard_map(local, mesh=fine, in_specs=in_specs, out_specs=out_specs, check_vma=False)
```

```python
import jax
import jax.numpy as jnp
from jax import lax
from jax.experimental import pallas as pl
from jax.experimental.pallas import tpu as pltpu
from jax.sharding import Mesh, PartitionSpec as P

BF = jnp.bfloat16
F32 = jnp.float32
ALL = ("z", "yh", "x", "c", "yl")
NEAR = ("c", "yh", "x", "yl")
PLANE = ("yh", "x", "yl")
GX, GY, GZ = (("z", "yh"), ("x", "c"), ("yl",))
FAR = ("z",)
PARAMS = pltpu.CompilerParams(vmem_limit_bytes=24 * 1024 * 1024)
WIDE = pltpu.CompilerParams(vmem_limit_bytes=60 * 1024 * 1024)


def call(kernel, outs, args, scratch=(), flops=100_000_000):
    size = sum(a.size * a.dtype.itemsize for a in args) + sum(o.size * o.dtype.itemsize for o in outs)
    return pl.pallas_call(
        kernel,
        out_shape=outs,
        in_specs=[pl.BlockSpec(memory_space=pltpu.VMEM) for _ in args],
        out_specs=[pl.BlockSpec(memory_space=pltpu.VMEM) for _ in outs],
        scratch_shapes=list(scratch),
        compiler_params=PARAMS,
        cost_estimate=pl.CostEstimate(flops=flops, bytes_accessed=size, transcendentals=0),
    )(*args)


def shape(dims, dtype):
    return jax.ShapeDtypeStruct(dims, dtype)


def dot(left, right, dims=((1,), (0,))):
    return lax.dot_general(left, right, (dims, ((), ())), preferred_element_type=F32)


def row_picker(rows, step, offset):
    r = lax.broadcasted_iota(jnp.int32, (rows, rows * step), 0)
    k = lax.broadcasted_iota(jnp.int32, (rows, rows * step), 1)
    return (k == r * step + offset).astype(BF)


def rows_at(value, depth):
    return jnp.concatenate([value[i, depth : depth + 1] for i in range(value.shape[0])], axis=0)


def with_edge(value, edge, at, shift):
    groups, depth, lanes = value.shape
    moved = pltpu.roll(value.reshape(groups * depth, lanes), shift % (groups * depth), 0)
    moved = moved.reshape(groups, depth, lanes)
    q = lax.broadcasted_iota(jnp.int32, value.shape, 1)
    return jnp.where(q == at, jnp.broadcast_to(edge[:, None, :], value.shape), moved)


def mask_row(active, mz, width):
    ny, z = active.shape
    pair = lax.broadcasted_iota(jnp.int32, (mz, z), 1) // 2
    sel = (pair == lax.broadcasted_iota(jnp.int32, (mz, z), 0)).astype(F32)
    lane = lax.broadcasted_iota(jnp.int32, (z, width), 1) // (width // 2)
    widen = (lax.broadcasted_iota(jnp.int32, (z, width), 0) % 2 == lane).astype(BF)
    rep = jnp.broadcast_to(active.astype(F32)[:, None, :], (ny, mz, z)) * sel[None]
    m = dot(rep.astype(BF).reshape(ny * mz, z), widen).astype(BF)
    return m.reshape(ny // 2, 2, mz, width)


def ring_index(axes):
    index = 0
    for name in axes:
        index = index * lax.axis_size(name) + lax.axis_index(name)
    return index


def ring_size(axes):
    size = 1
    for name in axes:
        size = size * lax.axis_size(name)
    return size


def unless(condition):
    return jnp.where(condition, 0.0, 1.0)


def face_kernel(feat, active, pack, row, cells, sems):
    _, slabs, mz, width = pack.shape
    my = slabs - 1
    copies = [
        pltpu.make_async_copy(feat.at[feat.shape[0] - 1], row, sems.at[0]),
        pltpu.make_async_copy(active.at[active.shape[0] - 1], cells, sems.at[1]),
    ]
    for copy in copies:
        copy.start()
    keep = unless(ring_index(GX) == ring_size(GX) - 1)
    pick = row_picker(my, mz, mz - 1)
    for copy in copies:
        copy.wait()
    m = mask_row(cells[...], mz, width)
    value = row[...].reshape(m.shape) * m
    for py in range(2):
        held = (value[:, py].astype(F32) * keep).astype(BF)
        pack[py, :my] = held
        pack[py, my] = dot(pick, held.reshape(my * mz, width)).astype(BF)


def mask_kernel(feat, active, gain, bias, xin, act, zface, norm):
    nx, _, my, mz, width = xin.shape
    pick = row_picker(my, mz, mz - 1)
    norm[0:1] = gain[...]
    norm[1:2] = bias[...]
    count = None
    for x in range(nx):
        m = mask_row(active[x], mz, width)
        value = feat[x].reshape(m.shape) * m
        for py in range(2):
            part = m[:, py]
            held = value[:, py]
            xin[x, py] = held
            zface[x, py] = dot(pick, held.reshape(my * mz, width)).astype(BF)
            term = part.astype(F32).reshape(my * mz, width)
            count = term if count is None else count + term
        if x % 2 == 1:
            both = count + pltpu.roll(count, width // 2, 1)
            act[x // 2] = (both > 0.0).astype(F32).astype(BF).reshape(my, mz, width)
            count = None


def tile_of(xin, xh, yh, row, b):
    py = 0 if b == 1 else 1
    my = xin.shape[2]
    base = xh[py, :my] if row == 0 else xin[row - 1, py]
    if b == 0:
        base = jnp.concatenate([yh[row][None], base[: my - 1]], axis=0)
    return base


def edge_of(zh, row, b):
    base = zh[2 * row + (0 if b == 1 else 1)]
    if b == 0:
        wide = base.astype(F32)
        first = zh[zh.shape[0] - 1].astype(F32)[row : row + 1]
        wide = jnp.concatenate([first, wide[: wide.shape[0] - 1]], axis=0)
        base = wide.astype(BF)
    return base


TAPS = [(a, b) for a in range(3) for b in range(3)]


def build_matrix(weight, wmat):
    half, cout = weight.shape[3:]
    width = 2 * half
    zero = jnp.zeros((half, cout), BF)
    for i, (a, b) in enumerate(TAPS):
        lo = i * width
        wmat[lo : lo + half, :cout] = weight[a, b, 1]
        wmat[lo + half : lo + width, :cout] = weight[a, b, 2]
        wmat[lo : lo + half, cout:] = zero
        wmat[lo + half : lo + width, cout:] = weight[a, b, 0]


OFF = 1e30


def standardized(value, mean, rstd):
    active = value < 0.1 * OFF
    return jnp.where(active, 1.0, 0.0), jnp.where(active, value - mean, 0.0) * rstd


def slope_of(normed, sig, cot):
    return cot * sig * (1.0 + normed * (1.0 - sig))


def rim_parts(value, on, cot):
    high, low = split(value, 2)
    return [part.astype(BF) for part in (jnp.where(on > 0.0, high, OFF), low, cot)]


def merge_kernel(parts, xd, yface, zface, out, yplane):
    mx = yface.shape[1]
    my = zface.shape[2]
    counts, sums, squares = (
        jnp.concatenate([parts[j, i : i + 1] for j in range(parts.shape[0])], axis=0) for i in range(3)
    )
    count = jnp.sum(counts, axis=0, keepdims=True)
    total = jnp.sum(sums, axis=0, keepdims=True)
    mean = total / jnp.maximum(count, 1.0)
    apart = sums / jnp.maximum(counts, 1.0) - mean
    square = jnp.sum(squares + counts * apart * apart, axis=0, keepdims=True)
    for i in range(out.shape[0]):
        out[i, 0:1] = count
        out[i, 1:2] = total
        out[i, 2:3] = square
    depth = yplane.shape[2]
    yplane[:, :mx] = yface[...]
    yplane[:, mx] = xd[:, 0]
    for i in range(3):
        rows = [zface[i, m].astype(F32)[0:1] for m in range(mx)] + [xd[i, my].astype(F32)[0:1]]
        rows.append(jnp.zeros((depth - mx - 1, yplane.shape[3]), F32))
        yplane[i, mx + 1] = jnp.concatenate(rows, axis=0).astype(BF)


def forward_kernel(
    xin, act, xh, yh, zh, weight, cot, pre, stats, xface, yface, zface, wmat
):
    mx, my, mz, cout = pre.shape
    width = xin.shape[4]
    build_matrix(weight, wmat)
    rows = my * mz
    total = jnp.zeros((1, cout), F32)
    count = jnp.zeros((1, cout), F32)
    w = wmat[...]
    for m in range(mx):
        left = jnp.concatenate(
            [tile_of(xin, xh, yh, 2 * m + a, b).reshape(rows, width) for a, b in TAPS], axis=1
        )
        edge = jnp.concatenate([edge_of(zh, 2 * m + a, b) for a, b in TAPS], axis=1)
        out = dot(left, w)
        rim = dot(edge, w[:, cout:])
        prev = with_edge(out[:, cout:].reshape(my, mz, cout), rim, 0, 1)
        value = out[:, :cout].reshape(my, mz, cout) + prev
        on = act[m].astype(F32)
        pre[m] = jnp.where(on > 0.0, value, OFF)
        planes = (value, on, cot[m].astype(F32))
        side = rim_parts(*[rows_at(part, 0) for part in planes])
        line = rim_parts(*[part[0] for part in planes])
        whole = rim_parts(*planes) if m == 0 else None
        for i in range(3):
            yface[i, m] = line[i]
            zface[i, m] = side[i]
            if m == 0:
                xface[i, :my] = whole[i]
                xface[i, my] = side[i]
        total = total + jnp.sum((on * value).reshape(rows, cout), axis=0, keepdims=True)
        count = count + jnp.sum(on.reshape(rows, cout), axis=0, keepdims=True)
    mean = total / jnp.maximum(count, 1.0)
    squares = jnp.zeros((1, cout), F32)
    for m in range(mx):
        on = act[m].astype(F32).reshape(rows, cout)
        apart = jnp.where(on > 0.0, pre[m].reshape(rows, cout) - mean, 0.0)
        squares = squares + jnp.sum(apart * apart, axis=0, keepdims=True)
    for i in range(stats.shape[0]):
        stats[i, 0:1] = count
        stats[i, 1:2] = total
        stats[i, 2:3] = squares


def split(value, parts):
    out = []
    for _ in range(parts):
        out.append(value.astype(BF).astype(F32))
        value = value - out[-1]
    return out


def rounded(value):
    high, low = split(value, 2)
    return high + low


def outer(column, rows):
    return lax.dot_general(
        column, rows, (((0,), (0,)), ((), ())), precision=lax.Precision.HIGHEST, preferred_element_type=F32
    )


def write_chunk(ref, i, body, column, common):
    left, right = common
    line = lax.broadcasted_iota(jnp.int32, left.shape, 0)
    for at, part in enumerate(split(column, 3)):
        left = jnp.where(line == at, part, left)
    ref[i] = jnp.concatenate([body, jnp.concatenate([left, right], axis=1)], axis=0).astype(BF)


def common_rows(first, second, alpha, beta, high):
    zero = jnp.zeros_like(first)
    rows = split(first, 3) + split(second, 3) + split(alpha, 3) + split(beta, 2) + split(high, 2)
    return (
        jnp.concatenate([zero] * 3 + rows[:5], axis=0),
        jnp.concatenate(rows[5:], axis=0),
    )


def read_chunks(ref):
    devices, depth, _ = ref.shape
    rows = depth - 8
    cout = ref.shape[2] // 2
    slopes = hats = None
    firsts = seconds = None
    columns, vectors, betas = ([], [], None)
    for j in range(devices):
        value = ref[j].astype(F32)
        left, right = (value[rows:, :cout], value[rows:, cout:])
        part = value[:rows, cout:]
        beta = right[4:5] + right[5:6]
        term = value[:rows, :cout] + part * beta
        first = left[3:4] + left[4:5] + left[5:6]
        second = left[6:7] + left[7:8] + right[0:1]
        alpha = right[1:2] + right[2:3] + right[3:4]
        columns.append(left[0:1] + left[1:2] + left[2:3])
        vectors.append(jnp.concatenate([alpha, right[6:7] + right[7:8]], axis=1))
        if j == 0:
            slopes, hats, firsts, seconds, betas = (term, part, first, second, beta)
        else:
            slopes, hats = (slopes + term, hats + part)
            firsts, seconds, betas = (firsts + first, seconds + second, betas + beta)
    columns = jnp.concatenate(columns, axis=0)
    vectors = jnp.concatenate(vectors, axis=0)
    both = outer(columns, vectors)[:rows]
    slopes = slopes + both[:, :cout]
    hats = hats + both[:, cout:]
    column = jnp.sum(columns, axis=0, keepdims=True)
    middle = jnp.sum(vectors, axis=0, keepdims=True) / devices
    return slopes, hats, column, firsts, seconds, middle[:, :cout], betas / devices, middle[:, cout:]


def eight(row):
    return jnp.broadcast_to(row, (8, row.shape[1]))


def lone(row):
    return jnp.where(lax.broadcasted_iota(jnp.int32, (8, row.shape[1]), 0) == 0, eight(row), 0.0)


def slope_kernel(pre, cot, par, out, slope, sums):
    mx, my, mz, cout = pre.shape
    rows = my * mz
    mean, rstd, gain, bias = (par[i : i + 1] for i in range(4))
    first, second, count, high, square = (jnp.zeros((1, cout), F32) for _ in range(5))
    for m in range(mx):
        on, hat = standardized(pre[m].reshape(rows, cout), mean, rstd)
        normed = hat * gain + bias
        sig = jax.nn.sigmoid(normed)
        out[m] = (on * normed * sig).astype(BF).reshape(my, mz, cout)
        tilt = slope_of(normed, sig, on * cot[m].astype(F32).reshape(rows, cout))
        slope[m] = tilt.reshape(my, mz, cout)
        first = first + jnp.sum(tilt, axis=0, keepdims=True)
        second = second + jnp.sum(tilt * hat, axis=0, keepdims=True)
        count = count + jnp.sum(on, axis=0, keepdims=True)
        high = high + jnp.sum(hat, axis=0, keepdims=True)
        square = square + jnp.sum(hat * hat, axis=0, keepdims=True)
    sums[...] = jnp.concatenate([first, second, count, high, square] + [jnp.zeros((3, cout), F32)], axis=0)


def product_kernel(
    pre, slope, sums, others, par, xin, xh, yh, zh, xd, yd, zface, keep, send, zplane, acc, big
):
    mx, my, mz, cout = pre.shape
    width = xin.shape[4]
    half = width // 2
    rows = my * mz
    mean, rstd = (par[i : i + 1] for i in range(2))
    zplane[:, :mx] = zface[...]
    zplane[:, mx] = xd[:, my]
    zplane[:, mx + 1] = yd[:, mx + 1]
    both = sums[...] + others[...]
    first, second, count, high, square = (both[i : i + 1] for i in range(5))
    some = jnp.maximum(count, 1.0)
    alpha = first / some
    high = rounded(high / some)
    beta = (second - high * first) / jnp.maximum(square - count * high * high, 0.01 * some)
    beta = rounded(beta)
    last = lax.broadcasted_iota(jnp.int32, (my, mz, cout), 1) == mz - 1
    total = None
    rims = [[], [], []]
    for m in range(mx):
        on, hat = standardized(pre[m].reshape(rows, cout), mean, rstd)
        hat = on * (hat - high)
        rest = slope[m].reshape(rows, cout) - on * alpha - hat * beta
        here, after = ([], [])
        for i, part in enumerate((rest, hat, on)):
            held = part.astype(BF)
            lines = 8 if i == 2 else cout
            wide = held.astype(F32)
            rims[i].append(rows_at(wide.reshape(my, mz, cout), 0))
            nxt = pltpu.roll(wide, rows - 1, 0).reshape(my, mz, cout)
            nxt = jnp.where(last, 0.0, nxt).reshape(rows, cout)
            here.append(wide.T[:lines])
            after.append(nxt.T[:lines])
        right = jnp.concatenate(here + after, axis=0).astype(BF)
        left = jnp.concatenate(
            [tile_of(xin, xh, yh, 2 * m + a, b).reshape(rows, width) for a, b in TAPS], axis=1
        )
        term = dot(right, left)
        total = term if total is None else total + term
    rim = [jnp.concatenate(parts, axis=0).T for parts in rims]
    rim = jnp.concatenate([rim[0], rim[1], rim[2][:8]], axis=0).astype(BF)
    edge = jnp.concatenate(
        [
            jnp.concatenate([edge_of(zh, 2 * m + a, b) for a, b in TAPS], axis=1)
            for m in range(mx)
        ],
        axis=0,
    )
    size = 2 * cout + 8
    own = total[:size]
    low = total[size:] + dot(rim, edge)
    taps = 3 * len(TAPS)
    for i in range(len(TAPS)):
        at = i * width
        to = 3 * half * i
        acc[to : to + half] = low[: 2 * cout, at : at + width].T[half:]
        acc[to + half : to + 3 * half] = own[: 2 * cout, at : at + width].T
    if acc.shape[0] > half * taps:
        acc[half * taps :] = jnp.zeros((acc.shape[0] - half * taps, 2 * cout), F32)
    common = common_rows(first, second, alpha, beta, high)
    lane = lax.broadcasted_iota(jnp.int32, (8, width), 1)
    _, plane, depth, _ = big.shape
    depth = depth - 8
    for n in range(2 * plane):
        column = jnp.zeros((8, width), F32)
        for tap in range(taps):
            start = half * tap - depth * n
            lo, hi = (max(start, 0), min(start + half, depth))
            if lo < hi:
                at = tap // 3 * width
                row = (low if tap % 3 == 0 else own)[2 * cout :, at : at + width]
                shift = (start - (0 if tap % 3 == 1 else half)) % width
                if shift:
                    row = pltpu.roll(row, shift, 1)
                column = jnp.where((lane >= lo) & (lane < hi), row, column)
        write_chunk(big.at[n // plane], n % plane, acc[depth * n : depth * (n + 1)], column, common)
    core = lax.axis_index("c")
    keep[...] = big[core]
    send[...] = big[1 - core]


def pair_kernel(mine, other, out):
    _, depth, width = mine.shape
    rows = depth - 8
    cout = width // 2
    for i in range(mine.shape[0]):
        value = mine[i].astype(F32)
        both = value + other[i].astype(F32)
        column = both[rows : rows + 1, :cout] + both[rows + 1 : rows + 2, :cout] + both[rows + 2 : rows + 3, :cout]
        write_chunk(out, i, both[:rows], eight(column), (value[rows:, :cout], value[rows:, cout:]))


def near_kernel(parts, out):
    slopes, hats, column, first, second, alpha, beta, high = read_chunks(parts)
    rows = slopes.shape[0]
    cout = slopes.shape[1]
    beta, high = (rounded(beta), rounded(high))
    both = outer(lone(column), lone(jnp.concatenate([alpha, high], axis=1)))[:rows]
    hats = hats - both[:, cout:]
    slopes = slopes - both[:, :cout] - hats * beta
    common = common_rows(first, second, alpha, beta, high)
    body = jnp.concatenate([slopes, hats], axis=1)
    for i in range(out.shape[0]):
        write_chunk(out, i, body, eight(column), common)


def far_kernel(parts, par, dw, shift_out, tilt_out, both):
    _, rstd, gain, _, count = (par[i : i + 1] for i in range(5))
    slopes, hats, column, first, second, _, _, _ = read_chunks(parts)
    shift, tilt = (first / count, second / count)
    shift_out[...] = shift
    tilt_out[...] = tilt
    both[0:1] = shift
    both[1:2] = tilt
    value = slopes - outer(lone(column), lone(shift))[: slopes.shape[0]] - hats * tilt
    value = (value * (rstd * gain / count)).astype(BF)
    for i in range(dw.shape[0]):
        dw[i] = value


def input_kernel(pre, cot, par, grads, xd, yd, zd, active, weight, out, ext, nxt, wmat):
    mx, my, mz, cout = pre.shape
    width = out.shape[4]
    rows = my * mz
    mean, rstd, gain, bias = (par[i : i + 1] for i in range(4))
    shift, tilt = (grads[i : i + 1] for i in range(2))
    scale = rstd * gain
    inside = [
        unless(ring_index(axes) == ring_size(axes) - 1) for axes in (GX, GY, GZ)
    ]

    def gradient(value, cot, keep):
        on, hat = standardized(value, mean, rstd)
        normed = hat * gain + bias
        slope = slope_of(normed, jax.nn.sigmoid(normed), cot)
        return (on * keep * scale * (slope - shift - hat * tilt)).astype(BF)

    def rim(parts, keep):
        high, low, cot = (part.astype(F32) for part in parts)
        return gradient(high + low, cot, keep)

    build_matrix(weight, wmat)
    for r in range(mx + 1):
        keep = 1.0 if r < mx else inside[0]
        if r < mx:
            own = cot[r].astype(F32).reshape(rows, cout)
            base = gradient(pre[r].reshape(rows, cout), own, keep).reshape(my, mz, cout)
        else:
            flat = [xd[i, :my].reshape(rows, cout) for i in range(3)]
            base = rim(flat, keep).reshape(my, mz, cout)
        row = rim([yd[i, r] for i in range(3)], keep * inside[1])
        ext[r, :my] = base
        ext[r, my] = row
        whole = jnp.concatenate([base, row[None]], axis=0).astype(F32)
        side = rim([zd[i, r] for i in range(3)], keep * inside[2]).astype(F32)
        last = [zd[i, mx + 1].astype(F32)[r : r + 1] for i in range(3)]
        last = rim(last, keep * inside[1] * inside[2]).astype(F32)
        nxt[r] = with_edge(whole, jnp.concatenate([side, last], axis=0), mz - 1, -1).astype(BF)
    taps = (((1, 0),), ((2, 0), (0, 1)))
    for m in range(mx):
        for px in range(2):
            x = 2 * m + px
            mask = mask_row(active[x], mz, width)
            for py in range(2):
                left, right = ([], [])
                for a, sx in taps[px]:
                    for b, sy in taps[py]:
                        left.append(ext[m + sx, sy : sy + my].reshape(rows, cout))
                        left.append(nxt[m + sx, sy : sy + my].reshape(rows, cout))
                        at = (a * 3 + b) * width
                        right.append(wmat[at : at + width])
                left = jnp.concatenate(left, axis=1)
                right = jnp.concatenate(right, axis=1)
                value = dot(left, right, ((1,), (1,)))
                value = value * mask[:, py].astype(F32).reshape(rows, width)
                out[x, :, py] = value.astype(BF).reshape(my, mz, width)


def moved(value, axes, by):
    count = lax.axis_size(axes)
    return lax.ppermute(value, axes, [(i, (i + by) % count) for i in range(count)])


def beyond(value, axes, by):
    end = lax.axis_size(axes) - 1 if by > 0 else 0
    keep = (lax.axis_index(axes) != end).astype(value.dtype)
    return moved(value * keep, axes, by)


def slab(rows, like):
    return jnp.pad(rows, ((0, like - rows.shape[0]), (0, 0)))[None]


def exchanged(value, axes):
    return lax.all_to_all(value, axes, 0, 0)


def merged(parts):
    counts, sums, squares = (parts[:, 0], parts[:, 1], parts[:, 2])
    count = jnp.sum(counts, axis=0)
    total = jnp.sum(sums, axis=0)
    mean = total / jnp.maximum(count, 1.0)
    apart = sums / jnp.maximum(counts, 1.0) - mean
    return jnp.stack([count, total, jnp.sum(squares + counts * apart * apart, axis=0)])


def local(features, active, weight, gain, bias, cotangent):
    vx, vy, mz, width = features.shape
    cin = width // 2
    cout = weight.shape[4]
    mx, my = (vx // 2, vy // 2)
    near = lax.axis_size(NEAR)
    pack = pl.pallas_call(
        face_kernel,
        out_shape=shape((2, my + 1, mz, width), BF),
        in_specs=[pl.BlockSpec(memory_space=pltpu.HBM)] * 2,
        out_specs=pl.BlockSpec(memory_space=pltpu.VMEM),
        scratch_shapes=[
            pltpu.VMEM((vy, mz, width), BF),
            pltpu.VMEM((vy, 2 * mz), jnp.int32),
            pltpu.SemaphoreType.DMA((2,)),
        ],
        compiler_params=WIDE,
        cost_estimate=pl.CostEstimate(flops=10_000_000, bytes_accessed=400_000, transcendentals=0),
    )(features, active)
    xh = moved(pack, GX, 1)
    xin, act, zface, norm = call(
        mask_kernel,
        [
            shape((vx, 2, my, mz, width), BF),
            shape((mx, my, mz, width), BF),
            shape((vx, 2, my, width), BF),
            shape((2, cout), F32),
        ],
        [features, active, gain[None], bias[None]],
    )
    yface = jnp.concatenate([xh[1:2, my - 1], xin[:, 1, my - 1]], axis=0)
    zfaces = jnp.concatenate([xh[None, :, my], zface], axis=0)
    rows = vx + 1
    yh = beyond(jnp.concatenate([yface, slab(zfaces[:, 1, my - 1], mz)], axis=0), GY, 1)
    zfaces = jnp.concatenate([zfaces.reshape(2 * rows, my, width), yh[rows:]], axis=0)
    zh = beyond(zfaces, GZ, 1)
    pre, stats, xface, yface, zface = call(
        forward_kernel,
        [
            shape((mx, my, mz, cout), F32),
            shape((near, 3, cout), F32),
            shape((3, my + 1, mz, cout), BF),
            shape((3, mx, mz, cout), BF),
            shape((3, mx, my, cout), BF),
        ],
        [xin, act, xh, yh, zh, weight, cotangent],
        scratch=[pltpu.VMEM((9 * width, 2 * cout), BF)],
        flops=1_200_000_000,
    )
    xd = moved(xface, GX, -1)
    stats, yplane = call(
        merge_kernel,
        [shape((lax.axis_size(FAR), 3, cout), F32), shape((3, mx + 2, mz, cout), BF)],
        [exchanged(stats, NEAR), xd, yface, zface],
    )
    yd = moved(yplane, GY, -1)
    stats = merged(exchanged(stats, FAR))
    count = stats[0]
    mean = stats[1] / count
    rstd = lax.rsqrt(stats[2] / count + 1e-05)
    par = jnp.stack([mean, rstd, norm[0], norm[1], count])
    taps = 27 * cin
    rows = -(-taps // (8 * near)) * 8
    section_out, slope, sums = call(
        slope_kernel,
        [shape((mx, my, mz, cout), BF), shape((mx, my, mz, cout), F32), shape((8, cout), F32)],
        [pre, cotangent, par],
    )
    plane = lax.axis_size(PLANE)
    chunks = (plane, rows + 8, 2 * cout)
    big, send, zplane = call(
        product_kernel,
        [shape(chunks, BF), shape(chunks, BF), shape((3, mx + 2, my, cout), BF)],
        [pre, slope, sums, moved(sums, "c", 1), par, xin, xh, yh, zh, xd, yd, zface],
        scratch=[pltpu.VMEM((near * rows, 2 * cout), F32), pltpu.VMEM((2,) + chunks, BF)],
        flops=2_400_000_000,
    )
    (big,) = call(pair_kernel, [shape(chunks, BF)], [big, moved(send, "c", 1)])
    zd = moved(zplane, GZ, -1)
    far = lax.axis_size(FAR)
    (big,) = call(near_kernel, [shape((far, rows + 8, 2 * cout), BF)], [exchanged(big, PLANE)])
    dw, shift, tilt, grads = call(
        far_kernel,
        [
            shape((plane, rows, cout), BF),
            shape((1, cout), F32),
            shape((1, cout), F32),
            shape((2, cout), F32),
        ],
        [exchanged(big, FAR), par],
    )
    shift_gradient, gain_gradient = (shift.reshape(cout), tilt.reshape(cout))
    (grad_features,) = call(
        input_kernel,
        [shape((vx, my, 2, mz, width), BF)],
        [pre, cotangent, par, grads, xd, yd, zd, active, weight],
        scratch=[
            pltpu.VMEM((mx + 1, my + 1, mz, cout), BF),
            pltpu.VMEM((mx + 1, my + 1, mz, cout), BF),
            pltpu.VMEM((9 * width, 2 * cout), BF),
        ],
        flops=2_400_000_000,
    )
    mine, grad_features = lax.optimization_barrier((exchanged(dw, PLANE), grad_features))
    other = moved(mine, "c", 1)
    low = lax.axis_index("c") == 0
    grad_weight = jnp.stack([jnp.where(low, mine, other), jnp.where(low, other, mine)])
    grad_weight = grad_weight.reshape(near * rows, cout)[:taps]
    grad_weight = grad_weight.astype(F32).reshape(weight.shape)
    grad_features = grad_features.reshape(features.shape)
    return (section_out, grad_features, grad_weight, gain_gradient, shift_gradient)


def solution(mesh):
    gx, gy, gz = (mesh.shape[name] for name in ("gx", "gy", "gz"))
    fine = Mesh(mesh.devices.reshape(gx // 2, 2, gy // 2, 2, gz), ALL)
    block = (("z", "yh"), ("x", "c"), "yl")
    in_specs = (P(*block, None), P(*block), P(), P(), P(), P(*block, None))
    out_specs = (P(*block, None), P(*block, None), P(), P(), P())
    return jax.shard_map(local, mesh=fine, in_specs=in_specs, out_specs=out_specs, check_vma=False)
```

```python
import jax
import jax.numpy as jnp
from jax import lax
from jax.experimental import pallas as pl
from jax.experimental.pallas import tpu as pltpu
from jax.sharding import Mesh, PartitionSpec as P

BF = jnp.bfloat16
F32 = jnp.float32
ALL = ("z", "yh", "x", "c", "yl")
NEAR = ("c", "yh", "x", "yl")
PLANE = ("yh", "x", "yl")
GX, GY, GZ = (("z", "yh"), ("x", "c"), ("yl",))
FAR = ("z",)
PARAMS = pltpu.CompilerParams(vmem_limit_bytes=24 * 1024 * 1024)
WIDE = pltpu.CompilerParams(vmem_limit_bytes=60 * 1024 * 1024)


def call(kernel, outs, args, scratch=(), flops=100_000_000):
    size = sum(a.size * a.dtype.itemsize for a in args) + sum(o.size * o.dtype.itemsize for o in outs)
    return pl.pallas_call(
        kernel,
        out_shape=outs,
        in_specs=[pl.BlockSpec(memory_space=pltpu.VMEM) for _ in args],
        out_specs=[pl.BlockSpec(memory_space=pltpu.VMEM) for _ in outs],
        scratch_shapes=list(scratch),
        compiler_params=PARAMS,
        cost_estimate=pl.CostEstimate(flops=flops, bytes_accessed=size, transcendentals=0),
    )(*args)


def shape(dims, dtype):
    return jax.ShapeDtypeStruct(dims, dtype)


def dot(left, right, dims=((1,), (0,))):
    return lax.dot_general(left, right, (dims, ((), ())), preferred_element_type=F32)


def row_picker(rows, step, offset):
    r = lax.broadcasted_iota(jnp.int32, (rows, rows * step), 0)
    k = lax.broadcasted_iota(jnp.int32, (rows, rows * step), 1)
    return (k == r * step + offset).astype(BF)


def rows_at(value, depth):
    return jnp.concatenate([value[i, depth : depth + 1] for i in range(value.shape[0])], axis=0)


def with_edge(value, edge, at, shift):
    groups, depth, lanes = value.shape
    moved = pltpu.roll(value.reshape(groups * depth, lanes), shift % (groups * depth), 0)
    moved = moved.reshape(groups, depth, lanes)
    q = lax.broadcasted_iota(jnp.int32, value.shape, 1)
    return jnp.where(q == at, jnp.broadcast_to(edge[:, None, :], value.shape), moved)


def mask_row(active, mz, width):
    ny, z = active.shape
    pair = lax.broadcasted_iota(jnp.int32, (mz, z), 1) // 2
    sel = (pair == lax.broadcasted_iota(jnp.int32, (mz, z), 0)).astype(F32)
    lane = lax.broadcasted_iota(jnp.int32, (z, width), 1) // (width // 2)
    widen = (lax.broadcasted_iota(jnp.int32, (z, width), 0) % 2 == lane).astype(BF)
    rep = jnp.broadcast_to(active.astype(F32)[:, None, :], (ny, mz, z)) * sel[None]
    m = dot(rep.astype(BF).reshape(ny * mz, z), widen).astype(BF)
    return m.reshape(ny // 2, 2, mz, width)


def ring_index(axes):
    index = 0
    for name in axes:
        index = index * lax.axis_size(name) + lax.axis_index(name)
    return index


def ring_size(axes):
    size = 1
    for name in axes:
        size = size * lax.axis_size(name)
    return size


def unless(condition):
    return jnp.where(condition, 0.0, 1.0)


def face_kernel(feat, active, pack, row, cells, sems):
    _, slabs, mz, width = pack.shape
    my = slabs - 1
    copies = [
        pltpu.make_async_copy(feat.at[feat.shape[0] - 1], row, sems.at[0]),
        pltpu.make_async_copy(active.at[active.shape[0] - 1], cells, sems.at[1]),
    ]
    for copy in copies:
        copy.start()
    keep = unless(ring_index(GX) == ring_size(GX) - 1)
    pick = row_picker(my, mz, mz - 1)
    copies[1].wait()
    m = mask_row(cells[...], mz, width)
    copies[0].wait()
    value = row[...].reshape(m.shape) * m
    for py in range(2):
        held = (value[:, py].astype(F32) * keep).astype(BF)
        pack[py, :my] = held
        pack[py, my] = dot(pick, held.reshape(my * mz, width)).astype(BF)


def mask_kernel(feat, active, gain, bias, xin, act, zface, norm):
    nx, _, my, mz, width = xin.shape
    pick = row_picker(my, mz, mz - 1)
    norm[0:1] = gain[...]
    norm[1:2] = bias[...]
    count = None
    for x in range(nx):
        m = mask_row(active[x], mz, width)
        value = feat[x].reshape(m.shape) * m
        for py in range(2):
            part = m[:, py]
            held = value[:, py]
            xin[x, py] = held
            zface[x, py] = dot(pick, held.reshape(my * mz, width)).astype(BF)
            term = part.astype(F32).reshape(my * mz, width)
            count = term if count is None else count + term
        if x % 2 == 1:
            both = count + pltpu.roll(count, width // 2, 1)
            act[x // 2] = (both > 0.0).astype(F32).astype(BF).reshape(my, mz, width)
            count = None


def tile_of(xin, xh, yh, row, b):
    py = 0 if b == 1 else 1
    my = xin.shape[2]
    base = xh[py, :my] if row == 0 else xin[row - 1, py]
    if b == 0:
        base = jnp.concatenate([yh[row][None], base[: my - 1]], axis=0)
    return base


def edge_of(zh, row, b):
    base = zh[2 * row + (0 if b == 1 else 1)]
    if b == 0:
        wide = base.astype(F32)
        first = zh[zh.shape[0] - 1].astype(F32)[row : row + 1]
        wide = jnp.concatenate([first, wide[: wide.shape[0] - 1]], axis=0)
        base = wide.astype(BF)
    return base


TAPS = [(a, b) for a in range(3) for b in range(3)]


def build_matrix(weight, wmat):
    half, cout = weight.shape[3:]
    width = 2 * half
    zero = jnp.zeros((half, cout), BF)
    for i, (a, b) in enumerate(TAPS):
        lo = i * width
        wmat[lo : lo + half, :cout] = weight[a, b, 1]
        wmat[lo + half : lo + width, :cout] = weight[a, b, 2]
        wmat[lo : lo + half, cout:] = zero
        wmat[lo + half : lo + width, cout:] = weight[a, b, 0]


OFF = 1e30


def standardized(value, mean, rstd):
    active = value < 0.1 * OFF
    return jnp.where(active, 1.0, 0.0), jnp.where(active, value - mean, 0.0) * rstd


def slope_of(normed, sig, cot):
    return cot * sig * (1.0 + normed * (1.0 - sig))


def rim_parts(value, cot):
    return [part.astype(BF) for part in split(value, 2) + [cot]]


def merge_kernel(parts, xd, yface, zface, out, yplane):
    mx = yface.shape[1]
    my = zface.shape[2]
    counts, sums, squares = (
        jnp.concatenate([parts[j, i : i + 1] for j in range(parts.shape[0])], axis=0) for i in range(3)
    )
    count = jnp.sum(counts, axis=0, keepdims=True)
    total = jnp.sum(sums, axis=0, keepdims=True)
    mean = total / jnp.maximum(count, 1.0)
    apart = sums / jnp.maximum(counts, 1.0) - mean
    square = jnp.sum(squares + counts * apart * apart, axis=0, keepdims=True)
    for i in range(out.shape[0]):
        out[i, 0:1] = count
        out[i, 1:2] = total
        out[i, 2:3] = square
    depth = yplane.shape[2]
    yplane[:, :mx] = yface[...]
    yplane[:, mx] = xd[:, 0]
    for i in range(3):
        rows = [zface[i, m].astype(F32)[0:1] for m in range(mx)] + [xd[i, my].astype(F32)[0:1]]
        rows.append(jnp.zeros((depth - mx - 1, yplane.shape[3]), F32))
        yplane[i, mx + 1] = jnp.concatenate(rows, axis=0).astype(BF)


def rim_kernel(pre, cot, xface, yface, zface):
    mx, my, mz, cout = pre.shape
    for m in range(mx):
        planes = (pre[m], cot[m].astype(F32))
        side = rim_parts(*[rows_at(part, 0) for part in planes])
        line = rim_parts(*[part[0] for part in planes])
        whole = rim_parts(*planes) if m == 0 else None
        for i in range(3):
            yface[i, m] = line[i]
            zface[i, m] = side[i]
            if m == 0:
                xface[i, :my] = whole[i]
                xface[i, my] = side[i]


def forward_kernel(xin, act, xh, yh, zh, weight, pre, stats, wmat):
    mx, my, mz, cout = pre.shape
    width = xin.shape[4]
    build_matrix(weight, wmat)
    rows = my * mz
    total = jnp.zeros((1, cout), F32)
    count = jnp.zeros((1, cout), F32)
    w = wmat[...]
    for m in range(mx):
        left = jnp.concatenate(
            [tile_of(xin, xh, yh, 2 * m + a, b).reshape(rows, width) for a, b in TAPS], axis=1
        )
        edge = jnp.concatenate([edge_of(zh, 2 * m + a, b) for a, b in TAPS], axis=1)
        out = dot(left, w)
        rim = dot(edge, w[:, cout:])
        prev = with_edge(out[:, cout:].reshape(my, mz, cout), rim, 0, 1)
        value = out[:, :cout].reshape(my, mz, cout) + prev
        on = act[m].astype(F32)
        pre[m] = jnp.where(on > 0.0, value, OFF)
        total = total + jnp.sum((on * value).reshape(rows, cout), axis=0, keepdims=True)
        count = count + jnp.sum(on.reshape(rows, cout), axis=0, keepdims=True)
    mean = total / jnp.maximum(count, 1.0)
    squares = jnp.zeros((1, cout), F32)
    for m in range(mx):
        on = act[m].astype(F32).reshape(rows, cout)
        apart = jnp.where(on > 0.0, pre[m].reshape(rows, cout) - mean, 0.0)
        squares = squares + jnp.sum(apart * apart, axis=0, keepdims=True)
    for i in range(stats.shape[0]):
        stats[i, 0:1] = count
        stats[i, 1:2] = total
        stats[i, 2:3] = squares


def split(value, parts):
    out = []
    for _ in range(parts):
        out.append(value.astype(BF).astype(F32))
        value = value - out[-1]
    return out


def rounded(value):
    return value.astype(BF).astype(F32)


def outer(column, rows):
    return lax.dot_general(
        column, rows, (((0,), (0,)), ((), ())), precision=lax.Precision.HIGHEST, preferred_element_type=F32
    )


def write_chunk(ref, i, body, columns, common):
    left, right = common
    line = lax.broadcasted_iota(jnp.int32, left.shape, 0)
    for k, column in enumerate(columns):
        for at, part in enumerate(split(column, 3)):
            left = jnp.where(line == 3 * k + at, part, left)
    ref[i] = jnp.concatenate([body, jnp.concatenate([left, right], axis=1)], axis=0).astype(BF)


def common_rows(alphas, highs, beta, first, second):
    zero = jnp.zeros_like(beta)
    return (
        jnp.concatenate([zero] * 6 + alphas, axis=0),
        jnp.concatenate(highs + [beta] + split(first, 3) + split(second, 2), axis=0),
    )


def total_of(rows, start, stop):
    value = rows[start : start + 1]
    for i in range(start + 1, stop):
        value = value + rows[i : i + 1]
    return value


def read_chunks(ref):
    devices, depth, _ = ref.shape
    rows = depth - 8
    cout = ref.shape[2] // 2
    slopes = hats = None
    firsts = seconds = betas = None
    columns, vectors = ([], [])
    for j in range(devices):
        value = ref[j].astype(F32)
        left, right = (value[rows:, :cout], value[rows:, cout:])
        part = value[:rows, cout:]
        beta = right[2:3]
        term = value[:rows, :cout] + part * beta
        first = total_of(right, 3, 6)
        second = total_of(right, 6, 8)
        for k in range(2):
            columns.append(total_of(left, 3 * k, 3 * k + 3))
            vectors.append(jnp.concatenate([left[6 + k : 7 + k], right[k : k + 1]], axis=1))
        if j == 0:
            slopes, hats, firsts, seconds, betas = (term, part, first, second, beta)
        else:
            slopes, hats = (slopes + term, hats + part)
            firsts, seconds, betas = (firsts + first, seconds + second, betas + beta)
    columns = jnp.concatenate(columns, axis=0)
    vectors = jnp.concatenate(vectors, axis=0)
    both = outer(columns, vectors)[:rows]
    slopes = slopes + both[:, :cout]
    hats = hats + both[:, cout:]
    column = jnp.sum(columns, axis=0, keepdims=True)
    middle = jnp.sum(vectors, axis=0, keepdims=True) / (2 * devices)
    return slopes, hats, column, firsts, seconds, middle[:, :cout], betas / devices, middle[:, cout:]


def eight(row):
    return jnp.broadcast_to(row, (8, row.shape[1]))


def lone(row):
    return jnp.where(lax.broadcasted_iota(jnp.int32, (8, row.shape[1]), 0) == 0, eight(row), 0.0)


def slope_kernel(
    pre, cot, par, xin, xh, yh, zh, xd, yd, zface, out, keep, send, zplane, slope, acc, big
):
    mx, my, mz, cout = pre.shape
    width = xin.shape[4]
    half = width // 2
    rows = my * mz
    mean, rstd, gain, bias = (par[i : i + 1] for i in range(4))
    zplane[:, :mx] = zface[...]
    zplane[:, mx] = xd[:, my]
    zplane[:, mx + 1] = yd[:, mx + 1]
    first, second, count, high, square = (jnp.zeros((1, cout), F32) for _ in range(5))
    for m in range(mx):
        on, hat = standardized(pre[m].reshape(rows, cout), mean, rstd)
        normed = hat * gain + bias
        sig = jax.nn.sigmoid(normed)
        out[m] = (on * normed * sig).astype(BF).reshape(my, mz, cout)
        tilt = slope_of(normed, sig, on * cot[m].astype(F32).reshape(rows, cout))
        slope[m] = tilt.reshape(my, mz, cout)
        first = first + jnp.sum(tilt, axis=0, keepdims=True)
        second = second + jnp.sum(tilt * hat, axis=0, keepdims=True)
        count = count + jnp.sum(on, axis=0, keepdims=True)
        high = high + jnp.sum(hat, axis=0, keepdims=True)
        square = square + jnp.sum(hat * hat, axis=0, keepdims=True)
    some = jnp.maximum(count, 1.0)
    alpha = rounded(first / some)
    high = rounded(high / some)
    beta = (second - high * first) / jnp.maximum(square - count * high * high, 0.01 * some)
    beta = rounded(beta)
    last = lax.broadcasted_iota(jnp.int32, (my, mz, cout), 1) == mz - 1
    total = None
    rims = [[], [], []]
    for m in range(mx):
        on, hat = standardized(pre[m].reshape(rows, cout), mean, rstd)
        hat = on * (hat - high)
        rest = slope[m].reshape(rows, cout) - on * alpha - hat * beta
        here, after = ([], [])
        for i, part in enumerate((rest, hat, on)):
            held = part.astype(BF)
            lines = 8 if i == 2 else cout
            wide = held.astype(F32)
            rims[i].append(rows_at(wide.reshape(my, mz, cout), 0))
            nxt = pltpu.roll(wide, rows - 1, 0).reshape(my, mz, cout)
            nxt = jnp.where(last, 0.0, nxt).reshape(rows, cout)
            here.append(wide.T[:lines])
            after.append(nxt.T[:lines])
        right = jnp.concatenate(here + after, axis=0).astype(BF)
        left = jnp.concatenate(
            [tile_of(xin, xh, yh, 2 * m + a, b).reshape(rows, width) for a, b in TAPS], axis=1
        )
        term = dot(right, left)
        total = term if total is None else total + term
    rim = [jnp.concatenate(parts, axis=0).T for parts in rims]
    rim = jnp.concatenate([rim[0], rim[1], rim[2][:8]], axis=0).astype(BF)
    edge = jnp.concatenate(
        [
            jnp.concatenate([edge_of(zh, 2 * m + a, b) for a, b in TAPS], axis=1)
            for m in range(mx)
        ],
        axis=0,
    )
    size = 2 * cout + 8
    own = total[:size]
    low = total[size:] + dot(rim, edge)
    taps = 3 * len(TAPS)
    for i in range(len(TAPS)):
        at = i * width
        to = 3 * half * i
        acc[to : to + half] = low[: 2 * cout, at : at + width].T[half:]
        acc[to + half : to + 3 * half] = own[: 2 * cout, at : at + width].T
    if acc.shape[0] > half * taps:
        acc[half * taps :] = jnp.zeros((acc.shape[0] - half * taps, 2 * cout), F32)
    zero = jnp.zeros_like(beta)
    common = common_rows([alpha, zero], [high, zero], beta, first, second)
    lane = lax.broadcasted_iota(jnp.int32, (8, width), 1)
    _, plane, depth, _ = big.shape
    depth = depth - 8
    for n in range(2 * plane):
        column = jnp.zeros((8, width), F32)
        for tap in range(taps):
            start = half * tap - depth * n
            lo, hi = (max(start, 0), min(start + half, depth))
            if lo < hi:
                at = tap // 3 * width
                row = (low if tap % 3 == 0 else own)[2 * cout :, at : at + width]
                shift = (start - (0 if tap % 3 == 1 else half)) % width
                if shift:
                    row = pltpu.roll(row, shift, 1)
                column = jnp.where((lane >= lo) & (lane < hi), row, column)
        write_chunk(big.at[n // plane], n % plane, acc[depth * n : depth * (n + 1)], [column], common)
    core = lax.axis_index("c")
    keep[...] = big[core]
    send[...] = big[1 - core]


def pair_kernel(mine, other, out):
    _, depth, width = mine.shape
    rows = depth - 8
    cout = width // 2
    for i in range(mine.shape[0]):
        pair = [ref[i].astype(F32) for ref in (mine, other)]
        left = [value[rows:, :cout] for value in pair]
        right = [value[rows:, cout:] for value in pair]
        beta = rounded(0.5 * (right[0][2:3] + right[1][2:3]))
        first = total_of(right[0], 3, 6) + total_of(right[1], 3, 6)
        second = total_of(right[0], 6, 8) + total_of(right[1], 6, 8)
        slopes = pair[0][:rows, :cout] + pair[1][:rows, :cout]
        hats = pair[0][:rows, cout:] + pair[1][:rows, cout:]
        for value, vectors in zip(pair, right):
            slopes = slopes + value[:rows, cout:] * (vectors[2:3] - beta)
        common = common_rows(
            [part[6:7] for part in left], [part[0:1] for part in right], beta, first, second
        )
        columns = [eight(total_of(part, 0, 3)) for part in left]
        write_chunk(out, i, jnp.concatenate([slopes, hats], axis=1), columns, common)


def near_kernel(parts, out):
    slopes, hats, column, first, second, alpha, beta, high = read_chunks(parts)
    rows = slopes.shape[0]
    cout = slopes.shape[1]
    alpha, beta, high = (rounded(alpha), rounded(beta), rounded(high))
    both = outer(lone(column), lone(jnp.concatenate([alpha, high], axis=1)))[:rows]
    hats = hats - both[:, cout:]
    slopes = slopes - both[:, :cout] - hats * beta
    zero = jnp.zeros_like(beta)
    common = common_rows([alpha, zero], [high, zero], beta, first, second)
    body = jnp.concatenate([slopes, hats], axis=1)
    for i in range(out.shape[0]):
        write_chunk(out, i, body, [eight(column)], common)


def far_kernel(parts, par, dw, shift_out, tilt_out, both):
    _, rstd, gain, _, count = (par[i : i + 1] for i in range(5))
    slopes, hats, column, first, second, _, _, _ = read_chunks(parts)
    shift, tilt = (first / count, second / count)
    shift_out[...] = shift
    tilt_out[...] = tilt
    both[0:1] = shift
    both[1:2] = tilt
    value = slopes - outer(lone(column), lone(shift))[: slopes.shape[0]] - hats * tilt
    value = (value * (rstd * gain / count)).astype(BF)
    for i in range(dw.shape[0]):
        dw[i] = value


def input_kernel(pre, cot, par, grads, xd, yd, zd, active, weight, out, ext, nxt, wmat):
    mx, my, mz, cout = pre.shape
    width = out.shape[4]
    rows = my * mz
    mean, rstd, gain, bias = (par[i : i + 1] for i in range(4))
    shift, tilt = (grads[i : i + 1] for i in range(2))
    scale = rstd * gain
    inside = [
        unless(ring_index(axes) == ring_size(axes) - 1) for axes in (GX, GY, GZ)
    ]

    def gradient(value, cot, keep):
        on, hat = standardized(value, mean, rstd)
        normed = hat * gain + bias
        slope = slope_of(normed, jax.nn.sigmoid(normed), cot)
        return (on * keep * scale * (slope - shift - hat * tilt)).astype(BF)

    def rim(parts, keep):
        high, low, cot = (part.astype(F32) for part in parts)
        return gradient(high + low, cot, keep)

    build_matrix(weight, wmat)
    for r in range(mx + 1):
        keep = 1.0 if r < mx else inside[0]
        if r < mx:
            own = cot[r].astype(F32).reshape(rows, cout)
            base = gradient(pre[r].reshape(rows, cout), own, keep).reshape(my, mz, cout)
        else:
            flat = [xd[i, :my].reshape(rows, cout) for i in range(3)]
            base = rim(flat, keep).reshape(my, mz, cout)
        row = rim([yd[i, r] for i in range(3)], keep * inside[1])
        ext[r, :my] = base
        ext[r, my] = row
        whole = jnp.concatenate([base, row[None]], axis=0).astype(F32)
        side = rim([zd[i, r] for i in range(3)], keep * inside[2]).astype(F32)
        last = [zd[i, mx + 1].astype(F32)[r : r + 1] for i in range(3)]
        last = rim(last, keep * inside[1] * inside[2]).astype(F32)
        nxt[r] = with_edge(whole, jnp.concatenate([side, last], axis=0), mz - 1, -1).astype(BF)
    taps = (((1, 0),), ((2, 0), (0, 1)))
    for m in range(mx):
        for px in range(2):
            x = 2 * m + px
            mask = mask_row(active[x], mz, width)
            for py in range(2):
                left, right = ([], [])
                for a, sx in taps[px]:
                    for b, sy in taps[py]:
                        left.append(ext[m + sx, sy : sy + my].reshape(rows, cout))
                        left.append(nxt[m + sx, sy : sy + my].reshape(rows, cout))
                        at = (a * 3 + b) * width
                        right.append(wmat[at : at + width])
                left = jnp.concatenate(left, axis=1)
                right = jnp.concatenate(right, axis=1)
                value = dot(left, right, ((1,), (1,)))
                value = value * mask[:, py].astype(F32).reshape(rows, width)
                out[x, :, py] = value.astype(BF).reshape(my, mz, width)


def moved(value, axes, by):
    count = lax.axis_size(axes)
    return lax.ppermute(value, axes, [(i, (i + by) % count) for i in range(count)])


def beyond(value, axes, by):
    end = lax.axis_size(axes) - 1 if by > 0 else 0
    keep = (lax.axis_index(axes) != end).astype(value.dtype)
    return moved(value * keep, axes, by)


def slab(rows, like):
    return jnp.pad(rows, ((0, like - rows.shape[0]), (0, 0)))[None]


def exchanged(value, axes):
    return lax.all_to_all(value, axes, 0, 0)


def merged(parts):
    counts, sums, squares = (parts[:, 0], parts[:, 1], parts[:, 2])
    count = jnp.sum(counts, axis=0)
    total = jnp.sum(sums, axis=0)
    mean = total / jnp.maximum(count, 1.0)
    apart = sums / jnp.maximum(counts, 1.0) - mean
    return jnp.stack([count, total, jnp.sum(squares + counts * apart * apart, axis=0)])


def local(features, active, weight, gain, bias, cotangent):
    vx, vy, mz, width = features.shape
    cin = width // 2
    cout = weight.shape[4]
    mx, my = (vx // 2, vy // 2)
    near = lax.axis_size(NEAR)
    pack = pl.pallas_call(
        face_kernel,
        out_shape=shape((2, my + 1, mz, width), BF),
        in_specs=[pl.BlockSpec(memory_space=pltpu.HBM)] * 2,
        out_specs=pl.BlockSpec(memory_space=pltpu.VMEM),
        scratch_shapes=[
            pltpu.VMEM((vy, mz, width), BF),
            pltpu.VMEM((vy, 2 * mz), jnp.int32),
            pltpu.SemaphoreType.DMA((2,)),
        ],
        compiler_params=WIDE,
        cost_estimate=pl.CostEstimate(flops=10_000_000, bytes_accessed=400_000, transcendentals=0),
    )(features, active)
    xh = moved(pack, GX, 1)
    xin, act, zface, norm = call(
        mask_kernel,
        [
            shape((vx, 2, my, mz, width), BF),
            shape((mx, my, mz, width), BF),
            shape((vx, 2, my, width), BF),
            shape((2, cout), F32),
        ],
        [features, active, gain[None], bias[None]],
    )
    yface = jnp.concatenate([xh[1:2, my - 1], xin[:, 1, my - 1]], axis=0)
    zfaces = jnp.concatenate([xh[None, :, my], zface], axis=0)
    rows = vx + 1
    yh = beyond(jnp.concatenate([yface, slab(zfaces[:, 1, my - 1], mz)], axis=0), GY, 1)
    zfaces = jnp.concatenate([zfaces.reshape(2 * rows, my, width), yh[rows:]], axis=0)
    zh = beyond(zfaces, GZ, 1)
    pre, stats = call(
        forward_kernel,
        [
            shape((mx, my, mz, cout), F32),
            shape((near, 3, cout), F32),
        ],
        [xin, act, xh, yh, zh, weight],
        scratch=[pltpu.VMEM((9 * width, 2 * cout), BF)],
        flops=1_200_000_000,
    )
    xface, yface, zface = call(
        rim_kernel,
        [
            shape((3, my + 1, mz, cout), BF),
            shape((3, mx, mz, cout), BF),
            shape((3, mx, my, cout), BF),
        ],
        [pre, cotangent],
    )
    xd = moved(xface, GX, -1)
    stats, yplane = call(
        merge_kernel,
        [shape((lax.axis_size(FAR), 3, cout), F32), shape((3, mx + 2, mz, cout), BF)],
        [exchanged(stats, NEAR), xd, yface, zface],
    )
    yd = moved(yplane, GY, -1)
    stats = merged(exchanged(stats, FAR))
    count = stats[0]
    mean = stats[1] / count
    rstd = lax.rsqrt(stats[2] / count + 1e-05)
    par = jnp.stack([mean, rstd, norm[0], norm[1], count])
    taps = 27 * cin
    rows = -(-taps // (8 * near)) * 8
    plane = lax.axis_size(PLANE)
    chunks = (plane, rows + 8, 2 * cout)
    section_out, big, send, zplane = call(
        slope_kernel,
        [
            shape((mx, my, mz, cout), BF),
            shape(chunks, BF),
            shape(chunks, BF),
            shape((3, mx + 2, my, cout), BF),
        ],
        [pre, cotangent, par, xin, xh, yh, zh, xd, yd, zface],
        scratch=[
            pltpu.VMEM(pre.shape, F32),
            pltpu.VMEM((near * rows, 2 * cout), F32),
            pltpu.VMEM((2,) + chunks, BF),
        ],
        flops=2_400_000_000,
    )
    (big,) = call(pair_kernel, [shape(chunks, BF)], [big, moved(send, "c", 1)])
    zd = moved(zplane, GZ, -1)
    far = lax.axis_size(FAR)
    (big,) = call(near_kernel, [shape((far, rows + 8, 2 * cout), BF)], [exchanged(big, PLANE)])
    dw, shift, tilt, grads = call(
        far_kernel,
        [
            shape((plane, rows, cout), BF),
            shape((1, cout), F32),
            shape((1, cout), F32),
            shape((2, cout), F32),
        ],
        [exchanged(big, FAR), par],
    )
    shift_gradient, gain_gradient = (shift.reshape(cout), tilt.reshape(cout))
    (grad_features,) = call(
        input_kernel,
        [shape((vx, my, 2, mz, width), BF)],
        [pre, cotangent, par, grads, xd, yd, zd, active, weight],
        scratch=[
            pltpu.VMEM((mx + 1, my + 1, mz, cout), BF),
            pltpu.VMEM((mx + 1, my + 1, mz, cout), BF),
            pltpu.VMEM((9 * width, 2 * cout), BF),
        ],
        flops=2_400_000_000,
    )
    mine, grad_features = lax.optimization_barrier((exchanged(dw, PLANE), grad_features))
    other = moved(mine, "c", 1)
    low = lax.axis_index("c") == 0
    grad_weight = jnp.stack([jnp.where(low, mine, other), jnp.where(low, other, mine)])
    grad_weight = grad_weight.reshape(near * rows, cout)[:taps]
    grad_weight = grad_weight.astype(F32).reshape(weight.shape)
    grad_features = grad_features.reshape(features.shape)
    return (section_out, grad_features, grad_weight, gain_gradient, shift_gradient)


def solution(mesh):
    gx, gy, gz = (mesh.shape[name] for name in ("gx", "gy", "gz"))
    fine = Mesh(mesh.devices.reshape(gx // 2, 2, gy // 2, 2, gz), ALL)
    block = (("z", "yh"), ("x", "c"), "yl")
    in_specs = (P(*block, None), P(*block), P(), P(), P(), P(*block, None))
    out_specs = (P(*block, None), P(*block, None), P(), P(), P())
    return jax.shard_map(local, mesh=fine, in_specs=in_specs, out_specs=out_specs, check_vma=False)
```

```python
import jax
import jax.numpy as jnp
from jax import lax
from jax.experimental import pallas as pl
from jax.experimental.pallas import tpu as pltpu
from jax.sharding import Mesh, PartitionSpec as P

BF = jnp.bfloat16
F32 = jnp.float32
ALL = ("z", "yh", "x", "c", "yl")
NEAR = ("c", "yh", "x", "yl")
PLANE = ("yh", "x", "yl")
GX, GY, GZ = (("z", "yh"), ("x", "c"), ("yl",))
FAR = ("z",)
PARAMS = pltpu.CompilerParams(vmem_limit_bytes=24 * 1024 * 1024)
WIDE = pltpu.CompilerParams(vmem_limit_bytes=60 * 1024 * 1024)


def call(kernel, outs, args, scratch=(), flops=100_000_000):
    size = sum(a.size * a.dtype.itemsize for a in args) + sum(o.size * o.dtype.itemsize for o in outs)
    return pl.pallas_call(
        kernel,
        out_shape=outs,
        in_specs=[pl.BlockSpec(memory_space=pltpu.VMEM) for _ in args],
        out_specs=[pl.BlockSpec(memory_space=pltpu.VMEM) for _ in outs],
        scratch_shapes=list(scratch),
        compiler_params=PARAMS,
        cost_estimate=pl.CostEstimate(flops=flops, bytes_accessed=size, transcendentals=0),
    )(*args)


def shape(dims, dtype):
    return jax.ShapeDtypeStruct(dims, dtype)


def dot(left, right, dims=((1,), (0,))):
    return lax.dot_general(left, right, (dims, ((), ())), preferred_element_type=F32)


def row_picker(rows, step, offset):
    r = lax.broadcasted_iota(jnp.int32, (rows, rows * step), 0)
    k = lax.broadcasted_iota(jnp.int32, (rows, rows * step), 1)
    return (k == r * step + offset).astype(BF)


def rows_at(value, depth):
    return jnp.concatenate([value[i, depth : depth + 1] for i in range(value.shape[0])], axis=0)


def with_edge(value, edge, at, shift):
    groups, depth, lanes = value.shape
    moved = pltpu.roll(value.reshape(groups * depth, lanes), shift % (groups * depth), 0)
    moved = moved.reshape(groups, depth, lanes)
    q = lax.broadcasted_iota(jnp.int32, value.shape, 1)
    return jnp.where(q == at, jnp.broadcast_to(edge[:, None, :], value.shape), moved)


def mask_row(active, mz, width):
    ny, z = active.shape
    pair = lax.broadcasted_iota(jnp.int32, (mz, z), 1) // 2
    sel = (pair == lax.broadcasted_iota(jnp.int32, (mz, z), 0)).astype(F32)
    lane = lax.broadcasted_iota(jnp.int32, (z, width), 1) // (width // 2)
    widen = (lax.broadcasted_iota(jnp.int32, (z, width), 0) % 2 == lane).astype(BF)
    rep = jnp.broadcast_to(active.astype(F32)[:, None, :], (ny, mz, z)) * sel[None]
    m = dot(rep.astype(BF).reshape(ny * mz, z), widen).astype(BF)
    return m.reshape(ny // 2, 2, mz, width)


def ring_index(axes):
    index = 0
    for name in axes:
        index = index * lax.axis_size(name) + lax.axis_index(name)
    return index


def ring_size(axes):
    size = 1
    for name in axes:
        size = size * lax.axis_size(name)
    return size


def unless(condition):
    return jnp.where(condition, 0.0, 1.0)


def face_kernel(feat, active, pack, row, cells, sems):
    _, slabs, mz, width = pack.shape
    my = slabs - 1
    copies = [
        pltpu.make_async_copy(feat.at[feat.shape[0] - 1], row, sems.at[0]),
        pltpu.make_async_copy(active.at[active.shape[0] - 1], cells, sems.at[1]),
    ]
    for copy in copies:
        copy.start()
    keep = unless(ring_index(GX) == ring_size(GX) - 1)
    pick = row_picker(my, mz, mz - 1)
    copies[1].wait()
    m = mask_row(cells[...], mz, width)
    copies[0].wait()
    value = row[...].reshape(m.shape) * m
    for py in range(2):
        held = (value[:, py].astype(F32) * keep).astype(BF)
        pack[py, :my] = held
        pack[py, my] = dot(pick, held.reshape(my * mz, width)).astype(BF)


def mask_kernel(feat, active, gain, bias, xin, act, zface, norm):
    nx, _, my, mz, width = xin.shape
    pick = row_picker(my, mz, mz - 1)
    norm[0:1] = gain[...]
    norm[1:2] = bias[...]
    count = None
    for x in range(nx):
        m = mask_row(active[x], mz, width)
        value = feat[x].reshape(m.shape) * m
        for py in range(2):
            part = m[:, py]
            held = value[:, py]
            xin[x, py] = held
            zface[x, py] = dot(pick, held.reshape(my * mz, width)).astype(BF)
            term = part.astype(F32).reshape(my * mz, width)
            count = term if count is None else count + term
        if x % 2 == 1:
            both = count + pltpu.roll(count, width // 2, 1)
            act[x // 2] = (both > 0.0).astype(F32).astype(BF).reshape(my, mz, width)
            count = None


def tile_of(xin, xh, yh, row, b):
    py = 0 if b == 1 else 1
    my = xin.shape[2]
    base = xh[py, :my] if row == 0 else xin[row - 1, py]
    if b == 0:
        base = jnp.concatenate([yh[row][None], base[: my - 1]], axis=0)
    return base


def edge_of(zh, row, b):
    base = zh[2 * row + (0 if b == 1 else 1)]
    if b == 0:
        wide = base.astype(F32)
        first = zh[zh.shape[0] - 1].astype(F32)[row : row + 1]
        wide = jnp.concatenate([first, wide[: wide.shape[0] - 1]], axis=0)
        base = wide.astype(BF)
    return base


TAPS = [(a, b) for a in range(3) for b in range(3)]


def build_matrix(weight, wmat):
    half, cout = weight.shape[3:]
    width = 2 * half
    zero = jnp.zeros((half, cout), BF)
    for i, (a, b) in enumerate(TAPS):
        lo = i * width
        wmat[lo : lo + half, :cout] = weight[a, b, 1]
        wmat[lo + half : lo + width, :cout] = weight[a, b, 2]
        wmat[lo : lo + half, cout:] = zero
        wmat[lo + half : lo + width, cout:] = weight[a, b, 0]


OFF = 1e30


def standardized(value, mean, rstd):
    active = value < 0.1 * OFF
    return jnp.where(active, 1.0, 0.0), jnp.where(active, value - mean, 0.0) * rstd


def slope_of(normed, sig, cot):
    return cot * sig * (1.0 + normed * (1.0 - sig))


def rim_parts(value, cot):
    return [part.astype(BF) for part in split(value, 2) + [cot]]


def merge_kernel(parts, out):
    counts, sums, squares = (
        jnp.concatenate([parts[j, i : i + 1] for j in range(parts.shape[0])], axis=0) for i in range(3)
    )
    count = jnp.sum(counts, axis=0, keepdims=True)
    total = jnp.sum(sums, axis=0, keepdims=True)
    mean = total / jnp.maximum(count, 1.0)
    apart = sums / jnp.maximum(counts, 1.0) - mean
    square = jnp.sum(squares + counts * apart * apart, axis=0, keepdims=True)
    out[...] = jnp.concatenate([count, total, square] + [jnp.zeros_like(count)] * 5, axis=0)


def pack_kernel(stats, xd, yface, zface, out, yplane):
    mx = yface.shape[1]
    my = zface.shape[2]
    for i in range(out.shape[0]):
        out[i] = stats[:3]
    depth = yplane.shape[2]
    yplane[:, :mx] = yface[...]
    yplane[:, mx] = xd[:, 0]
    for i in range(3):
        rows = [zface[i, m].astype(F32)[0:1] for m in range(mx)] + [xd[i, my].astype(F32)[0:1]]
        rows.append(jnp.zeros((depth - mx - 1, yplane.shape[3]), F32))
        yplane[i, mx + 1] = jnp.concatenate(rows, axis=0).astype(BF)


def rim_kernel(pre, cot, xface, yface, zface):
    mx, my, mz, cout = pre.shape
    for m in range(mx):
        planes = (pre[m], cot[m].astype(F32))
        side = rim_parts(*[rows_at(part, 0) for part in planes])
        line = rim_parts(*[part[0] for part in planes])
        whole = rim_parts(*planes) if m == 0 else None
        for i in range(3):
            yface[i, m] = line[i]
            zface[i, m] = side[i]
            if m == 0:
                xface[i, :my] = whole[i]
                xface[i, my] = side[i]


def forward_kernel(xin, act, xh, yh, zh, weight, pre, stats, wmat):
    mx, my, mz, cout = pre.shape
    width = xin.shape[4]
    build_matrix(weight, wmat)
    rows = my * mz
    total = jnp.zeros((1, cout), F32)
    count = jnp.zeros((1, cout), F32)
    w = wmat[...]
    for m in range(mx):
        left = jnp.concatenate(
            [tile_of(xin, xh, yh, 2 * m + a, b).reshape(rows, width) for a, b in TAPS], axis=1
        )
        edge = jnp.concatenate([edge_of(zh, 2 * m + a, b) for a, b in TAPS], axis=1)
        out = dot(left, w)
        rim = dot(edge, w[:, cout:])
        prev = with_edge(out[:, cout:].reshape(my, mz, cout), rim, 0, 1)
        value = out[:, :cout].reshape(my, mz, cout) + prev
        on = act[m].astype(F32)
        pre[m] = jnp.where(on > 0.0, value, OFF)
        total = total + jnp.sum((on * value).reshape(rows, cout), axis=0, keepdims=True)
        count = count + jnp.sum(on.reshape(rows, cout), axis=0, keepdims=True)
    mean = total / jnp.maximum(count, 1.0)
    squares = jnp.zeros((1, cout), F32)
    for m in range(mx):
        on = act[m].astype(F32).reshape(rows, cout)
        apart = jnp.where(on > 0.0, pre[m].reshape(rows, cout) - mean, 0.0)
        squares = squares + jnp.sum(apart * apart, axis=0, keepdims=True)
    for i in range(stats.shape[0]):
        stats[i, 0:1] = count
        stats[i, 1:2] = total
        stats[i, 2:3] = squares


def split(value, parts):
    out = []
    for _ in range(parts):
        out.append(value.astype(BF).astype(F32))
        value = value - out[-1]
    return out


def rounded(value):
    return value.astype(BF).astype(F32)


def outer(column, rows):
    return lax.dot_general(
        column, rows, (((0,), (0,)), ((), ())), precision=lax.Precision.HIGHEST, preferred_element_type=F32
    )


def write_chunk(ref, i, body, columns, common):
    left, right = common
    line = lax.broadcasted_iota(jnp.int32, left.shape, 0)
    for k, column in enumerate(columns):
        for at, part in enumerate(split(column, 3)):
            left = jnp.where(line == 3 * k + at, part, left)
    ref[i] = jnp.concatenate([body, jnp.concatenate([left, right], axis=1)], axis=0).astype(BF)


def common_rows(alphas, highs, beta, first, second):
    zero = jnp.zeros_like(beta)
    return (
        jnp.concatenate([zero] * 6 + alphas, axis=0),
        jnp.concatenate(highs + [beta] + split(first, 3) + split(second, 2), axis=0),
    )


def total_of(rows, start, stop):
    value = rows[start : start + 1]
    for i in range(start + 1, stop):
        value = value + rows[i : i + 1]
    return value


def read_chunks(ref):
    devices, depth, _ = ref.shape
    rows = depth - 8
    cout = ref.shape[2] // 2
    slopes = hats = None
    firsts = seconds = betas = None
    columns, vectors = ([], [])
    for j in range(devices):
        value = ref[j].astype(F32)
        left, right = (value[rows:, :cout], value[rows:, cout:])
        part = value[:rows, cout:]
        beta = right[2:3]
        term = value[:rows, :cout] + part * beta
        first = total_of(right, 3, 6)
        second = total_of(right, 6, 8)
        for k in range(2):
            columns.append(total_of(left, 3 * k, 3 * k + 3))
            vectors.append(jnp.concatenate([left[6 + k : 7 + k], right[k : k + 1]], axis=1))
        if j == 0:
            slopes, hats, firsts, seconds, betas = (term, part, first, second, beta)
        else:
            slopes, hats = (slopes + term, hats + part)
            firsts, seconds, betas = (firsts + first, seconds + second, betas + beta)
    columns = jnp.concatenate(columns, axis=0)
    vectors = jnp.concatenate(vectors, axis=0)
    both = outer(columns, vectors)[:rows]
    slopes = slopes + both[:, :cout]
    hats = hats + both[:, cout:]
    column = jnp.sum(columns, axis=0, keepdims=True)
    middle = jnp.sum(vectors, axis=0, keepdims=True) / (2 * devices)
    return slopes, hats, column, firsts, seconds, middle[:, :cout], betas / devices, middle[:, cout:]


def eight(row):
    return jnp.broadcast_to(row, (8, row.shape[1]))


def lone(row):
    return jnp.where(lax.broadcasted_iota(jnp.int32, (8, row.shape[1]), 0) == 0, eight(row), 0.0)


def slope_kernel(
    pre, cot, par, xin, xh, yh, zh, _, out, keep, send, slope, acc, big
):
    mx, my, mz, cout = pre.shape
    width = xin.shape[4]
    half = width // 2
    rows = my * mz
    mean, rstd, gain, bias = (par[i : i + 1] for i in range(4))
    first, second, count, high, square = (jnp.zeros((1, cout), F32) for _ in range(5))
    for m in range(mx):
        on, hat = standardized(pre[m].reshape(rows, cout), mean, rstd)
        normed = hat * gain + bias
        sig = jax.nn.sigmoid(normed)
        out[m] = (on * normed * sig).astype(BF).reshape(my, mz, cout)
        tilt = slope_of(normed, sig, on * cot[m].astype(F32).reshape(rows, cout))
        slope[m] = tilt.reshape(my, mz, cout)
        first = first + jnp.sum(tilt, axis=0, keepdims=True)
        second = second + jnp.sum(tilt * hat, axis=0, keepdims=True)
        count = count + jnp.sum(on, axis=0, keepdims=True)
        high = high + jnp.sum(hat, axis=0, keepdims=True)
        square = square + jnp.sum(hat * hat, axis=0, keepdims=True)
    some = jnp.maximum(count, 1.0)
    alpha = rounded(first / some)
    high = rounded(high / some)
    beta = (second - high * first) / jnp.maximum(square - count * high * high, 0.01 * some)
    beta = rounded(beta)
    last = lax.broadcasted_iota(jnp.int32, (my, mz, cout), 1) == mz - 1
    total = None
    rims = [[], [], []]
    for m in range(mx):
        on, hat = standardized(pre[m].reshape(rows, cout), mean, rstd)
        hat = on * (hat - high)
        rest = slope[m].reshape(rows, cout) - on * alpha - hat * beta
        here, after = ([], [])
        for i, part in enumerate((rest, hat, on)):
            held = part.astype(BF)
            lines = 8 if i == 2 else cout
            wide = held.astype(F32)
            rims[i].append(rows_at(wide.reshape(my, mz, cout), 0))
            nxt = pltpu.roll(wide, rows - 1, 0).reshape(my, mz, cout)
            nxt = jnp.where(last, 0.0, nxt).reshape(rows, cout)
            here.append(wide.T[:lines])
            after.append(nxt.T[:lines])
        right = jnp.concatenate(here + after, axis=0).astype(BF)
        left = jnp.concatenate(
            [tile_of(xin, xh, yh, 2 * m + a, b).reshape(rows, width) for a, b in TAPS], axis=1
        )
        term = dot(right, left)
        total = term if total is None else total + term
    rim = [jnp.concatenate(parts, axis=0).T for parts in rims]
    rim = jnp.concatenate([rim[0], rim[1], rim[2][:8]], axis=0).astype(BF)
    edge = jnp.concatenate(
        [
            jnp.concatenate([edge_of(zh, 2 * m + a, b) for a, b in TAPS], axis=1)
            for m in range(mx)
        ],
        axis=0,
    )
    size = 2 * cout + 8
    own = total[:size]
    low = total[size:] + dot(rim, edge)
    taps = 3 * len(TAPS)
    for i in range(len(TAPS)):
        at = i * width
        to = 3 * half * i
        acc[to : to + half] = low[: 2 * cout, at : at + width].T[half:]
        acc[to + half : to + 3 * half] = own[: 2 * cout, at : at + width].T
    if acc.shape[0] > half * taps:
        acc[half * taps :] = jnp.zeros((acc.shape[0] - half * taps, 2 * cout), F32)
    zero = jnp.zeros_like(beta)
    common = common_rows([alpha, zero], [high, zero], beta, first, second)
    lane = lax.broadcasted_iota(jnp.int32, (8, width), 1)
    _, plane, depth, _ = big.shape
    depth = depth - 8
    for n in range(2 * plane):
        column = jnp.zeros((8, width), F32)
        for tap in range(taps):
            start = half * tap - depth * n
            lo, hi = (max(start, 0), min(start + half, depth))
            if lo < hi:
                at = tap // 3 * width
                row = (low if tap % 3 == 0 else own)[2 * cout :, at : at + width]
                shift = (start - (0 if tap % 3 == 1 else half)) % width
                if shift:
                    row = pltpu.roll(row, shift, 1)
                column = jnp.where((lane >= lo) & (lane < hi), row, column)
        write_chunk(big.at[n // plane], n % plane, acc[depth * n : depth * (n + 1)], [column], common)
    core = lax.axis_index("c")
    keep[...] = big[core]
    send[...] = big[1 - core]


def pair_kernel(mine, other, out):
    _, depth, width = mine.shape
    rows = depth - 8
    cout = width // 2
    for i in range(mine.shape[0]):
        pair = [ref[i].astype(F32) for ref in (mine, other)]
        left = [value[rows:, :cout] for value in pair]
        right = [value[rows:, cout:] for value in pair]
        beta = rounded(0.5 * (right[0][2:3] + right[1][2:3]))
        first = total_of(right[0], 3, 6) + total_of(right[1], 3, 6)
        second = total_of(right[0], 6, 8) + total_of(right[1], 6, 8)
        slopes = pair[0][:rows, :cout] + pair[1][:rows, :cout]
        hats = pair[0][:rows, cout:] + pair[1][:rows, cout:]
        for value, vectors in zip(pair, right):
            slopes = slopes + value[:rows, cout:] * (vectors[2:3] - beta)
        common = common_rows(
            [part[6:7] for part in left], [part[0:1] for part in right], beta, first, second
        )
        columns = [eight(total_of(part, 0, 3)) for part in left]
        write_chunk(out, i, jnp.concatenate([slopes, hats], axis=1), columns, common)


def near_kernel(parts, out):
    slopes, hats, column, first, second, alpha, beta, high = read_chunks(parts)
    rows = slopes.shape[0]
    cout = slopes.shape[1]
    alpha, beta, high = (rounded(alpha), rounded(beta), rounded(high))
    both = outer(lone(column), lone(jnp.concatenate([alpha, high], axis=1)))[:rows]
    hats = hats - both[:, cout:]
    slopes = slopes - both[:, :cout] - hats * beta
    zero = jnp.zeros_like(beta)
    common = common_rows([alpha, zero], [high, zero], beta, first, second)
    body = jnp.concatenate([slopes, hats], axis=1)
    write_chunk(out, 0, body, [eight(column)], common)
    message = out[0]
    for i in range(1, out.shape[0]):
        out[i] = message


def far_kernel(parts, par, xd, yd, zface, dw, shift_out, tilt_out, both, zplane):
    mx, my = zface.shape[1:3]
    zplane[:, :mx] = zface[...]
    zplane[:, mx] = xd[:, my]
    zplane[:, mx + 1] = yd[:, mx + 1]
    _, rstd, gain, _, count = (par[i : i + 1] for i in range(5))
    slopes, hats, column, first, second, _, _, _ = read_chunks(parts)
    shift, tilt = (first / count, second / count)
    shift_out[...] = shift
    tilt_out[...] = tilt
    both[0:1] = shift
    both[1:2] = tilt
    value = slopes - outer(lone(column), lone(shift))[: slopes.shape[0]] - hats * tilt
    value = (value * (rstd * gain / count)).astype(BF)
    for i in range(dw.shape[0]):
        dw[i] = value


def input_kernel(pre, cot, par, grads, xd, yd, zd, active, weight, out, ext, nxt, wmat):
    mx, my, mz, cout = pre.shape
    width = out.shape[4]
    rows = my * mz
    mean, rstd, gain, bias = (par[i : i + 1] for i in range(4))
    shift, tilt = (grads[i : i + 1] for i in range(2))
    scale = rstd * gain
    inside = [
        unless(ring_index(axes) == ring_size(axes) - 1) for axes in (GX, GY, GZ)
    ]

    def gradient(value, cot, keep):
        on, hat = standardized(value, mean, rstd)
        normed = hat * gain + bias
        slope = slope_of(normed, jax.nn.sigmoid(normed), cot)
        return (on * keep * scale * (slope - shift - hat * tilt)).astype(BF)

    def rim(parts, keep):
        high, low, cot = (part.astype(F32) for part in parts)
        return gradient(high + low, cot, keep)

    build_matrix(weight, wmat)
    for r in range(mx + 1):
        keep = 1.0 if r < mx else inside[0]
        if r < mx:
            own = cot[r].astype(F32).reshape(rows, cout)
            base = gradient(pre[r].reshape(rows, cout), own, keep).reshape(my, mz, cout)
        else:
            flat = [xd[i, :my].reshape(rows, cout) for i in range(3)]
            base = rim(flat, keep).reshape(my, mz, cout)
        row = rim([yd[i, r] for i in range(3)], keep * inside[1])
        ext[r, :my] = base
        ext[r, my] = row
        whole = jnp.concatenate([base, row[None]], axis=0).astype(F32)
        side = rim([zd[i, r] for i in range(3)], keep * inside[2]).astype(F32)
        last = [zd[i, mx + 1].astype(F32)[r : r + 1] for i in range(3)]
        last = rim(last, keep * inside[1] * inside[2]).astype(F32)
        nxt[r] = with_edge(whole, jnp.concatenate([side, last], axis=0), mz - 1, -1).astype(BF)
    taps = (((1, 0),), ((2, 0), (0, 1)))
    for m in range(mx):
        for px in range(2):
            x = 2 * m + px
            mask = mask_row(active[x], mz, width)
            for py in range(2):
                left, right = ([], [])
                for a, sx in taps[px]:
                    for b, sy in taps[py]:
                        left.append(ext[m + sx, sy : sy + my].reshape(rows, cout))
                        left.append(nxt[m + sx, sy : sy + my].reshape(rows, cout))
                        at = (a * 3 + b) * width
                        right.append(wmat[at : at + width])
                left = jnp.concatenate(left, axis=1)
                right = jnp.concatenate(right, axis=1)
                value = dot(left, right, ((1,), (1,)))
                value = value * mask[:, py].astype(F32).reshape(rows, width)
                out[x, :, py] = value.astype(BF).reshape(my, mz, width)


def moved(value, axes, by):
    count = lax.axis_size(axes)
    return lax.ppermute(value, axes, [(i, (i + by) % count) for i in range(count)])


def beyond(value, axes, by):
    end = lax.axis_size(axes) - 1 if by > 0 else 0
    keep = (lax.axis_index(axes) != end).astype(value.dtype)
    return moved(value * keep, axes, by)


def slab(rows, like):
    return jnp.pad(rows, ((0, like - rows.shape[0]), (0, 0)))[None]


def exchanged(value, axes):
    return lax.all_to_all(value, axes, 0, 0)


def merged(parts):
    counts, sums, squares = (parts[:, 0], parts[:, 1], parts[:, 2])
    count = jnp.sum(counts, axis=0)
    total = jnp.sum(sums, axis=0)
    mean = total / jnp.maximum(count, 1.0)
    apart = sums / jnp.maximum(counts, 1.0) - mean
    return jnp.stack([count, total, jnp.sum(squares + counts * apart * apart, axis=0)])


def local(features, active, weight, gain, bias, cotangent):
    vx, vy, mz, width = features.shape
    cin = width // 2
    cout = weight.shape[4]
    mx, my = (vx // 2, vy // 2)
    near = lax.axis_size(NEAR)
    pack = pl.pallas_call(
        face_kernel,
        out_shape=shape((2, my + 1, mz, width), BF),
        in_specs=[pl.BlockSpec(memory_space=pltpu.HBM)] * 2,
        out_specs=pl.BlockSpec(memory_space=pltpu.VMEM),
        scratch_shapes=[
            pltpu.VMEM((vy, mz, width), BF),
            pltpu.VMEM((vy, 2 * mz), jnp.int32),
            pltpu.SemaphoreType.DMA((2,)),
        ],
        compiler_params=WIDE,
        cost_estimate=pl.CostEstimate(flops=10_000_000, bytes_accessed=400_000, transcendentals=0),
    )(features, active)
    xh = moved(pack, GX, 1)
    xin, act, zface, norm = call(
        mask_kernel,
        [
            shape((vx, 2, my, mz, width), BF),
            shape((mx, my, mz, width), BF),
            shape((vx, 2, my, width), BF),
            shape((2, cout), F32),
        ],
        [features, active, gain[None], bias[None]],
    )
    yface = jnp.concatenate([xh[1:2, my - 1], xin[:, 1, my - 1]], axis=0)
    zfaces = jnp.concatenate([xh[None, :, my], zface], axis=0)
    rows = vx + 1
    yh = beyond(jnp.concatenate([yface, slab(zfaces[:, 1, my - 1], mz)], axis=0), GY, 1)
    zfaces = jnp.concatenate([zfaces.reshape(2 * rows, my, width), yh[rows:]], axis=0)
    zh = beyond(zfaces, GZ, 1)
    pre, stats = call(
        forward_kernel,
        [
            shape((mx, my, mz, cout), F32),
            shape((near, 3, cout), F32),
        ],
        [xin, act, xh, yh, zh, weight],
        scratch=[pltpu.VMEM((9 * width, 2 * cout), BF)],
        flops=1_200_000_000,
    )
    xface, yface, zface = call(
        rim_kernel,
        [
            shape((3, my + 1, mz, cout), BF),
            shape((3, mx, mz, cout), BF),
            shape((3, mx, my, cout), BF),
        ],
        [pre, cotangent],
    )
    xd = moved(xface, GX, -1)
    (stats,) = call(merge_kernel, [shape((8, cout), F32)], [exchanged(stats, NEAR)])
    stats, yplane = call(
        pack_kernel,
        [shape((lax.axis_size(FAR), 3, cout), F32), shape((3, mx + 2, mz, cout), BF)],
        [stats, xd, yface, zface],
    )
    yd = moved(yplane, GY, -1)
    stats = merged(exchanged(stats, FAR))
    count = stats[0]
    mean = stats[1] / count
    rstd = lax.rsqrt(stats[2] / count + 1e-05)
    par = jnp.stack([mean, rstd, norm[0], norm[1], count])
    taps = 27 * cin
    rows = -(-taps // (8 * near)) * 8
    plane = lax.axis_size(PLANE)
    chunks = (plane, rows + 8, 2 * cout)
    section_out, big, send = call(
        slope_kernel,
        [
            shape((mx, my, mz, cout), BF),
            shape(chunks, BF),
            shape(chunks, BF),
        ],
        [pre, cotangent, par, xin, xh, yh, zh, yd],
        scratch=[
            pltpu.VMEM(pre.shape, F32),
            pltpu.VMEM((near * rows, 2 * cout), F32),
            pltpu.VMEM((2,) + chunks, BF),
        ],
        flops=2_400_000_000,
    )
    (big,) = call(pair_kernel, [shape(chunks, BF)], [big, moved(send, "c", 1)])
    far = lax.axis_size(FAR)
    (big,) = call(near_kernel, [shape((far, rows + 8, 2 * cout), BF)], [exchanged(big, PLANE)])
    dw, shift, tilt, grads, zplane = call(
        far_kernel,
        [
            shape((plane, rows, cout), BF),
            shape((1, cout), F32),
            shape((1, cout), F32),
            shape((2, cout), F32),
            shape((3, mx + 2, my, cout), BF),
        ],
        [exchanged(big, FAR), par, xd, yd, zface],
    )
    zd = moved(zplane, GZ, -1)
    shift_gradient, gain_gradient = (shift.reshape(cout), tilt.reshape(cout))
    (grad_features,) = call(
        input_kernel,
        [shape((vx, my, 2, mz, width), BF)],
        [pre, cotangent, par, grads, xd, yd, zd, active, weight],
        scratch=[
            pltpu.VMEM((mx + 1, my + 1, mz, cout), BF),
            pltpu.VMEM((mx + 1, my + 1, mz, cout), BF),
            pltpu.VMEM((9 * width, 2 * cout), BF),
        ],
        flops=2_400_000_000,
    )
    mine, grad_features = lax.optimization_barrier((exchanged(dw, PLANE), grad_features))
    other = moved(mine, "c", 1)
    low = lax.axis_index("c") == 0
    grad_weight = jnp.stack([jnp.where(low, mine, other), jnp.where(low, other, mine)])
    grad_weight = grad_weight.reshape(near * rows, cout)[:taps]
    grad_weight = grad_weight.astype(F32).reshape(weight.shape)
    grad_features = grad_features.reshape(features.shape)
    return (section_out, grad_features, grad_weight, gain_gradient, shift_gradient)


def solution(mesh):
    gx, gy, gz = (mesh.shape[name] for name in ("gx", "gy", "gz"))
    fine = Mesh(mesh.devices.reshape(gx // 2, 2, gy // 2, 2, gz), ALL)
    block = (("z", "yh"), ("x", "c"), "yl")
    in_specs = (P(*block, None), P(*block), P(), P(), P(), P(*block, None))
    out_specs = (P(*block, None), P(*block, None), P(), P(), P())
    return jax.shard_map(local, mesh=fine, in_specs=in_specs, out_specs=out_specs, check_vma=False)
```

```python
import jax
import jax.numpy as jnp
from jax import lax
from jax.experimental import pallas as pl
from jax.experimental.pallas import tpu as pltpu
from jax.sharding import Mesh, PartitionSpec as P

BF = jnp.bfloat16
F32 = jnp.float32
ALL = ("z", "yh", "x", "c", "yl")
NEAR = ("c", "yh", "x", "yl")
PLANE = ("yh", "x", "yl")
GX, GY, GZ = (("z", "yh"), ("x", "c"), ("yl",))
FAR = ("z",)
PARAMS = pltpu.CompilerParams(vmem_limit_bytes=24 * 1024 * 1024)
WIDE = pltpu.CompilerParams(vmem_limit_bytes=60 * 1024 * 1024)


def call(kernel, outs, args, scratch=(), flops=100_000_000):
    size = sum(a.size * a.dtype.itemsize for a in args) + sum(o.size * o.dtype.itemsize for o in outs)
    return pl.pallas_call(
        kernel,
        out_shape=outs,
        in_specs=[pl.BlockSpec(memory_space=pltpu.VMEM) for _ in args],
        out_specs=[pl.BlockSpec(memory_space=pltpu.VMEM) for _ in outs],
        scratch_shapes=list(scratch),
        compiler_params=PARAMS,
        cost_estimate=pl.CostEstimate(flops=flops, bytes_accessed=size, transcendentals=0),
    )(*args)


def shape(dims, dtype):
    return jax.ShapeDtypeStruct(dims, dtype)


def dot(left, right, dims=((1,), (0,))):
    return lax.dot_general(left, right, (dims, ((), ())), preferred_element_type=F32)


def row_picker(rows, step, offset):
    r = lax.broadcasted_iota(jnp.int32, (rows, rows * step), 0)
    k = lax.broadcasted_iota(jnp.int32, (rows, rows * step), 1)
    return (k == r * step + offset).astype(BF)


def rows_at(value, depth):
    return jnp.concatenate([value[i, depth : depth + 1] for i in range(value.shape[0])], axis=0)


def with_edge(value, edge, at, shift):
    groups, depth, lanes = value.shape
    moved = pltpu.roll(value.reshape(groups * depth, lanes), shift % (groups * depth), 0)
    moved = moved.reshape(groups, depth, lanes)
    q = lax.broadcasted_iota(jnp.int32, value.shape, 1)
    return jnp.where(q == at, jnp.broadcast_to(edge[:, None, :], value.shape), moved)


def mask_row(active, mz, width):
    ny, z = active.shape
    pair = lax.broadcasted_iota(jnp.int32, (mz, z), 1) // 2
    sel = (pair == lax.broadcasted_iota(jnp.int32, (mz, z), 0)).astype(F32)
    lane = lax.broadcasted_iota(jnp.int32, (z, width), 1) // (width // 2)
    widen = (lax.broadcasted_iota(jnp.int32, (z, width), 0) % 2 == lane).astype(BF)
    rep = jnp.broadcast_to(active.astype(F32)[:, None, :], (ny, mz, z)) * sel[None]
    m = dot(rep.astype(BF).reshape(ny * mz, z), widen).astype(BF)
    return m.reshape(ny // 2, 2, mz, width)


def ring_index(axes):
    index = 0
    for name in axes:
        index = index * lax.axis_size(name) + lax.axis_index(name)
    return index


def ring_size(axes):
    size = 1
    for name in axes:
        size = size * lax.axis_size(name)
    return size


def unless(condition):
    return jnp.where(condition, 0.0, 1.0)


def face_kernel(feat, active, pack, row, cells, sems):
    _, slabs, mz, width = pack.shape
    my = slabs - 1
    copies = [
        pltpu.make_async_copy(feat.at[feat.shape[0] - 1], row, sems.at[0]),
        pltpu.make_async_copy(active.at[active.shape[0] - 1], cells, sems.at[1]),
    ]
    for copy in copies:
        copy.start()
    keep = unless(ring_index(GX) == ring_size(GX) - 1)
    pick = row_picker(my, mz, mz - 1)
    copies[1].wait()
    m = mask_row(cells[...], mz, width)
    copies[0].wait()
    value = row[...].reshape(m.shape) * m
    for py in range(2):
        held = (value[:, py].astype(F32) * keep).astype(BF)
        pack[py, :my] = held
        pack[py, my] = dot(pick, held.reshape(my * mz, width)).astype(BF)


def mask_kernel(feat, active, gain, bias, xin, act, zface, norm):
    nx, _, my, mz, width = xin.shape
    pick = row_picker(my, mz, mz - 1)
    norm[0:1] = gain[...]
    norm[1:2] = bias[...]
    count = None
    for x in range(nx):
        m = mask_row(active[x], mz, width)
        value = feat[x].reshape(m.shape) * m
        for py in range(2):
            part = m[:, py]
            held = value[:, py]
            xin[x, py] = held
            zface[x, py] = dot(pick, held.reshape(my * mz, width)).astype(BF)
            term = part.astype(F32).reshape(my * mz, width)
            count = term if count is None else count + term
        if x % 2 == 1:
            both = count + pltpu.roll(count, width // 2, 1)
            act[x // 2] = (both > 0.0).astype(F32).astype(BF).reshape(my, mz, width)
            count = None


def tile_of(xin, xh, yh, row, b):
    py = 0 if b == 1 else 1
    my = xin.shape[2]
    base = xh[py, :my] if row == 0 else xin[row - 1, py]
    if b == 0:
        base = jnp.concatenate([yh[row][None], base[: my - 1]], axis=0)
    return base


def edge_of(zh, row, b):
    base = zh[2 * row + (0 if b == 1 else 1)]
    if b == 0:
        wide = base.astype(F32)
        first = zh[zh.shape[0] - 1].astype(F32)[row : row + 1]
        wide = jnp.concatenate([first, wide[: wide.shape[0] - 1]], axis=0)
        base = wide.astype(BF)
    return base


TAPS = [(a, b) for a in range(3) for b in range(3)]


def build_matrix(weight, wmat):
    half, cout = weight.shape[3:]
    width = 2 * half
    zero = jnp.zeros((half, cout), BF)
    for i, (a, b) in enumerate(TAPS):
        lo = i * width
        wmat[lo : lo + half, :cout] = weight[a, b, 1]
        wmat[lo + half : lo + width, :cout] = weight[a, b, 2]
        wmat[lo : lo + half, cout:] = zero
        wmat[lo + half : lo + width, cout:] = weight[a, b, 0]


OFF = 1e30


def standardized(value, mean, rstd):
    active = value < 0.1 * OFF
    return jnp.where(active, 1.0, 0.0), jnp.where(active, value - mean, 0.0) * rstd


def slope_of(normed, sig, cot):
    return cot * sig * (1.0 + normed * (1.0 - sig))


def rim_parts(value, cot):
    return [part.astype(BF) for part in split(value, 2) + [cot]]


def merge_kernel(parts, out):
    counts, sums, squares = (
        jnp.concatenate([parts[j, i : i + 1] for j in range(parts.shape[0])], axis=0) for i in range(3)
    )
    count = jnp.sum(counts, axis=0, keepdims=True)
    total = jnp.sum(sums, axis=0, keepdims=True)
    mean = total / jnp.maximum(count, 1.0)
    apart = sums / jnp.maximum(counts, 1.0) - mean
    square = jnp.sum(squares + counts * apart * apart, axis=0, keepdims=True)
    out[...] = jnp.concatenate([count, total, square] + [jnp.zeros_like(count)] * 5, axis=0)


def spread_kernel(stats, _, out):
    for i in range(out.shape[0]):
        out[i] = stats[:3]


def pack_y(xd, yface, zface, yplane):
    mx = yface.shape[1]
    my = zface.shape[2]
    depth = yplane.shape[2]
    yplane[:, :mx] = yface[...]
    yplane[:, mx] = xd[:, 0]
    for i in range(3):
        rows = [zface[i, m].astype(F32)[0:1] for m in range(mx)] + [xd[i, my].astype(F32)[0:1]]
        rows.append(jnp.zeros((depth - mx - 1, yplane.shape[3]), F32))
        yplane[i, mx + 1] = jnp.concatenate(rows, axis=0).astype(BF)


def rim_kernel(pre, cot, xface, yface, zface):
    mx, my, mz, cout = pre.shape
    for m in range(mx):
        planes = (pre[m], cot[m].astype(F32))
        side = rim_parts(*[rows_at(part, 0) for part in planes])
        line = rim_parts(*[part[0] for part in planes])
        whole = rim_parts(*planes) if m == 0 else None
        for i in range(3):
            yface[i, m] = line[i]
            zface[i, m] = side[i]
            if m == 0:
                xface[i, :my] = whole[i]
                xface[i, my] = side[i]


def forward_kernel(xin, act, xh, yh, zh, weight, pre, stats, wmat):
    mx, my, mz, cout = pre.shape
    width = xin.shape[4]
    build_matrix(weight, wmat)
    rows = my * mz
    total = jnp.zeros((1, cout), F32)
    count = jnp.zeros((1, cout), F32)
    w = wmat[...]
    for m in range(mx):
        left = jnp.concatenate(
            [tile_of(xin, xh, yh, 2 * m + a, b).reshape(rows, width) for a, b in TAPS], axis=1
        )
        edge = jnp.concatenate([edge_of(zh, 2 * m + a, b) for a, b in TAPS], axis=1)
        out = dot(left, w)
        rim = dot(edge, w[:, cout:])
        prev = with_edge(out[:, cout:].reshape(my, mz, cout), rim, 0, 1)
        value = out[:, :cout].reshape(my, mz, cout) + prev
        on = act[m].astype(F32)
        pre[m] = jnp.where(on > 0.0, value, OFF)
        total = total + jnp.sum((on * value).reshape(rows, cout), axis=0, keepdims=True)
        count = count + jnp.sum(on.reshape(rows, cout), axis=0, keepdims=True)
    mean = total / jnp.maximum(count, 1.0)
    squares = jnp.zeros((1, cout), F32)
    for m in range(mx):
        on = act[m].astype(F32).reshape(rows, cout)
        apart = jnp.where(on > 0.0, pre[m].reshape(rows, cout) - mean, 0.0)
        squares = squares + jnp.sum(apart * apart, axis=0, keepdims=True)
    for i in range(stats.shape[0]):
        stats[i, 0:1] = count
        stats[i, 1:2] = total
        stats[i, 2:3] = squares


def split(value, parts):
    out = []
    for _ in range(parts):
        out.append(value.astype(BF).astype(F32))
        value = value - out[-1]
    return out


def rounded(value):
    return value.astype(BF).astype(F32)


def outer(column, rows):
    return lax.dot_general(
        column, rows, (((0,), (0,)), ((), ())), precision=lax.Precision.HIGHEST, preferred_element_type=F32
    )


def write_chunk(ref, i, body, columns, common):
    left, right = common
    line = lax.broadcasted_iota(jnp.int32, left.shape, 0)
    for k, column in enumerate(columns):
        for at, part in enumerate(split(column, 3)):
            left = jnp.where(line == 3 * k + at, part, left)
    ref[i] = jnp.concatenate([body, jnp.concatenate([left, right], axis=1)], axis=0).astype(BF)


def common_rows(alphas, highs, beta, first, second):
    zero = jnp.zeros_like(beta)
    return (
        jnp.concatenate([zero] * 6 + alphas, axis=0),
        jnp.concatenate(highs + [beta] + split(first, 3) + split(second, 2), axis=0),
    )


def total_of(rows, start, stop):
    value = rows[start : start + 1]
    for i in range(start + 1, stop):
        value = value + rows[i : i + 1]
    return value


def read_chunks(ref):
    devices, depth, _ = ref.shape
    rows = depth - 8
    cout = ref.shape[2] // 2
    slopes = hats = None
    firsts = seconds = betas = None
    columns, vectors = ([], [])
    for j in range(devices):
        value = ref[j].astype(F32)
        left, right = (value[rows:, :cout], value[rows:, cout:])
        part = value[:rows, cout:]
        beta = right[2:3]
        term = value[:rows, :cout] + part * beta
        first = total_of(right, 3, 6)
        second = total_of(right, 6, 8)
        for k in range(2):
            columns.append(total_of(left, 3 * k, 3 * k + 3))
            vectors.append(jnp.concatenate([left[6 + k : 7 + k], right[k : k + 1]], axis=1))
        if j == 0:
            slopes, hats, firsts, seconds, betas = (term, part, first, second, beta)
        else:
            slopes, hats = (slopes + term, hats + part)
            firsts, seconds, betas = (firsts + first, seconds + second, betas + beta)
    columns = jnp.concatenate(columns, axis=0)
    vectors = jnp.concatenate(vectors, axis=0)
    both = outer(columns, vectors)[:rows]
    slopes = slopes + both[:, :cout]
    hats = hats + both[:, cout:]
    column = jnp.sum(columns, axis=0, keepdims=True)
    middle = jnp.sum(vectors, axis=0, keepdims=True) / (2 * devices)
    return slopes, hats, column, firsts, seconds, middle[:, :cout], betas / devices, middle[:, cout:]


def eight(row):
    return jnp.broadcast_to(row, (8, row.shape[1]))


def lone(row):
    return jnp.where(lax.broadcasted_iota(jnp.int32, (8, row.shape[1]), 0) == 0, eight(row), 0.0)


def slope_kernel(
    pre, cot, par, xin, xh, yh, zh, out, keep, send, slope, acc, big
):
    mx, my, mz, cout = pre.shape
    width = xin.shape[4]
    half = width // 2
    rows = my * mz
    mean, rstd, gain, bias = (par[i : i + 1] for i in range(4))
    first, second, count, high, square = (jnp.zeros((1, cout), F32) for _ in range(5))
    for m in range(mx):
        on, hat = standardized(pre[m].reshape(rows, cout), mean, rstd)
        normed = hat * gain + bias
        sig = jax.nn.sigmoid(normed)
        out[m] = (on * normed * sig).astype(BF).reshape(my, mz, cout)
        tilt = slope_of(normed, sig, on * cot[m].astype(F32).reshape(rows, cout))
        slope[m] = tilt.reshape(my, mz, cout)
        first = first + jnp.sum(tilt, axis=0, keepdims=True)
        second = second + jnp.sum(tilt * hat, axis=0, keepdims=True)
        count = count + jnp.sum(on, axis=0, keepdims=True)
        high = high + jnp.sum(hat, axis=0, keepdims=True)
        square = square + jnp.sum(hat * hat, axis=0, keepdims=True)
    some = jnp.maximum(count, 1.0)
    alpha = rounded(first / some)
    high = rounded(high / some)
    beta = (second - high * first) / jnp.maximum(square - count * high * high, 0.01 * some)
    beta = rounded(beta)
    last = lax.broadcasted_iota(jnp.int32, (my, mz, cout), 1) == mz - 1
    total = None
    rims = [[], [], []]
    for m in range(mx):
        on, hat = standardized(pre[m].reshape(rows, cout), mean, rstd)
        hat = on * (hat - high)
        rest = slope[m].reshape(rows, cout) - on * alpha - hat * beta
        here, after = ([], [])
        for i, part in enumerate((rest, hat, on)):
            held = part.astype(BF)
            lines = 8 if i == 2 else cout
            wide = held.astype(F32)
            rims[i].append(rows_at(wide.reshape(my, mz, cout), 0))
            nxt = pltpu.roll(wide, rows - 1, 0).reshape(my, mz, cout)
            nxt = jnp.where(last, 0.0, nxt).reshape(rows, cout)
            here.append(wide.T[:lines])
            after.append(nxt.T[:lines])
        right = jnp.concatenate(here + after, axis=0).astype(BF)
        left = jnp.concatenate(
            [tile_of(xin, xh, yh, 2 * m + a, b).reshape(rows, width) for a, b in TAPS], axis=1
        )
        term = dot(right, left)
        total = term if total is None else total + term
    rim = [jnp.concatenate(parts, axis=0).T for parts in rims]
    rim = jnp.concatenate([rim[0], rim[1], rim[2][:8]], axis=0).astype(BF)
    edge = jnp.concatenate(
        [
            jnp.concatenate([edge_of(zh, 2 * m + a, b) for a, b in TAPS], axis=1)
            for m in range(mx)
        ],
        axis=0,
    )
    size = 2 * cout + 8
    own = total[:size]
    low = total[size:] + dot(rim, edge)
    taps = 3 * len(TAPS)
    for i in range(len(TAPS)):
        at = i * width
        to = 3 * half * i
        acc[to : to + half] = low[: 2 * cout, at : at + width].T[half:]
        acc[to + half : to + 3 * half] = own[: 2 * cout, at : at + width].T
    if acc.shape[0] > half * taps:
        acc[half * taps :] = jnp.zeros((acc.shape[0] - half * taps, 2 * cout), F32)
    zero = jnp.zeros_like(beta)
    common = common_rows([alpha, zero], [high, zero], beta, first, second)
    lane = lax.broadcasted_iota(jnp.int32, (8, width), 1)
    _, plane, depth, _ = big.shape
    depth = depth - 8
    for n in range(2 * plane):
        column = jnp.zeros((8, width), F32)
        for tap in range(taps):
            start = half * tap - depth * n
            lo, hi = (max(start, 0), min(start + half, depth))
            if lo < hi:
                at = tap // 3 * width
                row = (low if tap % 3 == 0 else own)[2 * cout :, at : at + width]
                shift = (start - (0 if tap % 3 == 1 else half)) % width
                if shift:
                    row = pltpu.roll(row, shift, 1)
                column = jnp.where((lane >= lo) & (lane < hi), row, column)
        write_chunk(big.at[n // plane], n % plane, acc[depth * n : depth * (n + 1)], [column], common)
    core = lax.axis_index("c")
    keep[...] = big[core]
    send[...] = big[1 - core]


def pair_kernel(mine, other, out):
    _, depth, width = mine.shape
    rows = depth - 8
    cout = width // 2
    for i in range(mine.shape[0]):
        pair = [ref[i].astype(F32) for ref in (mine, other)]
        left = [value[rows:, :cout] for value in pair]
        right = [value[rows:, cout:] for value in pair]
        beta = rounded(0.5 * (right[0][2:3] + right[1][2:3]))
        first = total_of(right[0], 3, 6) + total_of(right[1], 3, 6)
        second = total_of(right[0], 6, 8) + total_of(right[1], 6, 8)
        slopes = pair[0][:rows, :cout] + pair[1][:rows, :cout]
        hats = pair[0][:rows, cout:] + pair[1][:rows, cout:]
        for value, vectors in zip(pair, right):
            slopes = slopes + value[:rows, cout:] * (vectors[2:3] - beta)
        common = common_rows(
            [part[6:7] for part in left], [part[0:1] for part in right], beta, first, second
        )
        columns = [eight(total_of(part, 0, 3)) for part in left]
        write_chunk(out, i, jnp.concatenate([slopes, hats], axis=1), columns, common)


def near_kernel(parts, xd, yface, zface, out, yplane):
    pack_y(xd, yface, zface, yplane)
    slopes, hats, column, first, second, alpha, beta, high = read_chunks(parts)
    rows = slopes.shape[0]
    cout = slopes.shape[1]
    alpha, beta, high = (rounded(alpha), rounded(beta), rounded(high))
    both = outer(lone(column), lone(jnp.concatenate([alpha, high], axis=1)))[:rows]
    hats = hats - both[:, cout:]
    slopes = slopes - both[:, :cout] - hats * beta
    zero = jnp.zeros_like(beta)
    common = common_rows([alpha, zero], [high, zero], beta, first, second)
    body = jnp.concatenate([slopes, hats], axis=1)
    write_chunk(out, 0, body, [eight(column)], common)
    message = out[0]
    for i in range(1, out.shape[0]):
        out[i] = message


def far_kernel(parts, par, xd, yd, zface, dw, shift_out, tilt_out, both, zplane):
    mx, my = zface.shape[1:3]
    zplane[:, :mx] = zface[...]
    zplane[:, mx] = xd[:, my]
    zplane[:, mx + 1] = yd[:, mx + 1]
    _, rstd, gain, _, count = (par[i : i + 1] for i in range(5))
    slopes, hats, column, first, second, _, _, _ = read_chunks(parts)
    shift, tilt = (first / count, second / count)
    shift_out[...] = shift
    tilt_out[...] = tilt
    both[0:1] = shift
    both[1:2] = tilt
    value = slopes - outer(lone(column), lone(shift))[: slopes.shape[0]] - hats * tilt
    value = (value * (rstd * gain / count)).astype(BF)
    for i in range(dw.shape[0]):
        dw[i] = value


def input_kernel(pre, cot, par, grads, xd, yd, zd, active, weight, out, ext, nxt, wmat):
    mx, my, mz, cout = pre.shape
    width = out.shape[4]
    rows = my * mz
    mean, rstd, gain, bias = (par[i : i + 1] for i in range(4))
    shift, tilt = (grads[i : i + 1] for i in range(2))
    scale = rstd * gain
    inside = [
        unless(ring_index(axes) == ring_size(axes) - 1) for axes in (GX, GY, GZ)
    ]

    def gradient(value, cot, keep):
        on, hat = standardized(value, mean, rstd)
        normed = hat * gain + bias
        slope = slope_of(normed, jax.nn.sigmoid(normed), cot)
        return (on * keep * scale * (slope - shift - hat * tilt)).astype(BF)

    def rim(parts, keep):
        high, low, cot = (part.astype(F32) for part in parts)
        return gradient(high + low, cot, keep)

    build_matrix(weight, wmat)
    for r in range(mx + 1):
        keep = 1.0 if r < mx else inside[0]
        if r < mx:
            own = cot[r].astype(F32).reshape(rows, cout)
            base = gradient(pre[r].reshape(rows, cout), own, keep).reshape(my, mz, cout)
        else:
            flat = [xd[i, :my].reshape(rows, cout) for i in range(3)]
            base = rim(flat, keep).reshape(my, mz, cout)
        row = rim([yd[i, r] for i in range(3)], keep * inside[1])
        ext[r, :my] = base
        ext[r, my] = row
        whole = jnp.concatenate([base, row[None]], axis=0).astype(F32)
        side = rim([zd[i, r] for i in range(3)], keep * inside[2]).astype(F32)
        last = [zd[i, mx + 1].astype(F32)[r : r + 1] for i in range(3)]
        last = rim(last, keep * inside[1] * inside[2]).astype(F32)
        nxt[r] = with_edge(whole, jnp.concatenate([side, last], axis=0), mz - 1, -1).astype(BF)
    taps = (((1, 0),), ((2, 0), (0, 1)))
    for m in range(mx):
        for px in range(2):
            x = 2 * m + px
            mask = mask_row(active[x], mz, width)
            for py in range(2):
                left, right = ([], [])
                for a, sx in taps[px]:
                    for b, sy in taps[py]:
                        left.append(ext[m + sx, sy : sy + my].reshape(rows, cout))
                        left.append(nxt[m + sx, sy : sy + my].reshape(rows, cout))
                        at = (a * 3 + b) * width
                        right.append(wmat[at : at + width])
                left = jnp.concatenate(left, axis=1)
                right = jnp.concatenate(right, axis=1)
                value = dot(left, right, ((1,), (1,)))
                value = value * mask[:, py].astype(F32).reshape(rows, width)
                out[x, :, py] = value.astype(BF).reshape(my, mz, width)


def moved(value, axes, by):
    count = lax.axis_size(axes)
    return lax.ppermute(value, axes, [(i, (i + by) % count) for i in range(count)])


def beyond(value, axes, by):
    end = lax.axis_size(axes) - 1 if by > 0 else 0
    keep = (lax.axis_index(axes) != end).astype(value.dtype)
    return moved(value * keep, axes, by)


def slab(rows, like):
    return jnp.pad(rows, ((0, like - rows.shape[0]), (0, 0)))[None]


def exchanged(value, axes):
    return lax.all_to_all(value, axes, 0, 0)


def merged(parts):
    counts, sums, squares = (parts[:, 0], parts[:, 1], parts[:, 2])
    count = jnp.sum(counts, axis=0)
    total = jnp.sum(sums, axis=0)
    mean = total / jnp.maximum(count, 1.0)
    apart = sums / jnp.maximum(counts, 1.0) - mean
    return jnp.stack([count, total, jnp.sum(squares + counts * apart * apart, axis=0)])


def local(features, active, weight, gain, bias, cotangent):
    vx, vy, mz, width = features.shape
    cin = width // 2
    cout = weight.shape[4]
    mx, my = (vx // 2, vy // 2)
    near = lax.axis_size(NEAR)
    pack = pl.pallas_call(
        face_kernel,
        out_shape=shape((2, my + 1, mz, width), BF),
        in_specs=[pl.BlockSpec(memory_space=pltpu.HBM)] * 2,
        out_specs=pl.BlockSpec(memory_space=pltpu.VMEM),
        scratch_shapes=[
            pltpu.VMEM((vy, mz, width), BF),
            pltpu.VMEM((vy, 2 * mz), jnp.int32),
            pltpu.SemaphoreType.DMA((2,)),
        ],
        compiler_params=WIDE,
        cost_estimate=pl.CostEstimate(flops=10_000_000, bytes_accessed=400_000, transcendentals=0),
    )(features, active)
    xh = moved(pack, GX, 1)
    xin, act, zface, norm = call(
        mask_kernel,
        [
            shape((vx, 2, my, mz, width), BF),
            shape((mx, my, mz, width), BF),
            shape((vx, 2, my, width), BF),
            shape((2, cout), F32),
        ],
        [features, active, gain[None], bias[None]],
    )
    yface = jnp.concatenate([xh[1:2, my - 1], xin[:, 1, my - 1]], axis=0)
    zfaces = jnp.concatenate([xh[None, :, my], zface], axis=0)
    rows = vx + 1
    yh = beyond(jnp.concatenate([yface, slab(zfaces[:, 1, my - 1], mz)], axis=0), GY, 1)
    zfaces = jnp.concatenate([zfaces.reshape(2 * rows, my, width), yh[rows:]], axis=0)
    zh = beyond(zfaces, GZ, 1)
    pre, stats = call(
        forward_kernel,
        [
            shape((mx, my, mz, cout), F32),
            shape((near, 3, cout), F32),
        ],
        [xin, act, xh, yh, zh, weight],
        scratch=[pltpu.VMEM((9 * width, 2 * cout), BF)],
        flops=1_200_000_000,
    )
    xface, yface, zface = call(
        rim_kernel,
        [
            shape((3, my + 1, mz, cout), BF),
            shape((3, mx, mz, cout), BF),
            shape((3, mx, my, cout), BF),
        ],
        [pre, cotangent],
    )
    xd = moved(xface, GX, -1)
    (stats,) = call(merge_kernel, [shape((8, cout), F32)], [exchanged(stats, NEAR)])
    (stats,) = call(spread_kernel, [shape((lax.axis_size(FAR), 3, cout), F32)], [stats, xd])
    stats = merged(exchanged(stats, FAR))
    count = stats[0]
    mean = stats[1] / count
    rstd = lax.rsqrt(stats[2] / count + 1e-05)
    par = jnp.stack([mean, rstd, norm[0], norm[1], count])
    taps = 27 * cin
    rows = -(-taps // (8 * near)) * 8
    plane = lax.axis_size(PLANE)
    chunks = (plane, rows + 8, 2 * cout)
    section_out, big, send = call(
        slope_kernel,
        [
            shape((mx, my, mz, cout), BF),
            shape(chunks, BF),
            shape(chunks, BF),
        ],
        [pre, cotangent, par, xin, xh, yh, zh],
        scratch=[
            pltpu.VMEM(pre.shape, F32),
            pltpu.VMEM((near * rows, 2 * cout), F32),
            pltpu.VMEM((2,) + chunks, BF),
        ],
        flops=2_400_000_000,
    )
    (big,) = call(pair_kernel, [shape(chunks, BF)], [big, moved(send, "c", 1)])
    far = lax.axis_size(FAR)
    big, yplane = call(
        near_kernel,
        [shape((far, rows + 8, 2 * cout), BF), shape((3, mx + 2, mz, cout), BF)],
        [exchanged(big, PLANE), xd, yface, zface],
    )
    yd = moved(yplane, GY, -1)
    dw, shift, tilt, grads, zplane = call(
        far_kernel,
        [
            shape((plane, rows, cout), BF),
            shape((1, cout), F32),
            shape((1, cout), F32),
            shape((2, cout), F32),
            shape((3, mx + 2, my, cout), BF),
        ],
        [exchanged(big, FAR), par, xd, yd, zface],
    )
    zd = moved(zplane, GZ, -1)
    shift_gradient, gain_gradient = (shift.reshape(cout), tilt.reshape(cout))
    (grad_features,) = call(
        input_kernel,
        [shape((vx, my, 2, mz, width), BF)],
        [pre, cotangent, par, grads, xd, yd, zd, active, weight],
        scratch=[
            pltpu.VMEM((mx + 1, my + 1, mz, cout), BF),
            pltpu.VMEM((mx + 1, my + 1, mz, cout), BF),
            pltpu.VMEM((9 * width, 2 * cout), BF),
        ],
        flops=2_400_000_000,
    )
    mine, grad_features = lax.optimization_barrier((exchanged(dw, PLANE), grad_features))
    other = moved(mine, "c", 1)
    low = lax.axis_index("c") == 0
    grad_weight = jnp.stack([jnp.where(low, mine, other), jnp.where(low, other, mine)])
    grad_weight = grad_weight.reshape(near * rows, cout)[:taps]
    grad_weight = grad_weight.astype(F32).reshape(weight.shape)
    grad_features = grad_features.reshape(features.shape)
    return (section_out, grad_features, grad_weight, gain_gradient, shift_gradient)


def solution(mesh):
    gx, gy, gz = (mesh.shape[name] for name in ("gx", "gy", "gz"))
    fine = Mesh(mesh.devices.reshape(gx // 2, 2, gy // 2, 2, gz), ALL)
    block = (("z", "yh"), ("x", "c"), "yl")
    in_specs = (P(*block, None), P(*block), P(), P(), P(), P(*block, None))
    out_specs = (P(*block, None), P(*block, None), P(), P(), P())
    return jax.shard_map(local, mesh=fine, in_specs=in_specs, out_specs=out_specs, check_vma=False)
```
